32 devices in a mesh: head: 4 (over x, core), blk: 8 (over z, y).
Axes of the slice: x: 2, y: 2, z: 4, core: 2. Of those that a mesh axis runs over, the one named last changes fastest.
Arguments:
- layer_input: bfloat16 [2, 4096, 512], P(None, ('head', 'blk')), may hold values from -9 to 9
- segments: int32 [2, 4096], P(None, ('head', 'blk')), may hold values from 0 to 7, never falling along the last dimension, each value on 1 to 1024 neighbouring positions
- input_weight: bfloat16 [512, 1536], P(('head', 'blk')), may hold values from -0.25 to 0.25
- output_weight: bfloat16 [512, 512], P(('head', 'blk')), may hold values from -1 to 1
- up_weight: bfloat16 [512, 2048], P(('head', 'blk')), may hold values from -0.25 to 0.25
- down_weight: bfloat16 [2048, 512], P(('head', 'blk')), may hold values from -0.375 to 0.375
- query_bias: bfloat16 [512], P(('head', 'blk')), may hold values from -3 to 3
- value_bias: bfloat16 [512], P(('head', 'blk')), may hold values from -3 to 3
- output_bias: bfloat16 [512], P(('head', 'blk')), may hold values from -3 to 3
- up_bias: bfloat16 [2048], P(('head', 'blk')), may hold values from -3 to 3
- down_bias: bfloat16 [512], P(('head', 'blk')), may hold values from -3 to 3
- alphas: float32 [2], replicated, may hold values from 0.2 to 0.45
- out_grad: bfloat16 [2, 4096, 512], P(None, ('head', 'blk')), may hold values from -6 to 6
Outputs:
- layer_output: bfloat16 [2, 4096, 512], P(None, ('head', 'blk'))
- input_grad: bfloat16 [2, 4096, 512], P(None, ('head', 'blk'))
- input_weight_grad: float32 [512, 1536], P(('head', 'blk'))
- output_weight_grad: float32 [512, 512], P(('head', 'blk'))
- up_weight_grad: float32 [512, 2048], P(('head', 'blk'))
- down_weight_grad: float32 [2048, 512], P(('head', 'blk'))
- query_bias_grad: float32 [512], P(('head', 'blk'))
- value_bias_grad: float32 [512], P(('head', 'blk'))
- output_bias_grad: float32 [512], P(('head', 'blk'))
- up_bias_grad: float32 [2048], P(('head', 'blk'))
- down_bias_grad: float32 [512], P(('head', 'blk'))
- alphas_grad: float32 [2], replicated
- rms_values: float32 [3], replicated
The draws below stay inside these ranges and needn't reach their ends.
Inputs may be any that keep to these rules, and one draw needn't show every extreme that they name: `segments`: A sequence's segment numbers never fall; each document holds 1 to 1024 tokens and some document holds exactly 1024.
All inputs are finite; a program needn't handle non-finite values.
Results may differ from the reference program's by a relative error of at most 0.017.
The reference program's roundings to bfloat16 on the way count: a program that leaves them out, or rounds other values in their place, can miss the bound.
Values may be sent and summed in bfloat16 or wider, within the bound.
A program may use at most 64 MiB of HBM per device.

```python
import math
import jax
import jax.numpy as jnp
import numpy as np
from jax import lax

D = 512
HEADS = 8
HD = 64
FF = 2048
SEQS = 2
SEQ_LEN = 4096
DOC_MOST = 1024
DOCS = 8


def draw_layer_input(key, part):
    places = jnp.arange(SEQ_LEN, dtype=jnp.float32) / SEQ_LEN
    spread = (0.6 * jnp.exp(math.log(3.0) * places))[None, :, None]
    drawn = jnp.clip(jax.random.normal(key, (SEQS, SEQ_LEN, D), jnp.float32), -5.0, 5.0) * spread
    return drawn.astype(jnp.bfloat16)


def shard_levels(key, shape, cuts, least, high):
    def one(axis_at, shards_of):
        draws = jax.random.uniform(jax.random.fold_in(jax.random.fold_in(key, 6), axis_at), (shards_of,), jnp.float32, least / len(cuts), high / len(cuts))
        return jnp.repeat(jnp.exp(draws), shape[axis_at] // shards_of).reshape((-1,) + (1,) * (len(shape) - axis_at - 1))

    loudness = one(*cuts[0])
    for cut in cuts[1:]:
        loudness = loudness * one(*cut)
    return loudness


def length_profile(amount, total, bound, slope):
    loads = [(1 << 20) // math.isqrt(grade ** slope) + 1 for grade in range(2, amount + 1)]
    rest, counts = total - bound - (amount - 1), [1] * (amount - 1)
    while rest > 0:
        free = [i for i in range(amount - 1) if counts[i] < bound]
        mass, remaining = sum([loads[i] for i in free]), rest
        for i in free:
            extra = min(bound - counts[i], max(1, remaining * loads[i] // mass), rest)
            counts[i] = counts[i] + extra
            rest = rest - extra
    return np.array([bound] + counts)


def uneven_parts(key, number_of, total, bound, lean):
    if number_of == 2:
        one = jax.random.randint(key, (), max(1, total - bound), min(bound, total - 1) + 1)
        return jnp.stack([one, total - one])
    sizes = jnp.asarray(length_profile(number_of, total, bound, lean), jnp.int32)
    twos = (number_of - 1) // 2
    donor, taker = sizes[1:1 + 2 * twos:2], sizes[2:2 + 2 * twos:2]
    margin = jnp.minimum(donor - 1, bound - taker)
    shifted = jax.random.randint(jax.random.fold_in(key, 1), (twos,), 0, 1 << 20) % (margin + 1)
    sizes = sizes.at[1:1 + 2 * twos:2].set(donor - shifted).at[2:2 + 2 * twos:2].set(taker + shifted)
    return sizes[jax.random.permutation(jax.random.fold_in(key, 2), number_of)]


def normal_values(own_key, dims, deviation, reach, shards=(), held_as=jnp.bfloat16):
    level = shard_levels(own_key, dims, shards, -0.22, 0.18) if shards else 1.0
    array = jax.random.normal(own_key, dims, jnp.float32) * deviation * level
    return jnp.minimum(jnp.maximum(array, -reach), reach).astype(held_as)


def setup_inputs(seed: int = 0) -> dict:
    keys = jax.random.split(jax.random.key(seed), 14)
    return {
        "layer_input": draw_layer_input(jax.random.fold_in(keys[13], 71), 0),
        "segments": jax.vmap(lambda own: jnp.searchsorted(jnp.cumsum(uneven_parts(own, DOCS, SEQ_LEN, DOC_MOST, 0)), jnp.arange(SEQ_LEN), side="right"))(jax.random.split(keys[1], SEQS)).reshape((SEQS, SEQ_LEN)).astype(jnp.int32),
        "input_weight": normal_values(keys[2], (D, 3 * D), D ** -0.5, 0.25, ((0, 32),)),
        "output_weight": normal_values(keys[3], (D, D), (D // 16) ** -0.5, 1.0, ((0, 32),)),
        "up_weight": normal_values(keys[4], (D, FF), D ** -0.5, 0.25, ((0, 32),)),
        "down_weight": normal_values(keys[5], (FF, D), (FF // 8) ** -0.5, 0.375, ((0, 32),)),
        "query_bias": normal_values(keys[6], (D,), 0.5, 3.0, ((0, 32),)),
        "value_bias": normal_values(keys[7], (D,), 0.5, 3.0, ((0, 32),)),
        "output_bias": normal_values(keys[8], (D,), 0.5, 3.0, ((0, 32),)),
        "up_bias": normal_values(keys[9], (FF,), 0.5, 3.0, ((0, 32),)),
        "down_bias": normal_values(keys[10], (D,), 0.5, 3.0, ((0, 32),)),
        "alphas": jnp.clip(jax.random.uniform(keys[11], (2,), jnp.float32, 0.2, 0.45), 0.2, 0.45),
        "out_grad": normal_values(keys[12], (SEQS, SEQ_LEN, D), 1.0, 6.0, ((1, 32),)),
    }


@jax.custom_vjp
def low(v):
    return lax.optimization_barrier(v.astype(jnp.bfloat16)).astype(jnp.float32)

@jax.custom_vjp
def low_back(v):
    return v

def low_keep(v):
    return (low(v), None)

def low_pass(kept, grad):
    return (grad,)

def back_keep(v):
    return (v, None)

def back_low(kept, grad):
    return (low(grad),)
low.defvjp(low_keep, low_pass)
low_back.defvjp(back_keep, back_low)

def attend_sequence(queries, keys_all, values_all, numbers):
    block_size = min(512, SEQ_LEN)
    places = jnp.arange(SEQ_LEN, dtype=jnp.int32)

    def one_block(block_index):
        row_start = block_index * block_size
        rows_query = lax.dynamic_slice_in_dim(queries, row_start, block_size, 0)
        numbers_query = lax.dynamic_slice_in_dim(numbers, row_start, block_size, 0)
        places_query = row_start + jnp.arange(block_size, dtype=jnp.int32)
        raw_scores = low_back(0.125 * jnp.einsum('qhd,khd->hqk', rows_query, keys_all, precision=lax.Precision.HIGHEST))
        visible = (numbers_query[:, None] == numbers[None, :]) & (places[None, :] <= places_query[:, None])
        scores = jnp.where(visible[None], raw_scores, -1e+30)
        row_peak = lax.optimization_barrier(jnp.max(scores, -1, keepdims=True))
        weights = jnp.exp(scores - row_peak)
        probs = weights / lax.optimization_barrier(jnp.sum(weights, -1, keepdims=True))
        result = jnp.einsum('hqk,khd->qhd', probs, values_all, precision=lax.Precision.HIGHEST)
        return result.reshape(block_size, D)
    blocks_out = lax.map(jax.checkpoint(one_block), jnp.arange(SEQ_LEN // block_size, dtype=jnp.int32))
    return blocks_out.reshape(SEQ_LEN, D)

def forward_layer(inputs, parameters, segments):
    input_weight, output_weight, up_weight, down_weight, query_bias, value_bias, output_bias, up_bias, down_bias, alphas = parameters
    highest = lax.Precision.HIGHEST
    joint_bias = jnp.concatenate([query_bias, jnp.zeros((D,), jnp.float32), value_bias])

    def one_sequence(scan_carry, seq_item):
        tokens, numbers = seq_item
        projected = low(low_back(jnp.dot(tokens, input_weight, precision=highest) + joint_bias))
        queries = projected[:, :D].reshape(SEQ_LEN, HEADS, HD)
        keys_all = projected[:, D:2 * D].reshape(SEQ_LEN, HEADS, HD)
        values_all = projected[:, 2 * D:].reshape(SEQ_LEN, HEADS, HD)
        mixed = low(low_back(attend_sequence(queries, keys_all, values_all, numbers)))
        branch_attn = low_back(jnp.dot(mixed, output_weight, precision=highest) + output_bias)
        residual = tokens + alphas[0] * branch_attn
        pre_act = low_back(jnp.dot(low(residual), up_weight, precision=highest) + up_bias)
        activation = low(jax.nn.gelu(pre_act, approximate=False))
        branch_ffn = low_back(jnp.dot(activation, down_weight, precision=highest) + down_bias)
        stream = residual + alphas[1] * branch_ffn
        return (scan_carry, (stream, alphas[0] * branch_attn, alphas[1] * branch_ffn))
    scan_carry, outputs = lax.scan(one_sequence, jnp.zeros((), jnp.float32), (inputs, segments))
    streams, attn_terms, ffn_terms = outputs
    squares = jnp.stack([jnp.mean(streams * streams), jnp.mean(attn_terms * attn_terms), jnp.mean(ffn_terms * ffn_terms)])
    return (streams, squares)

def reference(layer_input, segments, input_weight, output_weight, up_weight, down_weight, query_bias, value_bias, output_bias, up_bias, down_bias, alphas, out_grad):
    parameters = (input_weight.astype(jnp.float32), output_weight.astype(jnp.float32), up_weight.astype(jnp.float32), down_weight.astype(jnp.float32), query_bias.astype(jnp.float32), value_bias.astype(jnp.float32), output_bias.astype(jnp.float32), up_bias.astype(jnp.float32), down_bias.astype(jnp.float32), alphas.astype(jnp.float32))
    inputs = layer_input.astype(jnp.float32)

    def run_layer(inputs, parameters):
        return forward_layer(inputs, parameters, segments)
    streams, pullback, squares = jax.vjp(run_layer, inputs, parameters, has_aux=True)
    input_grad, grads = pullback(out_grad.astype(jnp.float32))
    rms_values = jnp.sqrt(squares)
    return (streams.astype(jnp.bfloat16), input_grad.astype(jnp.bfloat16), grads[0], grads[1], grads[2], grads[3], grads[4], grads[5], grads[6], grads[7], grads[8], grads[9], rms_values)
```

```python
import functools
import math

import jax
import jax.numpy as jnp
from jax import lax
from jax.experimental import pallas as pl
from jax.experimental.pallas import tpu as pltpu
from jax.sharding import PartitionSpec as P

HEADS = 8
HD = 64
LANES = 128
GROUP = 16
BLOCK = 256
VMEM_BYTES = 56 * 1024 * 1024
F32 = jnp.float32
BF16 = jnp.bfloat16
VMEM = pltpu.VMEM
NEG = -1e30


class Place:
    def __init__(self, blocks):
        self.blocks = blocks
        self.depth = blocks // 2
        head = lax.axis_index("head")
        block = lax.axis_index("blk")
        self.x, self.core = lax.div(head, 2), lax.rem(head, 2)
        self.z, self.y = lax.div(block, 2), lax.rem(block, 2)
        flat = head * blocks + block
        self.part, self.slot = lax.div(flat, GROUP), lax.rem(flat, GROUP)

    def at(self, x=None, core=None, z=None, y=None):
        x = self.x if x is None else x
        core = self.core if core is None else core
        z = self.z if z is None else z
        y = self.y if y is None else y
        return (x * 2 + core, z * 2 + y)

    def deeper(self, offset):
        return lax.rem(self.z + offset + self.depth, self.depth)

    def member(self, slot, part=None):
        part = self.part if part is None else part
        flat = part * GROUP + slot
        return (lax.div(flat, self.blocks), lax.rem(flat, self.blocks))

    def other_slot(self, offset):
        return lax.rem(self.slot + offset + GROUP, GROUP)


def remote(src, dst, send, recv, device):
    return pltpu.make_async_remote_copy(
        src_ref=src,
        dst_ref=dst,
        send_sem=send,
        recv_sem=recv,
        device_id=device,
        device_id_type=pl.DeviceIdType.MESH,
    )


def greet(place, parts, tree):
    barrier = pltpu.get_barrier_semaphore()

    def hello(device):
        pl.semaphore_signal(barrier, inc=1, device_id=device, device_id_type=pl.DeviceIdType.MESH)

    def group(offset, carry):
        hello(place.member(place.other_slot(offset)))
        return carry

    lax.fori_loop(1, GROUP, group, 0)
    total = GROUP - 1
    if tree:

        def line(offset, carry):
            hello(place.at(z=place.deeper(offset)))
            return carry

        lax.fori_loop(1, place.depth, line, 0)
        hello(place.at(x=1 - place.x))
        hello(place.at(y=1 - place.y))
        hello(place.at(core=1 - place.core))
        total += place.depth + 2
    if parts > 1 and tree:

        @pl.when(place.part > 0)
        def _():
            hello(place.member(place.slot, place.part - 1))

        @pl.when(place.part < parts - 1)
        def _():
            hello(place.member(place.slot, place.part + 1))

        total += jnp.where(place.part > 0, 1, 0) + jnp.where(place.part < parts - 1, 1, 0)
    pl.semaphore_wait(barrier, total)


def halves_of(columns):
    if columns < 2 * LANES:
        return ((0, columns, "yx"),)
    return ((0, columns // 2, "yx"), (columns // 2, columns // 2, "xy"))


class Gather:
    def __init__(self, place, src, dst, send, recv, local):
        self.place, self.src, self.dst = place, src, dst
        self.send, self.recv, self.local = send, recv, local
        self.halves = halves_of(dst.shape[-1])
        self.lines = place.depth - 1

    @staticmethod
    def semaphores(depth):
        return depth + 8

    def cut(self, half, *index):
        start, width, _ = half
        return self.dst.at[index + (slice(None), pl.ds(start, width))]

    def pair(self, half, first, x, y):
        place, every = self.place, slice(None)
        if first:
            return self.cut(half, x, place.core, every, y)
        if half[2] == "yx":
            return self.cut(half, x, place.core, every, every)
        return self.cut(half, every, place.core, every, y)

    def across(self, half, first):
        place = self.place
        if (half[2] == "yx") == first:
            return place.x, 1 - place.y
        return 1 - place.x, place.y

    def line(self, offset, come):
        place = self.place
        z = place.deeper(-offset) if come else place.z
        return remote(
            self.src,
            self.dst.at[place.x, place.core, z, place.y],
            self.send.at[offset - 1],
            self.recv.at[offset - 1],
            place.at(z=place.deeper(offset)),
        )

    def own(self):
        place = self.place
        return pltpu.make_async_copy(
            self.src, self.dst.at[place.x, place.core, place.z, place.y], self.local
        )

    def exchange(self, number, first, come):
        half = self.halves[number]
        place = self.place
        x, y = self.across(half, first)
        slot = self.lines + (0 if first else 2) + number
        mine = self.pair(half, first, place.x, place.y)
        landing = self.pair(half, first, x, y) if come else mine
        return remote(
            mine, landing, self.send.at[slot], self.recv.at[slot], place.at(x=x, y=y)
        )

    def hand(self, which, come):
        place, every = self.place, slice(None)
        slot = self.lines + 4 + which
        core = 1 - place.core if come else place.core

        def region(core):
            if which == 0:
                return self.dst.at[place.x, core, every, place.y]
            number = (which - 1) % 2
            half = self.halves[number]
            first = which < 3
            x, y = self.across(half, first)
            if first:
                return self.cut(half, x, core, every, y)
            if half[2] == "yx":
                return self.cut(half, x, core, every, every)
            return self.cut(half, every, core, every, y)

        return remote(
            region(place.core),
            region(core),
            self.send.at[slot],
            self.recv.at[slot],
            place.at(core=1 - place.core),
        )

    def start_line(self):
        for offset in range(1, self.lines + 1):
            self.line(offset, False).start()
        self.own().start()

    def start_first(self):
        self.own().wait()
        for offset in range(1, self.lines + 1):
            self.line(offset, True).wait_recv()
        for number in range(len(self.halves)):
            self.exchange(number, True, False).start()
        self.hand(0, False).start()

    def start_second(self):
        for number in range(len(self.halves)):
            self.exchange(number, True, True).wait_recv()
            self.exchange(number, False, False).start()
            self.hand(1 + number, False).start()

    def start_last(self):
        for number in range(len(self.halves)):
            self.exchange(number, False, True).wait_recv()
            self.hand(3 + number, False).start()

    def hands(self):
        for number in range(len(self.halves)):
            yield 1 + number
            yield 3 + number

    def finish(self):
        self.hand(0, True).wait_recv()
        for which in self.hands():
            self.hand(which, True).wait_recv()

    def drain(self):
        for offset in range(1, self.lines + 1):
            self.line(offset, False).wait_send()
        for number in range(len(self.halves)):
            self.exchange(number, True, False).wait_send()
            self.exchange(number, False, False).wait_send()
        self.hand(0, False).wait_send()
        for which in self.hands():
            self.hand(which, False).wait_send()


class Reduce:
    def __init__(self, place, part, out, rc, total, ra, rb, fa, fb, rz, send, recv):
        self.place, self.part, self.out = place, part, out
        self.rc, self.total, self.rz = rc, total, rz
        self.second, self.first = (ra, rb), (fa, fb)
        self.send, self.recv = send, recv
        self.halves = halves_of(part.shape[-1])
        self.lines = place.depth - 1

    @staticmethod
    def semaphores(depth):
        return depth + 4

    @staticmethod
    def scratch(depth, rows, cols, dtype):
        wide = halves_of(cols)[0][1]
        return [
            VMEM((2, depth, 2, rows, cols), dtype),
            VMEM((2, depth, 2, rows, cols), dtype),
            VMEM((depth, 2, rows, wide), dtype),
            VMEM((2, depth, rows, wide), dtype),
            VMEM((depth, rows, wide), dtype),
            VMEM((depth, rows, wide), dtype),
            VMEM((depth - 1, rows, cols), dtype),
            pltpu.SemaphoreType.DMA((Reduce.semaphores(depth),)),
            pltpu.SemaphoreType.DMA((Reduce.semaphores(depth),)),
        ]

    def core(self):
        place, every = self.place, slice(None)
        return remote(
            self.part.at[every, 1 - place.core],
            self.rc,
            self.send.at[0],
            self.recv.at[0],
            place.at(core=1 - place.core),
        )

    def cut(self, half, *index):
        start, width, _ = half
        return index + (slice(None), pl.ds(start, width))

    def exchange(self, number, second):
        place, every = self.place, slice(None)
        half = self.halves[number]
        slot = (1 if second else 3) + number
        over_x = (half[2] == "yx") == second
        device = place.at(x=1 - place.x) if over_x else place.at(y=1 - place.y)
        if second:
            index = (1 - place.x, every, every) if over_x else (every, every, 1 - place.y)
            landing = self.second[number]
        else:
            index = (1 - place.x, every, place.y) if over_x else (place.x, every, 1 - place.y)
            landing = self.first[number]
        return remote(
            self.total.at[self.cut(half, *index)],
            landing,
            self.send.at[slot],
            self.recv.at[slot],
            device,
        )

    def line(self, offset):
        place = self.place
        return remote(
            self.total.at[place.x, place.deeper(offset), place.y],
            self.rz.at[offset - 1],
            self.send.at[4 + offset],
            self.recv.at[4 + offset],
            place.at(z=place.deeper(offset)),
        )

    def start_core(self):
        self.core().start()

    def start_second(self):
        place = self.place
        self.core().wait_recv()
        dtype = self.total.dtype

        def add(z, carry):
            for x in range(2):
                for y in range(2):
                    self.total[x, z, y] = (
                        self.part[x, place.core, z, y].astype(F32) + self.rc[x, z, y].astype(F32)
                    ).astype(dtype)
            return carry

        lax.fori_loop(0, place.depth, add, 0)
        for number in range(len(self.halves)):
            self.exchange(number, True).start()

    def accumulate(self, index, value):
        self.total[index] = (self.total[index].astype(F32) + value.astype(F32)).astype(
            self.total.dtype
        )

    def start_first(self):
        place = self.place
        for number, half in enumerate(self.halves):
            self.exchange(number, True).wait_recv()
            landed = self.second[number]

            def add(z, carry):
                for other in range(2):
                    if half[2] == "yx":
                        self.accumulate(self.cut(half, place.x, z, other), landed[z, other])
                    else:
                        self.accumulate(self.cut(half, other, z, place.y), landed[other, z])
                return carry

            lax.fori_loop(0, place.depth, add, 0)
            self.exchange(number, False).start()

    def start_line(self):
        place = self.place
        for number, half in enumerate(self.halves):
            self.exchange(number, False).wait_recv()
            landed = self.first[number]

            def add(z, carry):
                self.accumulate(self.cut(half, place.x, z, place.y), landed[z])
                return carry

            lax.fori_loop(0, place.depth, add, 0)
        for offset in range(1, self.lines + 1):
            self.line(offset).start()

    def finish(self):
        place = self.place
        for offset in range(1, self.lines + 1):
            self.line(offset).wait_recv()
        result = self.total[place.x, place.z, place.y].astype(F32)
        for offset in range(1, self.lines + 1):
            result = result + self.rz[offset - 1].astype(F32)
        self.out[...] = result

    def drain(self):
        self.core().wait_send()
        for number in range(len(self.halves)):
            self.exchange(number, True).wait_send()
            self.exchange(number, False).wait_send()
        for offset in range(1, self.lines + 1):
            self.line(offset).wait_send()


def iota(shape, dim):
    return lax.broadcasted_iota(jnp.int32, shape, dim)


def dot(left, right):
    return lax.dot_general(left, right, (((1,), (0,)), ((), ())), preferred_element_type=F32)


def dot_nt(left, right):
    return lax.dot_general(left, right, (((1,), (1,)), ((), ())), preferred_element_type=F32)


def dot_tn(left, right):
    return lax.dot_general(left, right, (((0,), (0,)), ((), ())), preferred_element_type=F32)


def shift_of(size):
    assert size & (size - 1) == 0
    return size.bit_length() - 1


def spread_bias(gathered, offset, per, total):
    rows = gathered.shape[0]
    column = iota((LANES, total), 1)
    pick = iota((LANES, total), 0) == offset + (column & (per - 1))
    spread = dot(gathered.astype(BF16), pick.astype(BF16))
    owner = jnp.right_shift(iota((rows, total), 1), shift_of(per)) * 8
    return jnp.sum(jnp.where(iota((rows, total), 0) == owner, spread, 0.0), axis=0, keepdims=True)


def fold_bias(row, rows, offset, per):
    total = row.shape[1]
    owner = jnp.right_shift(iota((rows, total), 1), shift_of(per)) * 8
    chosen = jnp.where(iota((rows, total), 0) == owner, row, 0.0)
    column = iota((total, LANES), 0)
    put = iota((total, LANES), 1) == offset + (column & (per - 1))
    return lax.dot_general(
        chosen,
        put.astype(F32),
        (((1,), (0,)), ((), ())),
        precision=lax.Precision.HIGHEST,
        preferred_element_type=F32,
    )


def bias_places(devices, width, hidden):
    per, per_up = width // devices, hidden // devices
    return {
        "query": (0, per),
        "value": (per, per),
        "output": (2 * per, per),
        "down": (3 * per, per),
        "up": (4 * per, per_up),
    }


def project_kernel(
    blocks,
    parts,
    window,
    docs,
    places,
    x_ref,
    seg_ref,
    aux_ref,
    win_ref,
    wo_ref,
    wup_ref,
    wdown_ref,
    qt_ref,
    kv_ref,
    starts_ref,
    gwin,
    gwo,
    gwup,
    gwdown,
    gaux,
    segs,
    tile,
    qs,
    ks,
    *sems,
):
    place = Place(blocks)
    (
        win_s,
        win_r,
        aux_s,
        aux_r,
        wo_s,
        wo_r,
        wup_s,
        wup_r,
        wdown_s,
        wdown_r,
        seg_s,
        seg_r,
        q_s,
        q_r,
        k_s,
        k_r,
        halo_s,
        halo_r,
        local,
    ) = sems
    greet(place, parts, True)
    g_win = Gather(place, win_ref, gwin, win_s, win_r, local.at[0])
    g_aux = Gather(place, aux_ref, gaux, aux_s, aux_r, local.at[1])
    g_wo = Gather(place, wo_ref, gwo, wo_s, wo_r, local.at[2])
    g_wup = Gather(place, wup_ref, gwup, wup_s, wup_r, local.at[3])
    g_wdown = Gather(place, wdown_ref, gwdown, wdown_s, wdown_r, local.at[4])
    rest = (g_wo, g_wup, g_wdown)
    g_win.start_line()
    g_aux.start_line()

    row = iota((16, LANES), 0)
    numbers = seg_ref[...].astype(F32)
    tile[...] = jnp.where(row == 0, numbers[0:1], numbers[1:2]).astype(BF16)
    segs[window + place.slot] = tile[...]

    def seg_copy(offset, come):
        landing = place.other_slot(-offset) if come else place.slot
        return remote(
            tile,
            segs.at[window + landing],
            seg_s.at[offset],
            seg_r.at[offset],
            place.member(place.other_slot(offset)),
        )

    def seg_start(offset, carry):
        seg_copy(offset, False).start()
        return carry

    lax.fori_loop(1, GROUP, seg_start, 0)

    g_win.start_first()
    g_aux.start_first()
    for gather in rest:
        gather.start_line()
    g_win.start_second()
    g_aux.start_second()

    def seg_wait(offset, carry):
        seg_copy(offset, True).wait_recv()
        return carry

    lax.fori_loop(1, GROUP, seg_wait, 0)

    def seg_halo(part):
        return remote(
            segs.at[pl.ds(GROUP, window)],
            segs.at[pl.ds(0, window)],
            halo_s.at[window],
            halo_r.at[window],
            place.member(place.slot, part),
        )

    if parts > 1:

        @pl.when(place.part < parts - 1)
        def _():
            seg_halo(place.part + 1).start()

    g_win.start_last()
    g_aux.start_last()
    g_win.finish()
    g_aux.finish()

    width = x_ref.shape[-1]
    devices = gaux.shape[0] * gaux.shape[1] * gaux.shape[2] * gaux.shape[3]
    aux = gaux[...].reshape(devices * 8, LANES)
    bias_q = spread_bias(aux, *places["query"], width)
    bias_v = spread_bias(aux, *places["value"], width)
    tokens = x_ref[...].reshape(2 * LANES, width)
    low_lane = iota((LANES, LANES), 1) < HD
    wide = 2 * LANES
    for t in range(width // wide):

        def column(kind):
            weight = gwin[:, :, :, :, :, pl.ds(kind * width + t * wide, wide)]
            return dot(tokens, weight.reshape(width, wide))

        cols = slice(t * wide, (t + 1) * wide)
        q = (column(0) + bias_q[:, cols]).astype(BF16).astype(F32) * 0.125
        k = column(1).astype(BF16).astype(F32)
        v = (column(2) + bias_v[:, cols]).astype(BF16).astype(F32)
        for s in range(2):
            for u in range(2):
                first = s * HEADS + t * 4 + u * 2
                here = (slice(s * LANES, (s + 1) * LANES), slice(u * LANES, (u + 1) * LANES))
                turned = q[here].T.astype(BF16)
                qs[first] = turned[:HD]
                qs[first + 1] = turned[HD:]
                k_here, v_here = k[here], v[here]
                ks[first] = jnp.where(low_lane, k_here, pltpu.roll(v_here, HD, 1)).astype(BF16)
                ks[first + 1] = jnp.where(low_lane, pltpu.roll(k_here, HD, 1), v_here).astype(BF16)

    def q_copy(offset, come):
        landing = place.other_slot(-offset) if come else place.slot
        target = place.other_slot(offset)
        return remote(
            qs.at[target], qt_ref.at[landing], q_s.at[offset], q_r.at[offset], place.member(target)
        )

    def k_copy(offset, come):
        landing = place.other_slot(-offset) if come else place.slot
        target = place.other_slot(offset)
        return remote(
            ks.at[target],
            kv_ref.at[window + landing],
            k_s.at[offset],
            k_r.at[offset],
            place.member(target),
        )

    def qk_start(offset, carry):
        k_copy(offset, False).start()
        q_copy(offset, False).start()
        return carry

    lax.fori_loop(1, GROUP, qk_start, 0)
    qt_ref[place.slot] = qs[place.slot]
    kv_ref[window + place.slot] = ks[place.slot]

    for gather in rest:
        gather.start_first()

    if parts > 1:

        @pl.when(place.part < parts - 1)
        def _():
            seg_halo(place.part + 1).wait_send()

        @pl.when(place.part > 0)
        def _():
            seg_halo(place.part - 1).wait_recv()

    span = window + GROUP
    sequence = lax.div(place.slot, HEADS)
    chosen = jnp.where(iota((span, 16, LANES), 1) == sequence, segs[...].astype(F32), 0.0)
    seen = jnp.sum(chosen, axis=1)
    outside = (iota((span, LANES), 0) < window) & (place.part == 0)
    seen = jnp.where(outside, -1.0, seen)
    own = seen[window:]
    start = jnp.zeros((GROUP, LANES), F32)
    for number in range(docs):
        count = jnp.sum(jnp.where(seen == number - 1, 1.0, 0.0), axis=0, keepdims=True)
        count = jnp.sum(count, axis=1, keepdims=True)
        start = start + jnp.where(own >= number, count, 0.0)
    starts_ref[...] = start.astype(jnp.int32)

    for gather in rest:
        gather.start_second()

    def halo_copy(entry, part):
        return remote(
            kv_ref.at[GROUP + entry],
            kv_ref.at[entry],
            halo_s.at[entry],
            halo_r.at[entry],
            place.member(place.slot, part),
        )

    def pass_on(source):
        if parts > 1:

            @pl.when((place.part < parts - 1) & (source >= GROUP - window))
            def _():
                halo_copy(source - (GROUP - window), place.part + 1).start()

    pass_on(place.slot)

    def qk_wait(offset, carry):
        k_copy(offset, True).wait_recv()
        q_copy(offset, True).wait_recv()
        pass_on(place.other_slot(-offset))
        return carry

    lax.fori_loop(1, GROUP, qk_wait, 0)
    for gather in rest:
        gather.start_last()
    if parts > 1:

        @pl.when(place.part > 0)
        def _():
            def wait(entry, carry):
                halo_copy(entry, place.part - 1).wait_recv()
                return carry

            lax.fori_loop(0, window, wait, 0)

    for gather in rest:
        gather.finish()

    if parts > 1:

        @pl.when(place.part < parts - 1)
        def _():
            def wait(entry, carry):
                halo_copy(entry, place.part + 1).wait_send()
                return carry

            lax.fori_loop(0, window, wait, 0)

    def sent(offset, carry):
        seg_copy(offset, False).wait_send()
        q_copy(offset, False).wait_send()
        k_copy(offset, False).wait_send()
        return carry

    lax.fori_loop(1, GROUP, sent, 0)
    for gather in (g_win, g_aux) + rest:
        gather.drain()


def block_scores(kv, q_wide, u, start, q_place):
    scores = dot(kv, q_wide)
    k_place = u * BLOCK + iota((BLOCK, BLOCK), 0)
    visible = (k_place >= start) & (k_place <= q_place)
    return jnp.where(visible, scores, NEG)


def two(ref, index):
    return jnp.concatenate([ref[index], ref[index + 1]], axis=1)


def two_rows(ref, index):
    return jnp.concatenate([ref[pl.ds(index, 1)], ref[pl.ds(index + 1, 1)]], axis=1)


def attend_kernel(window, qt_ref, kv_ref, starts_ref, first_ref, ot_ref, of_ref, lse_ref, kvt):
    span = window + GROUP

    def turn(c, carry):
        kvt[c] = kv_ref[c].T
        return carry

    lax.fori_loop(0, span, turn, 0)

    def q_block(m, carry):
        q_wide = jnp.concatenate([two(qt_ref, 2 * m), jnp.zeros((HD, BLOCK), BF16)], axis=0)
        start = two_rows(starts_ref, 2 * m)
        diagonal = window // 2 + m
        q_place = diagonal * BLOCK + iota((1, BLOCK), 1)
        lowest = lax.div(first_ref[2 * m, 0], BLOCK)

        def k_block(step, state):
            peak, total, out = state
            u = diagonal - step
            kv = kv_ref[pl.ds(2 * u, 2)].reshape(BLOCK, LANES)
            scores = block_scores(kv, q_wide, u, start, q_place)
            newest = jnp.maximum(peak, jnp.max(scores, axis=0, keepdims=True))
            weights = jnp.exp(scores - newest)
            factor = jnp.exp(peak - newest)
            values = two(kvt, 2 * u)[HD:]
            out = out * factor + dot(values, weights.astype(BF16))
            total = total * factor + jnp.sum(weights, axis=0, keepdims=True)
            return newest, total, out

        state = (
            jnp.full((1, BLOCK), NEG, F32),
            jnp.zeros((1, BLOCK), F32),
            jnp.zeros((HD, BLOCK), F32),
        )
        peak, total, out = lax.fori_loop(0, diagonal - lowest + 1, k_block, state)
        out = out / total
        lse = peak + jnp.log(total)
        for side in range(2):
            lanes = slice(side * LANES, (side + 1) * LANES)
            of_ref[2 * m + side] = out[:, lanes]
            ot_ref[2 * m + side] = out[:, lanes].astype(BF16)
            lse_ref[pl.ds(2 * m + side, 1)] = lse[:, lanes]
        return carry

    lax.fori_loop(0, GROUP // 2, q_block, 0)


def middle_kernel(
    blocks,
    parts,
    places,
    ot_ref,
    x_ref,
    grad_ref,
    alphas_ref,
    wo_ref,
    wup_ref,
    wdown_ref,
    gaux_ref,
    out_ref,
    doct_ref,
    gres_ref,
    gup_ref,
    gdown_ref,
    gout_ref,
    rows_ref,
    up_row_ref,
    mixed_t,
    dos,
    act_s,
    gpre_s,
    o_s,
    o_r,
    d_s,
    d_r,
):
    place = Place(blocks)
    greet(place, parts, False)

    def o_copy(offset, come):
        landing = place.other_slot(-offset) if come else place.slot
        target = place.other_slot(offset)
        return remote(
            ot_ref.at[target], mixed_t.at[landing], o_s.at[offset], o_r.at[offset], place.member(target)
        )

    def d_copy(offset, come):
        landing = place.other_slot(-offset) if come else place.slot
        target = place.other_slot(offset)
        return remote(
            dos.at[target], doct_ref.at[landing], d_s.at[offset], d_r.at[offset], place.member(target)
        )

    def loop(call):
        def step(offset, carry):
            call(offset)
            return carry

        lax.fori_loop(1, GROUP, step, 0)

    loop(lambda offset: o_copy(offset, False).start())
    mixed_t[place.slot] = ot_ref[place.slot]

    width, hidden = wup_ref.shape
    a0, a1 = alphas_ref[0], alphas_ref[1]
    bias_out = spread_bias(gaux_ref[...], *places["output"], width)
    bias_down = spread_bias(gaux_ref[...], *places["down"], width)
    bias_up = spread_bias(gaux_ref[...], *places["up"], hidden)
    rows = 2 * LANES
    tokens = x_ref[...].reshape(rows, width).astype(F32)
    grads = grad_ref[...].reshape(rows, width).astype(F32)
    grad_ffn = (a1 * grads).astype(BF16)

    loop(lambda offset: o_copy(offset, True).wait_recv())

    mixed_turned = mixed_t[...].reshape(2, width, LANES)
    mixed = jnp.concatenate([mixed_turned[0].T, mixed_turned[1].T], axis=0)
    branch = dot(mixed, wo_ref[...]) + bias_out
    attn_term = a0 * branch
    residual = tokens + attn_term
    hidden_in = residual.astype(BF16)

    ffn = jnp.zeros((rows, width), F32) + bias_down
    grad_res = grads
    wide = 512
    for t in range(hidden // wide):
        cols = pl.ds(t * wide, wide)
        w_up = wup_ref[:, cols]
        w_down = wdown_ref[cols, :]
        pre = dot(hidden_in, w_up) + bias_up[:, t * wide : (t + 1) * wide]
        phi = 0.5 * (1.0 + lax.erf(pre * (1.0 / math.sqrt(2.0))))
        act = (pre * phi).astype(BF16)
        act_s[:, cols] = act
        ffn = ffn + dot(act, w_down)
        slope = phi + pre * jnp.exp(-0.5 * pre * pre) * (1.0 / math.sqrt(2.0 * math.pi))
        gpre = (dot_nt(grad_ffn, w_down) * slope).astype(BF16)
        gpre_s[:, cols] = gpre
        grad_res = grad_res + dot_nt(gpre, w_up)
    gres_ref[...] = grad_res
    grad_branch = (a0 * grad_res).astype(BF16)
    grad_mixed = dot_nt(grad_branch, wo_ref[...]).astype(BF16).astype(F32)
    for s in range(2):
        turned = grad_mixed[s * LANES : (s + 1) * LANES].T.astype(BF16)
        dos[pl.ds(s * HEADS, HEADS)] = turned.reshape(HEADS, HD, LANES)
    loop(lambda offset: d_copy(offset, False).start())
    doct_ref[place.slot] = dos[place.slot]

    ffn_term = a1 * ffn
    stream = residual + ffn_term
    out_ref[...] = stream.astype(BF16).reshape(2, LANES, width)

    def whole(values):
        return jnp.sum(jnp.sum(values, axis=0, keepdims=True), axis=1, keepdims=True)

    sums = (
        whole(stream * stream),
        whole(attn_term * attn_term),
        whole(ffn_term * ffn_term),
        whole(grad_res * branch),
        whole(grads * ffn),
    )
    lane = iota((1, width), 1)
    scalars = jnp.zeros((1, width), F32)
    for number, value in enumerate(sums):
        scalars = scalars + jnp.where(lane == number, value, 0.0)
    down_row = jnp.sum(grad_ffn.astype(F32), axis=0, keepdims=True)
    out_row = jnp.sum(grad_branch.astype(F32), axis=0, keepdims=True)
    row = iota((8, width), 0)
    rows_ref[...] = jnp.where(
        row == 0, down_row, jnp.where(row == 1, out_row, jnp.where(row == 2, scalars, 0.0))
    )
    gout_ref[...] = dot(
        jnp.concatenate([mixed_turned[0], mixed_turned[1]], axis=1), grad_branch
    ).astype(BF16)
    for t in range(hidden // wide):
        cols = pl.ds(t * wide, wide)
        gpre = gpre_s[:, cols]
        up_row_ref[:, cols] = jnp.zeros((8, wide), F32) + jnp.sum(
            gpre.astype(F32), axis=0, keepdims=True
        )
        gup_ref[:, cols] = dot_tn(hidden_in, gpre).astype(BF16)
        gdown_ref[cols, :] = dot_tn(act_s[:, cols], grad_ffn).astype(BF16)

    loop(lambda offset: d_copy(offset, True).wait_recv())
    loop(lambda offset: o_copy(offset, False).wait_send())
    loop(lambda offset: d_copy(offset, False).wait_send())


def attend_back_kernel(
    window, qt_ref, kv_ref, starts_ref, first_ref, of_ref, lse_ref, dot_ref, dqt_ref, dkv_ref, kvt, acc
):
    span = window + GROUP

    def turn(c, carry):
        kvt[c] = kv_ref[c].T
        acc[c] = jnp.zeros((LANES, LANES), F32)
        return carry

    lax.fori_loop(0, span, turn, 0)
    low_lane = iota((BLOCK, LANES), 1) < HD

    def q_block(m, carry):
        qt, dt = two(qt_ref, 2 * m), two(dot_ref, 2 * m)
        blank = jnp.zeros((HD, BLOCK), BF16)
        q_wide = jnp.concatenate([qt, blank], axis=0)
        d_wide = jnp.concatenate([blank, dt], axis=0)
        both = jnp.concatenate([qt, dt], axis=0).astype(F32).T
        q_rows = jnp.where(low_lane, both, 0.0).astype(BF16)
        d_rows = jnp.where(low_lane, 0.0, both).astype(BF16)
        start = two_rows(starts_ref, 2 * m)
        lse = two_rows(lse_ref, 2 * m)
        delta = jnp.sum(dt.astype(F32) * two(of_ref, 2 * m), axis=0, keepdims=True)
        diagonal = window // 2 + m
        q_place = diagonal * BLOCK + iota((1, BLOCK), 1)
        lowest = lax.div(first_ref[2 * m, 0], BLOCK)

        def k_block(step, dq):
            u = diagonal - step
            kv = kv_ref[pl.ds(2 * u, 2)].reshape(BLOCK, LANES)
            probs = jnp.exp(block_scores(kv, q_wide, u, start, q_place) - lse)
            grad_probs = dot(kv, d_wide)
            grad_scores = (probs * (grad_probs - delta)).astype(BF16)
            grad = dot(grad_scores, q_rows) + dot(probs.astype(BF16), d_rows)
            acc[pl.ds(2 * u, 2)] += grad.reshape(2, LANES, LANES)
            return dq + dot(two(kvt, 2 * u)[:HD], grad_scores)

        dq = lax.fori_loop(0, diagonal - lowest + 1, k_block, jnp.zeros((HD, BLOCK), F32))
        for side in range(2):
            lanes = slice(side * LANES, (side + 1) * LANES)
            dqt_ref[2 * m + side] = (dq[:, lanes] * 0.125).astype(BF16)
        return carry

    lax.fori_loop(0, GROUP // 2, q_block, 0)

    def put(c, carry):
        dkv_ref[c] = acc[c].astype(BF16)
        return carry

    lax.fori_loop(0, span, put, 0)


def finish_kernel(
    blocks,
    parts,
    window,
    places,
    dqt_ref,
    dkv_ref,
    x_ref,
    gres_ref,
    win_ref,
    rows_ref,
    up_row_ref,
    p_out,
    p_up,
    p_down,
    gx_ref,
    r_win,
    r_out,
    r_up,
    r_down,
    r_aux,
    p_win,
    p_aux,
    dq_in,
    dkv_in,
    halo_in,
    dkv_sum,
    gp,
    *more,
):
    place = Place(blocks)
    greet(place, parts, True)
    depth = place.depth
    count = 9
    trees = []
    for number, (part, out) in enumerate(
        ((p_out, r_out), (p_up, r_up), (p_down, r_down), (p_win, r_win), (p_aux, r_aux))
    ):
        trees.append(Reduce(place, part, out, *more[number * count : (number + 1) * count]))
    t_out, t_up, t_down, t_win, t_aux = trees
    q_s, q_r, k_s, k_r, halo_s, halo_r = more[5 * count :]
    early = (t_out, t_up, t_down)
    for tree in early:
        tree.start_core()

    def halo_copy(part):
        return remote(
            dkv_ref.at[pl.ds(0, window)],
            halo_in,
            halo_s.at[0],
            halo_r.at[0],
            place.member(place.slot, part),
        )

    if parts > 1:

        @pl.when(place.part > 0)
        def _():
            halo_copy(place.part - 1).start()

    def q_copy(offset, come):
        landing = place.other_slot(-offset) if come else place.slot
        target = place.other_slot(offset)
        return remote(
            dqt_ref.at[target], dq_in.at[landing], q_s.at[offset], q_r.at[offset], place.member(target)
        )

    def k_copy(offset, come):
        landing = place.other_slot(-offset) if come else place.slot
        target = place.other_slot(offset)
        return remote(
            dkv_sum.at[target],
            dkv_in.at[landing],
            k_s.at[offset],
            k_r.at[offset],
            place.member(target),
        )

    def loop(call):
        def step(offset, carry):
            call(offset)
            return carry

        lax.fori_loop(1, GROUP, step, 0)

    loop(lambda offset: q_copy(offset, False).start())
    dq_in[place.slot] = dqt_ref[place.slot]
    dkv_sum[...] = dkv_ref[pl.ds(window, GROUP)]
    if window < GROUP:

        def early_k(offset):
            @pl.when(place.other_slot(offset) < GROUP - window)
            def _():
                k_copy(offset, False).start()

        loop(early_k)

    for tree in early:
        tree.start_second()

    if parts > 1:

        @pl.when(place.part < parts - 1)
        def _():
            halo_copy(place.part + 1).wait_recv()

            def add(entry, carry):
                here = GROUP - window + entry
                dkv_sum[here] = (
                    dkv_sum[here].astype(F32) + halo_in[entry].astype(F32)
                ).astype(BF16)
                return carry

            lax.fori_loop(0, window, add, 0)

    def late_k(offset):
        @pl.when(place.other_slot(offset) >= GROUP - window)
        def _():
            k_copy(offset, False).start()

    loop(late_k)
    dkv_in[place.slot] = dkv_sum[place.slot]

    for tree in early:
        tree.start_first()

    loop(lambda offset: q_copy(offset, True).wait_recv())
    loop(lambda offset: k_copy(offset, True).wait_recv())

    width = x_ref.shape[-1]
    low_lane = iota((LANES, LANES), 1) < HD
    for s in range(2):
        rows = slice(s * LANES, (s + 1) * LANES)
        turned = dq_in[pl.ds(s * HEADS, HEADS)].reshape(width, LANES).astype(F32)
        gp[rows, 0:width] = turned.T.astype(BF16)
        for pair in range(HEADS // 2):
            even = dkv_in[s * HEADS + 2 * pair].astype(F32)
            odd = dkv_in[s * HEADS + 2 * pair + 1].astype(F32)
            keys = jnp.where(low_lane, even, pltpu.roll(odd, HD, 1))
            values = jnp.where(low_lane, pltpu.roll(even, HD, 1), odd)
            at = pair * LANES
            gp[rows, width + at : width + at + LANES] = keys.astype(BF16)
            gp[rows, 2 * width + at : 2 * width + at + LANES] = values.astype(BF16)

    tokens = x_ref[...].reshape(2 * LANES, width)
    tokens_turned = tokens.T
    wide = 512
    for t in range(3 * width // wide):
        cols = slice(t * wide, (t + 1) * wide)
        part = dot(tokens_turned, gp[:, cols]).astype(BF16)
        p_win[:, :, :, :, :, cols] = part.reshape(2, 2, depth, 2, width // (8 * depth), wide)
    t_win.start_core()

    devices = 8 * depth
    query_row = jnp.sum(gp[:, 0:width].astype(F32), axis=0, keepdims=True)
    value_row = jnp.sum(gp[:, 2 * width :].astype(F32), axis=0, keepdims=True)
    folded = (
        fold_bias(query_row, devices * 8, *places["query"])
        + fold_bias(value_row, devices * 8, *places["value"])
        + fold_bias(rows_ref[1:2], devices * 8, *places["output"])
        + fold_bias(rows_ref[0:1], devices * 8, *places["down"])
        + fold_bias(up_row_ref[0:1], devices * 8, *places["up"])
    )
    scalars = rows_ref[2:3, 0:LANES]
    folded = folded + jnp.where((iota((devices * 8, LANES), 0) & 7) == 1, scalars, 0.0)
    p_aux[...] = folded.reshape(2, 2, depth, 2, 8, LANES)
    t_aux.start_core()

    gx = gres_ref[...]
    for t in range(3 * width // wide):
        cols = slice(t * wide, (t + 1) * wide)
        gx = gx + dot_nt(gp[:, cols], win_ref[:, cols])
    gx_ref[...] = gx.astype(BF16).reshape(2, LANES, width)

    t_win.start_second()
    t_aux.start_second()
    for tree in early:
        tree.start_line()
    t_win.start_first()
    t_aux.start_first()
    t_win.start_line()
    t_aux.start_line()
    for tree in trees:
        tree.finish()

    loop(lambda offset: q_copy(offset, False).wait_send())
    loop(lambda offset: k_copy(offset, False).wait_send())
    if parts > 1:

        @pl.when(place.part > 0)
        def _():
            halo_copy(place.part - 1).wait_send()

    for tree in trees:
        tree.drain()


def call(kernel, out_shape, in_specs, out_specs, scratch, collective=None):
    return pl.pallas_call(
        kernel,
        out_shape=out_shape,
        in_specs=in_specs,
        out_specs=out_specs,
        scratch_shapes=scratch,
        compiler_params=pltpu.CompilerParams(
            collective_id=collective,
            has_side_effects=collective is not None,
            vmem_limit_bytes=VMEM_BYTES,
        ),
    )


def local(
    layer_input,
    segments,
    input_weight,
    output_weight,
    up_weight,
    down_weight,
    query_bias,
    value_bias,
    output_bias,
    up_bias,
    down_bias,
    alphas,
    out_grad,
):
    heads, blocks = lax.axis_size("head"), lax.axis_size("blk")
    depth, devices = blocks // 2, heads * blocks
    seqs, rows, width = layer_input.shape
    hidden = up_weight.shape[1]
    seq_len = rows * devices
    assert heads == 4 and seqs * HEADS == GROUP and rows == LANES
    longest = 16 * math.isqrt(seq_len)
    window, parts = longest // rows, devices // GROUP
    docs = 2 * seq_len // longest
    assert window <= GROUP and window % 2 == 0
    span = window + GROUP
    places = bias_places(devices, width, hidden)

    def shape(*dims, dtype=BF16):
        return jax.ShapeDtypeStruct(dims, dtype)

    vmem, smem, anywhere = (
        pl.BlockSpec(memory_space=VMEM),
        pl.BlockSpec(memory_space=pltpu.SMEM),
        pl.BlockSpec(memory_space=pl.ANY),
    )
    dma = pltpu.SemaphoreType.DMA

    aux = jnp.concatenate(
        [query_bias, value_bias, output_bias, down_bias, up_bias]
    ).astype(F32)
    aux = jnp.broadcast_to(jnp.pad(aux, (0, LANES - aux.shape[0]))[None], (8, LANES))
    lead = (2, 2, depth, 2)
    in_rows, up_rows = input_weight.shape[0], down_weight.shape[0]
    sems = Gather.semaphores(depth)
    queries, pairs, starts, g_win, g_wo, g_wup, g_wdown, g_aux = call(
        functools.partial(project_kernel, blocks, parts, window, docs, places),
        (
            shape(GROUP, HD, LANES),
            shape(span, LANES, LANES),
            shape(GROUP, LANES, dtype=jnp.int32),
            shape(*lead, in_rows, 3 * width),
            shape(*lead, in_rows, width),
            shape(*lead, in_rows, hidden),
            shape(*lead, up_rows, width),
            shape(*lead, 8, LANES, dtype=F32),
        ),
        [vmem] * 7,
        (vmem, vmem, vmem, vmem, anywhere, anywhere, anywhere, vmem),
        [
            VMEM((span, 16, LANES), BF16),
            VMEM((16, LANES), BF16),
            VMEM((GROUP, HD, LANES), BF16),
            VMEM((GROUP, LANES, LANES), BF16),
        ]
        + [dma((sems,))] * 10
        + [dma((GROUP,))] * 6
        + [dma((window + 1,))] * 2
        + [dma((5,))],
        collective=0,
    )(layer_input, segments, aux, input_weight, output_weight, up_weight, down_weight)

    attended, attended_wide, lse = call(
        functools.partial(attend_kernel, window),
        (
            shape(GROUP, HD, LANES),
            shape(GROUP, HD, LANES, dtype=F32),
            shape(GROUP, LANES, dtype=F32),
        ),
        [vmem, vmem, vmem, smem],
        (vmem, vmem, vmem),
        [VMEM((span, LANES, LANES), BF16)],
    )(queries, pairs, starts, starts)

    full_in = g_win.reshape(width, 3 * width)
    full_out = g_wo.reshape(width, width)
    full_up = g_wup.reshape(width, hidden)
    full_down = g_wdown.reshape(hidden, width)
    flat_aux = g_aux.reshape(devices * 8, LANES)
    layer_output, grad_attended, grad_res, p_up, p_down, p_out, bias_rows, up_row = call(
        functools.partial(middle_kernel, blocks, parts, places),
        (
            shape(seqs, rows, width),
            shape(GROUP, HD, LANES),
            shape(seqs * rows, width, dtype=F32),
            shape(width, hidden),
            shape(hidden, width),
            shape(width, width),
            shape(8, width, dtype=F32),
            shape(8, hidden, dtype=F32),
        ),
        [vmem, vmem, vmem, smem, vmem, vmem, vmem, vmem],
        (vmem,) * 8,
        [
            VMEM((GROUP, HD, LANES), BF16),
            VMEM((GROUP, HD, LANES), BF16),
            VMEM((seqs * rows, hidden), BF16),
            VMEM((seqs * rows, hidden), BF16),
        ]
        + [dma((GROUP,))] * 4,
        collective=1,
    )(attended, layer_input, out_grad, alphas, full_out, full_up, full_down, flat_aux)

    grad_queries, grad_pairs = call(
        functools.partial(attend_back_kernel, window),
        (shape(GROUP, HD, LANES), shape(span, LANES, LANES)),
        [vmem, vmem, vmem, smem, vmem, vmem, vmem],
        (vmem, vmem),
        [VMEM((span, LANES, LANES), BF16), VMEM((span, LANES, LANES), F32)],
    )(queries, pairs, starts, starts, attended_wide, lse, grad_attended)

    reduced = (
        (in_rows, width, BF16),
        (in_rows, hidden, BF16),
        (up_rows, width, BF16),
        (in_rows, 3 * width, BF16),
        (8, LANES, F32),
    )
    scratch = [
        VMEM((*lead, in_rows, 3 * width), BF16),
        VMEM((*lead, 8, LANES), F32),
        VMEM((GROUP, HD, LANES), BF16),
        VMEM((GROUP, LANES, LANES), BF16),
        VMEM((window, LANES, LANES), BF16),
        VMEM((GROUP, LANES, LANES), BF16),
        VMEM((seqs * rows, 3 * width), BF16),
    ]
    for sizes in reduced:
        scratch += Reduce.scratch(depth, *sizes)
    scratch += [dma((GROUP,))] * 4 + [dma((1,))] * 2
    input_grad, win_grad, out_weight_grad, up_grad, down_grad, sums = call(
        functools.partial(finish_kernel, blocks, parts, window, places),
        (
            shape(seqs, rows, width),
            shape(in_rows, 3 * width, dtype=F32),
            shape(in_rows, width, dtype=F32),
            shape(in_rows, hidden, dtype=F32),
            shape(up_rows, width, dtype=F32),
            shape(8, LANES, dtype=F32),
        ),
        [vmem] * 10,
        (vmem,) * 6,
        scratch,
        collective=2,
    )(
        grad_queries,
        grad_pairs,
        layer_input,
        grad_res,
        full_in,
        bias_rows,
        up_row,
        p_out.reshape(*lead, in_rows, width),
        p_up.reshape(*lead, in_rows, hidden),
        p_down.reshape(*lead, up_rows, width),
    )

    def bias_grad(name):
        offset, per = places[name]
        return sums[0, offset : offset + per]

    rms_values = jnp.sqrt(sums[1, 0:3] / (seqs * seq_len * width))
    return (
        layer_output,
        input_grad,
        win_grad,
        out_weight_grad,
        up_grad,
        down_grad,
        bias_grad("query"),
        bias_grad("value"),
        bias_grad("output"),
        bias_grad("up"),
        bias_grad("down"),
        sums[1, 3:5],
        rms_values,
    )


def solution(mesh):
    tokens = P(None, ("head", "blk"), None)
    rows, flat = P(("head", "blk"), None), P(("head", "blk"))
    return jax.shard_map(
        local,
        mesh=mesh,
        in_specs=(
            tokens,
            P(None, ("head", "blk")),
            rows,
            rows,
            rows,
            rows,
            flat,
            flat,
            flat,
            flat,
            flat,
            P(),
            tokens,
        ),
        out_specs=(
            tokens,
            tokens,
            rows,
            rows,
            rows,
            rows,
            flat,
            flat,
            flat,
            flat,
            flat,
            P(),
            P(),
        ),
        check_vma=False,
    )
```

```python
import functools
import math

import jax
import jax.numpy as jnp
from jax import lax
from jax.experimental import pallas as pl
from jax.experimental.pallas import tpu as pltpu
from jax.sharding import PartitionSpec as P

HEADS = 8
HD = 64
LANES = 128
GROUP = 16
BLOCK = 256
VMEM_BYTES = 60 * 1024 * 1024
F32 = jnp.float32
BF16 = jnp.bfloat16
VMEM = pltpu.VMEM
NEG = -1e30


class Place:
    def __init__(self, blocks):
        self.blocks = blocks
        self.depth = blocks // 2
        head = lax.axis_index("head")
        block = lax.axis_index("blk")
        self.x, self.core = lax.div(head, 2), lax.rem(head, 2)
        self.z, self.y = lax.div(block, 2), lax.rem(block, 2)
        flat = head * blocks + block
        self.part, self.slot = lax.div(flat, GROUP), lax.rem(flat, GROUP)

    def at(self, x=None, core=None, z=None, y=None):
        x = self.x if x is None else x
        core = self.core if core is None else core
        z = self.z if z is None else z
        y = self.y if y is None else y
        return (x * 2 + core, z * 2 + y)

    def deeper(self, offset):
        return lax.rem(self.z + offset + self.depth, self.depth)

    def member(self, slot, part=None):
        part = self.part if part is None else part
        flat = part * GROUP + slot
        return (lax.div(flat, self.blocks), lax.rem(flat, self.blocks))

    def other_slot(self, offset):
        return lax.rem(self.slot + offset + GROUP, GROUP)


def remote(src, dst, send, recv, device):
    return pltpu.make_async_remote_copy(
        src_ref=src,
        dst_ref=dst,
        send_sem=send,
        recv_sem=recv,
        device_id=device,
        device_id_type=pl.DeviceIdType.MESH,
    )


def greet(place, parts, tree):
    barrier = pltpu.get_barrier_semaphore()

    def hello(device):
        pl.semaphore_signal(barrier, inc=1, device_id=device, device_id_type=pl.DeviceIdType.MESH)

    def group(offset, carry):
        hello(place.member(place.other_slot(offset)))
        return carry

    lax.fori_loop(1, GROUP, group, 0)
    total = GROUP - 1
    if tree:

        def line(offset, carry):
            hello(place.at(z=place.deeper(offset)))
            return carry

        lax.fori_loop(1, place.depth, line, 0)
        hello(place.at(x=1 - place.x))
        hello(place.at(y=1 - place.y))
        hello(place.at(core=1 - place.core))
        total += place.depth + 2
    if parts > 1 and tree:

        @pl.when(place.part > 0)
        def _():
            hello(place.member(place.slot, place.part - 1))

        @pl.when(place.part < parts - 1)
        def _():
            hello(place.member(place.slot, place.part + 1))

        total += jnp.where(place.part > 0, 1, 0) + jnp.where(place.part < parts - 1, 1, 0)
    pl.semaphore_wait(barrier, total)


def halves_of(columns):
    if columns < 2 * LANES:
        return ((0, columns, "yx"),)
    return ((0, columns // 2, "yx"), (columns // 2, columns // 2, "xy"))


class Gather:
    def __init__(self, place, src, dst, send, recv, local, cols=None):
        self.place, self.src, self.dst = place, src, dst
        self.send, self.recv, self.local = send, recv, local
        self.start, self.width = cols or (0, dst.shape[-1])
        self.halves = halves_of(self.width)
        self.lines = place.depth - 1

    @staticmethod
    def semaphores(depth):
        return depth + 8

    def cut(self, half, *index):
        start, width, _ = half
        return self.dst.at[index + (slice(None), pl.ds(self.start + start, width))]

    def shard(self):
        return self.src.at[:, pl.ds(self.start, self.width)]

    def whole(self, *index):
        return self.dst.at[index + (slice(None), pl.ds(self.start, self.width))]

    def pair(self, half, first, x, y):
        place, every = self.place, slice(None)
        if first:
            return self.cut(half, x, place.core, every, y)
        if half[2] == "yx":
            return self.cut(half, x, place.core, every, every)
        return self.cut(half, every, place.core, every, y)

    def across(self, half, first):
        place = self.place
        if (half[2] == "yx") == first:
            return place.x, 1 - place.y
        return 1 - place.x, place.y

    def line(self, offset, come):
        place = self.place
        z = place.deeper(-offset) if come else place.z
        return remote(
            self.shard(),
            self.whole(place.x, place.core, z, place.y),
            self.send.at[offset - 1],
            self.recv.at[offset - 1],
            place.at(z=place.deeper(offset)),
        )

    def own(self):
        place = self.place
        return pltpu.make_async_copy(
            self.shard(), self.whole(place.x, place.core, place.z, place.y), self.local
        )

    def exchange(self, number, first, come):
        half = self.halves[number]
        place = self.place
        x, y = self.across(half, first)
        slot = self.lines + (0 if first else 2) + number
        mine = self.pair(half, first, place.x, place.y)
        landing = self.pair(half, first, x, y) if come else mine
        return remote(
            mine, landing, self.send.at[slot], self.recv.at[slot], place.at(x=x, y=y)
        )

    def hand(self, which, come):
        place, every = self.place, slice(None)
        slot = self.lines + 4 + which
        core = 1 - place.core if come else place.core

        def region(core):
            if which == 0:
                return self.whole(place.x, core, every, place.y)
            number = (which - 1) % 2
            half = self.halves[number]
            first = which < 3
            x, y = self.across(half, first)
            if first:
                return self.cut(half, x, core, every, y)
            if half[2] == "yx":
                return self.cut(half, x, core, every, every)
            return self.cut(half, every, core, every, y)

        return remote(
            region(place.core),
            region(core),
            self.send.at[slot],
            self.recv.at[slot],
            place.at(core=1 - place.core),
        )

    def start_line(self):
        for offset in range(1, self.lines + 1):
            self.line(offset, False).start()
        self.own().start()

    def start_first(self):
        self.own().wait()
        for offset in range(1, self.lines + 1):
            self.line(offset, True).wait_recv()
        for number in range(len(self.halves)):
            self.exchange(number, True, False).start()
        self.hand(0, False).start()

    def start_second(self):
        for number in range(len(self.halves)):
            self.exchange(number, True, True).wait_recv()
            self.exchange(number, False, False).start()
            self.hand(1 + number, False).start()

    def start_last(self):
        for number in range(len(self.halves)):
            self.exchange(number, False, True).wait_recv()
            self.hand(3 + number, False).start()

    def hands(self):
        for number in range(len(self.halves)):
            yield 1 + number
            yield 3 + number

    def finish(self):
        self.hand(0, True).wait_recv()
        for which in self.hands():
            self.hand(which, True).wait_recv()

    def drain(self):
        for offset in range(1, self.lines + 1):
            self.line(offset, False).wait_send()
        for number in range(len(self.halves)):
            self.exchange(number, True, False).wait_send()
            self.exchange(number, False, False).wait_send()
        self.hand(0, False).wait_send()
        for which in self.hands():
            self.hand(which, False).wait_send()


class Reduce:
    def __init__(self, place, part, out, rc, total, ra, rb, fa, fb, rz, send, recv):
        self.place, self.part, self.out = place, part, out
        self.rc, self.total, self.rz = rc, total, rz
        self.second, self.first = (ra, rb), (fa, fb)
        self.send, self.recv = send, recv
        self.halves = halves_of(part.shape[-1])
        self.lines = place.depth - 1

    @staticmethod
    def semaphores(depth):
        return depth + 4

    @staticmethod
    def scratch(depth, rows, cols, dtype):
        wide = halves_of(cols)[0][1]
        return [
            VMEM((2, depth, 2, rows, cols), dtype),
            VMEM((2, depth, 2, rows, cols), dtype),
            VMEM((depth, 2, rows, wide), dtype),
            VMEM((2, depth, rows, wide), dtype),
            VMEM((depth, rows, wide), dtype),
            VMEM((depth, rows, wide), dtype),
            VMEM((depth - 1, rows, cols), dtype),
            pltpu.SemaphoreType.DMA((Reduce.semaphores(depth),)),
            pltpu.SemaphoreType.DMA((Reduce.semaphores(depth),)),
        ]

    def core(self):
        place, every = self.place, slice(None)
        return remote(
            self.part.at[every, 1 - place.core],
            self.rc,
            self.send.at[0],
            self.recv.at[0],
            place.at(core=1 - place.core),
        )

    def cut(self, half, *index):
        start, width, _ = half
        return index + (slice(None), pl.ds(start, width))

    def exchange(self, number, second):
        place, every = self.place, slice(None)
        half = self.halves[number]
        slot = (1 if second else 3) + number
        over_x = (half[2] == "yx") == second
        device = place.at(x=1 - place.x) if over_x else place.at(y=1 - place.y)
        if second:
            index = (1 - place.x, every, every) if over_x else (every, every, 1 - place.y)
            landing = self.second[number]
        else:
            index = (1 - place.x, every, place.y) if over_x else (place.x, every, 1 - place.y)
            landing = self.first[number]
        return remote(
            self.total.at[self.cut(half, *index)],
            landing,
            self.send.at[slot],
            self.recv.at[slot],
            device,
        )

    def line(self, offset):
        place = self.place
        return remote(
            self.total.at[place.x, place.deeper(offset), place.y],
            self.rz.at[offset - 1],
            self.send.at[4 + offset],
            self.recv.at[4 + offset],
            place.at(z=place.deeper(offset)),
        )

    def start_core(self):
        self.core().start()

    def start_second(self):
        place = self.place
        self.core().wait_recv()
        dtype = self.total.dtype

        def add(z, carry):
            for x in range(2):
                for y in range(2):
                    self.total[x, z, y] = (
                        self.part[x, place.core, z, y].astype(F32) + self.rc[x, z, y].astype(F32)
                    ).astype(dtype)
            return carry

        lax.fori_loop(0, place.depth, add, 0)
        for number in range(len(self.halves)):
            self.exchange(number, True).start()

    def accumulate(self, index, value):
        self.total[index] = (self.total[index].astype(F32) + value.astype(F32)).astype(
            self.total.dtype
        )

    def start_first(self):
        place = self.place
        for number, half in enumerate(self.halves):
            self.exchange(number, True).wait_recv()
            landed = self.second[number]

            def add(z, carry):
                for other in range(2):
                    if half[2] == "yx":
                        self.accumulate(self.cut(half, place.x, z, other), landed[z, other])
                    else:
                        self.accumulate(self.cut(half, other, z, place.y), landed[other, z])
                return carry

            lax.fori_loop(0, place.depth, add, 0)
            self.exchange(number, False).start()

    def start_line(self):
        place = self.place
        for number, half in enumerate(self.halves):
            self.exchange(number, False).wait_recv()
            landed = self.first[number]

            def add(z, carry):
                self.accumulate(self.cut(half, place.x, z, place.y), landed[z])
                return carry

            lax.fori_loop(0, place.depth, add, 0)
        for offset in range(1, self.lines + 1):
            self.line(offset).start()

    def finish(self):
        place = self.place
        for offset in range(1, self.lines + 1):
            self.line(offset).wait_recv()
        result = self.total[place.x, place.z, place.y].astype(F32)
        for offset in range(1, self.lines + 1):
            result = result + self.rz[offset - 1].astype(F32)
        self.out[...] = result

    def drain(self):
        self.core().wait_send()
        for number in range(len(self.halves)):
            self.exchange(number, True).wait_send()
            self.exchange(number, False).wait_send()
        for offset in range(1, self.lines + 1):
            self.line(offset).wait_send()


def iota(shape, dim):
    return lax.broadcasted_iota(jnp.int32, shape, dim)


def dot(left, right):
    return lax.dot_general(left, right, (((1,), (0,)), ((), ())), preferred_element_type=F32)


def dot_nt(left, right):
    return lax.dot_general(left, right, (((1,), (1,)), ((), ())), preferred_element_type=F32)


def dot_tn(left, right):
    return lax.dot_general(left, right, (((0,), (0,)), ((), ())), preferred_element_type=F32)


def shift_of(size):
    assert size & (size - 1) == 0
    return size.bit_length() - 1


BIASES = ("query", "value", "output", "down", "up")
SCALARS = len(BIASES)


def spread_bias(gathered, name, per, total):
    rows = gathered.shape[0]
    pick = iota((LANES, total), 0) == (iota((LANES, total), 1) & (per - 1))
    spread = dot(gathered.astype(BF16), pick.astype(BF16))
    owner = jnp.right_shift(iota((rows, total), 1), shift_of(per)) * 8 + BIASES.index(name)
    return jnp.sum(jnp.where(iota((rows, total), 0) == owner, spread, 0.0), axis=0, keepdims=True)


def fold_bias(row, rows, name, per):
    total = row.shape[1]
    owner = jnp.right_shift(iota((rows, total), 1), shift_of(per)) * 8 + BIASES.index(name)
    chosen = jnp.where(iota((rows, total), 0) == owner, row, 0.0)
    put = iota((total, LANES), 1) == (iota((total, LANES), 0) & (per - 1))
    return lax.dot_general(
        chosen,
        put.astype(F32),
        (((1,), (0,)), ((), ())),
        precision=lax.Precision.HIGHEST,
        preferred_element_type=F32,
    )


def layer_kernel(
    blocks,
    parts,
    window,
    docs,
    x_ref,
    seg_ref,
    win_ref,
    wo_ref,
    wup_ref,
    wdown_ref,
    bias_refs,
    alphas_ref,
    grad_ref,
    out_ref,
    gx_ref,
    r_win,
    r_out,
    r_up,
    r_down,
    r_aux,
    gathered,
    gather_sems,
    local,
    trees,
    exchange_sems,
    halo_sems,
    segs,
    tile,
    aux_ref,
    qs,
    ks,
    qt_ref,
    kv_ref,
    kvt,
    starts_ref,
    ot_ref,
    of_ref,
    lse_ref,
    mixed_t,
    dos,
    doct_ref,
    act_s,
    gpre_s,
    gres_ref,
    acc,
    dqt_ref,
    dkv_sum,
    dq_in,
    dkv_in,
    halo_out,
    halo_in,
    gp,
    partials,
):
    place = Place(blocks)
    depth, devices = place.depth, 4 * blocks
    gwin, gwo, gwup, gwdown, gaux = gathered
    p_win, p_out, p_up, p_down, p_aux = partials
    width, hidden = gwin.shape[-1] // 3, gwup.shape[-1]
    per, per_up = width // devices, hidden // devices
    span, pairs_of_chunks, reach = window + GROUP, GROUP // 2, window // 2
    free = pairs_of_chunks - reach

    def loop(call, low=1, high=GROUP):
        def step(number, carry):
            call(number)
            return carry

        lax.fori_loop(low, high, step, 0)

    def exchange(src, dst, number):
        send, recv = exchange_sems[2 * number : 2 * number + 2]

        def copy(offset, come):
            landing = place.other_slot(-offset) if come else place.slot
            target = place.other_slot(offset)
            return remote(
                src(target), dst(landing), send.at[offset], recv.at[offset], place.member(target)
            )

        return copy

    def entry(ref, base=0):
        return lambda index: ref.at[base + index]

    seg_copy = exchange(lambda target: tile, entry(segs, window), 0)
    k_copy = exchange(entry(ks), entry(kv_ref, window), 1)
    q_copy = exchange(entry(qs), entry(qt_ref), 2)
    o_copy = exchange(entry(ot_ref), entry(mixed_t), 3)
    d_copy = exchange(entry(dos), entry(doct_ref), 4)
    dq_copy = exchange(entry(dqt_ref), entry(dq_in), 5)
    dkv_copy = exchange(entry(dkv_sum), entry(dkv_in), 6)
    seg_hs, seg_hr, kv_hs, kv_hr, back_hs, back_hr = halo_sems

    def send_to(copy, target):
        offset = lax.rem(target - place.slot + GROUP, GROUP)

        @pl.when(offset != 0)
        def _():
            copy(offset, False).start()

    def await_from(copy, source):
        offset = lax.rem(place.slot - source + GROUP, GROUP)

        @pl.when(offset != 0)
        def _():
            copy(offset, True).wait_recv()

    greet(place, parts, True)

    row = iota((16, LANES), 0)
    numbers = seg_ref[...].astype(F32)
    tile[...] = jnp.where(row == 0, numbers[0:1], numbers[1:2]).astype(BF16)
    segs[window + place.slot] = tile[...]
    aux_ref[...] = jnp.zeros_like(aux_ref)
    for index, ref in enumerate(bias_refs):
        aux_ref[index : index + 1, 0 : ref.shape[-1]] = ref[...].astype(F32).reshape(1, ref.shape[-1])
    if window:

        @pl.when(place.part == 0)
        def _():
            kv_ref[pl.ds(0, window)] = jnp.zeros((window, LANES, LANES), BF16)

    plan = (
        (aux_ref, gaux, None),
        (win_ref, gwin, (width, 2 * width)),
        (win_ref, gwin, (0, width)),
        (wo_ref, gwo, None),
        (wup_ref, gwup, None),
        (wdown_ref, gwdown, None),
    )
    gathers = [
        Gather(place, src, dst, gather_sems[2 * i], gather_sems[2 * i + 1], local.at[i], cols)
        for i, (src, dst, cols) in enumerate(plan)
    ]
    first, rest = gathers[:3], gathers[3:]
    g_aux, g_kv, g_q = first
    for gather in first:
        gather.start_line()
    loop(lambda offset: seg_copy(offset, False).start())
    for gather in first:
        gather.start_first()
    for gather in rest:
        gather.start_line()
    for gather in first:
        gather.start_second()

    loop(lambda offset: seg_copy(offset, True).wait_recv())

    def seg_halo(part):
        return remote(
            segs.at[pl.ds(GROUP, window)],
            segs.at[pl.ds(0, window)],
            seg_hs.at[0],
            seg_hr.at[0],
            place.member(place.slot, part),
        )

    if parts > 1:

        @pl.when(place.part < parts - 1)
        def _():
            seg_halo(place.part + 1).start()

    for gather in first:
        gather.start_last()
    g_aux.finish()
    g_kv.finish()

    aux = gaux[...].reshape(devices * 8, LANES)
    bias_q = spread_bias(aux, "query", per, width)
    bias_v = spread_bias(aux, "value", per, width)
    tokens = x_ref[...].reshape(2 * LANES, width)
    low_lane = iota((LANES, LANES), 1) < HD
    wide = 2 * LANES

    def column(kind, t):
        weight = gwin[:, :, :, :, :, pl.ds(kind * width + t * wide, wide)]
        return dot(tokens, weight.reshape(width, wide))

    def corners(t):
        for s in range(2):
            for u in range(2):
                at = (slice(s * LANES, (s + 1) * LANES), slice(u * LANES, (u + 1) * LANES))
                yield s * HEADS + t * 4 + u * 2, at

    for t in range(width // wide):
        k = column(1, t).astype(BF16).astype(F32)
        v = (column(2, t) + bias_v[:, t * wide : (t + 1) * wide]).astype(BF16).astype(F32)
        for head, at in corners(t):
            k_at, v_at = k[at], v[at]
            ks[head] = jnp.where(low_lane, k_at, pltpu.roll(v_at, HD, 1)).astype(BF16)
            ks[head + 1] = jnp.where(low_lane, pltpu.roll(k_at, HD, 1), v_at).astype(BF16)
    loop(lambda offset: k_copy(offset, False).start())
    kv_ref[window + place.slot] = ks[place.slot]
    g_q.finish()
    for t in range(width // wide):
        q = (column(0, t) + bias_q[:, t * wide : (t + 1) * wide]).astype(BF16).astype(F32) * 0.125
        for head, at in corners(t):
            turned = q[at].T.astype(BF16)
            qs[head] = turned[:HD]
            qs[head + 1] = turned[HD:]
    loop(lambda offset: q_copy(offset, False).start())
    qt_ref[place.slot] = qs[place.slot]

    for gather in rest:
        gather.start_first()

    if parts > 1:

        @pl.when(place.part < parts - 1)
        def _():
            seg_halo(place.part + 1).wait_send()

        @pl.when(place.part > 0)
        def _():
            seg_halo(place.part - 1).wait_recv()

    sequence = lax.div(place.slot, HEADS)
    chosen = jnp.where(iota((span, 16, LANES), 1) == sequence, segs[...].astype(F32), 0.0)
    seen = jnp.sum(chosen, axis=1)
    outside = (iota((span, LANES), 0) < window) & (place.part == 0)
    seen = jnp.where(outside, -1.0, seen)
    own = seen[window:]
    start = jnp.zeros((GROUP, LANES), F32)
    for number in range(docs):
        count = jnp.sum(jnp.where(seen == number - 1, 1.0, 0.0), axis=0, keepdims=True)
        count = jnp.sum(count, axis=1, keepdims=True)
        start = start + jnp.where(own >= number, count, 0.0)
    starts_ref[...] = start.astype(jnp.int32)

    for gather in rest:
        gather.start_second()

    def kv_halo(number, part):
        return remote(
            kv_ref.at[GROUP + number],
            kv_ref.at[number],
            kv_hs.at[number],
            kv_hr.at[number],
            place.member(place.slot, part),
        )

    def arrived(source):
        kvt[window + source] = kv_ref[window + source].T
        if parts > 1:

            @pl.when((place.part < parts - 1) & (source >= GROUP - window))
            def _():
                kv_halo(source - (GROUP - window), place.part + 1).start()

    arrived(place.slot)

    def kv_wait(offset):
        k_copy(offset, True).wait_recv()
        arrived(place.other_slot(-offset))

    loop(kv_wait)
    loop(lambda offset: q_copy(offset, True).wait_recv())

    many = window + 2
    older = window * LANES

    def q_rows_of(ref, m):
        return jnp.concatenate([ref[pl.ds(2 * m, 1)], ref[pl.ds(2 * m + 1, 1)]], axis=1)

    def turned_window(m):
        return jnp.concatenate([kvt[2 * m + i] for i in range(many)], axis=1)

    def masked(scores, start, q_place, block, base):
        k_place = base + block * BLOCK + iota((BLOCK, BLOCK), 0)
        visible = k_place >= start
        if block == reach:
            visible = visible & (k_place <= q_place)
        return jnp.where(visible, scores, NEG)

    blank = jnp.zeros((HD, BLOCK), BF16)

    def attend(step, carry):
        for number, gather in enumerate(rest):

            @pl.when(step == 1 + 2 * number)
            def _():
                gather.start_last()

        if parts > 1:

            @pl.when((step == free) & (place.part > 0))
            def _():
                loop(lambda number: kv_halo(number, place.part - 1).wait_recv(), 0, window)

        @pl.when(step == free)
        def _():
            def turn(number):
                kvt[number] = kv_ref[number].T

            loop(turn, 0, window)

        turnover = place.slot
        late = lax.rem(step - free + GROUP + turnover, reach)
        if free:
            m = jnp.where(step < free, reach + lax.rem(step + turnover, free), late)
        else:
            m = late
        q_wide = jnp.concatenate([two(qt_ref, 2 * m), blank], axis=0)
        start = q_rows_of(starts_ref, m)
        base = m * BLOCK
        q_place = base + older + iota((1, BLOCK), 1)
        scores = [
            masked(
                dot(kv_ref[pl.ds(2 * (m + block), 2)].reshape(BLOCK, LANES), q_wide),
                start,
                q_place,
                block,
                base,
            )
            for block in range(reach + 1)
        ]
        peak = functools.reduce(jnp.maximum, scores)
        peak = jnp.max(peak, axis=0, keepdims=True)
        weights = [jnp.exp(score - peak) for score in scores]
        total = functools.reduce(jnp.add, weights)
        total = jnp.sum(total, axis=0, keepdims=True)
        weights = jnp.concatenate([weight.astype(BF16) for weight in weights], axis=0)
        out = dot(turned_window(m)[HD:], weights) / total
        lse = peak + jnp.log(total)
        for side in range(2):
            lanes = slice(side * LANES, (side + 1) * LANES)
            of_ref[2 * m + side] = out[:, lanes]
            ot_ref[2 * m + side] = out[:, lanes].astype(BF16)
            lse_ref[pl.ds(2 * m + side, 1)] = lse[:, lanes]
            send_to(o_copy, 2 * m + side)
        return carry

    lax.fori_loop(0, pairs_of_chunks, attend, 0)
    mixed_t[place.slot] = ot_ref[place.slot]

    a0, a1 = alphas_ref[0], alphas_ref[1]
    bias_out = spread_bias(aux, "output", per, width)
    bias_down = spread_bias(aux, "down", per, width)
    bias_up = spread_bias(aux, "up", per_up, hidden)
    rows = 2 * LANES
    wide_tokens = tokens.astype(F32)
    grads = grad_ref[...].reshape(rows, width).astype(F32)
    grad_ffn = (a1 * grads).astype(BF16)
    for gather in rest:
        gather.finish()
    full_out = gwo[...].reshape(width, width)

    loop(lambda offset: o_copy(offset, True).wait_recv())
    mixed_turned = mixed_t[...].reshape(2, width, LANES)
    mixed = jnp.concatenate([mixed_turned[0].T, mixed_turned[1].T], axis=0)
    branch = dot(mixed, full_out) + bias_out
    attn_term = a0 * branch
    residual = wide_tokens + attn_term
    hidden_in = residual.astype(BF16)

    ffn = jnp.zeros((rows, width), F32) + bias_down
    grad_res = grads
    tile_up = 512
    whole_up = gwup.reshape(width, hidden)
    whole_down = gwdown.reshape(hidden, width)
    for t in range(hidden // tile_up):
        cols = pl.ds(t * tile_up, tile_up)
        w_up = whole_up[:, cols]
        w_down = whole_down[cols, :]
        pre = dot(hidden_in, w_up) + bias_up[:, t * tile_up : (t + 1) * tile_up]
        phi = 0.5 * (1.0 + lax.erf(pre * (1.0 / math.sqrt(2.0))))
        act = (pre * phi).astype(BF16)
        act_s[:, cols] = act
        ffn = ffn + dot(act, w_down)
        slope = phi + pre * jnp.exp(-0.5 * pre * pre) * (1.0 / math.sqrt(2.0 * math.pi))
        gpre = (dot_nt(grad_ffn, w_down) * slope).astype(BF16)
        gpre_s[:, cols] = gpre
        grad_res = grad_res + dot_nt(gpre, w_up)
    gres_ref[...] = grad_res
    grad_branch = (a0 * grad_res).astype(BF16)
    grad_mixed = dot_nt(grad_branch, full_out).astype(BF16).astype(F32)
    for s in range(2):
        turned = grad_mixed[s * LANES : (s + 1) * LANES].T.astype(BF16)
        dos[pl.ds(s * HEADS, HEADS)] = turned.reshape(HEADS, HD, LANES)
    loop(lambda offset: d_copy(offset, False).start())
    doct_ref[place.slot] = dos[place.slot]

    t_out, t_up, t_down, t_kv, t_q, t_aux = [
        Reduce(place, part, out, *scratch)
        for (part, out), scratch in zip(
            (
                (p_out, r_out),
                (p_up, r_up),
                (p_down, r_down),
                (p_win[1], r_win.at[:, pl.ds(width, 2 * width)]),
                (p_win[0], r_win.at[:, pl.ds(0, width)]),
                (p_aux, r_aux),
            ),
            trees,
        )
    ]
    lead = (2, 2, depth, 2)
    for t in range(hidden // tile_up):
        cols = pl.ds(t * tile_up, tile_up)
        block = dot_tn(act_s[:, cols], grad_ffn).astype(BF16)
        p_down.reshape(hidden, width)[cols, :] = block
    t_down.start_core()
    for t in range(hidden // tile_up):
        cols = pl.ds(t * tile_up, tile_up)
        block = dot_tn(hidden_in, gpre_s[:, cols]).astype(BF16)
        p_up.reshape(width, hidden)[:, cols] = block
    t_up.start_core()
    p_out.reshape(width, width)[...] = dot(
        jnp.concatenate([mixed_turned[0], mixed_turned[1]], axis=1), grad_branch
    ).astype(BF16)
    t_out.start_core()

    ffn_term = a1 * ffn
    stream = residual + ffn_term
    out_ref[...] = stream.astype(BF16).reshape(2, LANES, width)

    def whole(values):
        return jnp.sum(jnp.sum(values, axis=0, keepdims=True), axis=1, keepdims=True)

    sums = (
        whole(stream * stream),
        whole(attn_term * attn_term),
        whole(ffn_term * ffn_term),
        whole(grad_res * branch),
        whole(grads * ffn),
    )
    lane = iota((devices * 8, LANES), 1)
    scalars = jnp.zeros((devices * 8, LANES), F32)
    for number, value in enumerate(sums):
        scalars = scalars + jnp.where(lane == number, value, 0.0)
    up_row = jnp.sum(gpre_s[...].astype(F32), axis=0, keepdims=True)
    down_row = jnp.sum(grad_ffn.astype(F32), axis=0, keepdims=True)
    out_row = jnp.sum(grad_branch.astype(F32), axis=0, keepdims=True)
    folded = (
        fold_bias(out_row, devices * 8, "output", per)
        + fold_bias(down_row, devices * 8, "down", per)
        + fold_bias(up_row, devices * 8, "up", per_up)
        + jnp.where((iota((devices * 8, LANES), 0) & 7) == SCALARS, scalars, 0.0)
    )
    p_aux[...] = folded.reshape(*lead, 8, LANES)

    early = (t_down, t_up, t_out)
    low_block = iota((BLOCK, LANES), 1) < HD

    def clear(number):
        acc[number] = jnp.zeros((LANES, LANES), F32)

    loop(clear, 0, span)

    def back_halo(part):
        return remote(
            halo_out, halo_in, back_hs.at[0], back_hr.at[0], place.member(place.slot, part)
        )

    def settle(number):
        dkv_sum[number] = acc[window + number].astype(BF16)

    def attend_back(m, carry):
        for number, tree in enumerate(early):

            @pl.when(m == 1 + number)
            def _():
                tree.start_second()

            @pl.when(m == pairs_of_chunks - 3 + number)
            def _():
                tree.start_first()

        await_from(d_copy, 2 * m)
        await_from(d_copy, 2 * m + 1)
        qt, dt = two(qt_ref, 2 * m), two(doct_ref, 2 * m)
        q_wide = jnp.concatenate([qt, blank], axis=0)
        d_wide = jnp.concatenate([blank, dt], axis=0)
        both = jnp.concatenate([qt, dt], axis=0).astype(F32).T
        q_and_d = jnp.concatenate(
            [jnp.where(low_block, both, 0.0), jnp.where(low_block, 0.0, both)], axis=0
        ).astype(BF16)
        start = q_rows_of(starts_ref, m)
        lse = q_rows_of(lse_ref, m)
        delta = jnp.sum(dt.astype(F32) * two(of_ref, 2 * m), axis=0, keepdims=True)
        base = m * BLOCK
        q_place = base + older + iota((1, BLOCK), 1)
        grad_scores = []
        for block in range(reach + 1):
            here = pl.ds(2 * (m + block), 2)
            kv = kv_ref[here].reshape(BLOCK, LANES)
            scores = masked(dot(kv, q_wide), start, q_place, block, base)
            probs = jnp.exp(scores - lse)
            grad_score = (probs * (dot(kv, d_wide) - delta)).astype(BF16)
            grad_scores.append(grad_score)
            both_scores = jnp.concatenate([grad_score, probs.astype(BF16)], axis=1)
            acc[here] += dot(both_scores, q_and_d).reshape(2, LANES, LANES)
        dq = dot(turned_window(m)[:HD], jnp.concatenate(grad_scores, axis=0)) * 0.125
        for side in range(2):
            dqt_ref[2 * m + side] = dq[:, side * LANES : (side + 1) * LANES].astype(BF16)
            send_to(dq_copy, 2 * m + side)
        if parts > 1:

            @pl.when((m == reach - 1) & (place.part > 0))
            def _():
                def put(number):
                    halo_out[number] = acc[number].astype(BF16)

                loop(put, 0, window)
                back_halo(place.part - 1).start()

        if free:

            @pl.when(m >= reach)
            def _():
                for side in range(2):
                    chunk = 2 * (m - reach) + side
                    settle(chunk)
                    send_to(dkv_copy, chunk)

        return carry

    lax.fori_loop(0, pairs_of_chunks, attend_back, 0)
    dq_in[place.slot] = dqt_ref[place.slot]
    loop(settle, GROUP - window, GROUP)
    if parts > 1:

        @pl.when(place.part < parts - 1)
        def _():
            back_halo(place.part + 1).wait_recv()

            def add(number):
                chunk = GROUP - window + number
                total = acc[window + chunk] + halo_in[number].astype(F32)
                dkv_sum[chunk] = total.astype(BF16)

            loop(add, 0, window)

    def late(offset):
        @pl.when(place.other_slot(offset) >= GROUP - window)
        def _():
            dkv_copy(offset, False).start()

    loop(late)
    dkv_in[place.slot] = dkv_sum[place.slot]

    tokens_turned = tokens.T
    loop(lambda offset: dq_copy(offset, True).wait_recv())
    for s in range(2):
        turned = dq_in[pl.ds(s * HEADS, HEADS)].reshape(width, LANES).astype(F32)
        gp[s * LANES : (s + 1) * LANES, 0:width] = turned.T.astype(BF16)
    query_row = jnp.sum(gp[:, 0:width].astype(F32), axis=0, keepdims=True)
    p_win[0][...] = (
        dot(tokens_turned, gp[:, 0:width])
        .astype(BF16)
        .reshape(*lead, width // devices, width)
    )
    t_q.start_core()
    full_in = gwin.reshape(width, 3 * width)
    gx = gres_ref[...] + dot_nt(gp[:, 0:width], full_in[:, 0:width])
    for tree in early:
        tree.start_line()
    t_q.start_second()

    loop(lambda offset: dkv_copy(offset, True).wait_recv())
    for s in range(2):
        at_rows = slice(s * LANES, (s + 1) * LANES)
        for pair in range(HEADS // 2):
            even = dkv_in[s * HEADS + 2 * pair].astype(F32)
            odd = dkv_in[s * HEADS + 2 * pair + 1].astype(F32)
            keys = jnp.where(low_lane, even, pltpu.roll(odd, HD, 1))
            values = jnp.where(low_lane, pltpu.roll(even, HD, 1), odd)
            at = width + pair * LANES
            gp[at_rows, at : at + LANES] = keys.astype(BF16)
            gp[at_rows, width + at : width + at + LANES] = values.astype(BF16)
    for t in range(2):
        part = dot(tokens_turned, gp[:, (1 + t) * width : (2 + t) * width]).astype(BF16)
        p_win[1][:, :, :, :, :, t * width : (t + 1) * width] = part.reshape(
            *lead, width // devices, width
        )
    t_kv.start_core()
    value_row = jnp.sum(gp[:, 2 * width :].astype(F32), axis=0, keepdims=True)
    folded = fold_bias(query_row, devices * 8, "query", per) + fold_bias(
        value_row, devices * 8, "value", per
    )
    p_aux[...] += folded.reshape(*lead, 8, LANES)
    t_aux.start_core()
    t_q.start_first()
    t_kv.start_second()
    t_aux.start_second()
    for t in range(1, 3):
        cols = slice(t * width, (t + 1) * width)
        gx = gx + dot_nt(gp[:, cols], full_in[:, cols])
    gx_ref[...] = gx.astype(BF16).reshape(2, LANES, width)
    for tree in early:
        tree.finish()
    t_q.start_line()
    t_aux.start_first()
    t_kv.start_first()
    t_aux.start_line()
    t_kv.start_line()
    t_q.finish()
    t_aux.finish()
    t_kv.finish()

    def sent(offset):
        for copy in (seg_copy, q_copy, k_copy, o_copy, d_copy, dq_copy, dkv_copy):
            copy(offset, False).wait_send()

    loop(sent)
    if parts > 1:

        @pl.when(place.part < parts - 1)
        def _():
            loop(lambda number: kv_halo(number, place.part + 1).wait_send(), 0, window)

        @pl.when(place.part > 0)
        def _():
            back_halo(place.part - 1).wait_send()

    for gather in gathers:
        gather.drain()
    for tree in early + (t_q, t_kv, t_aux):
        tree.drain()


def two(ref, index):
    return jnp.concatenate([ref[index], ref[index + 1]], axis=1)


def hand_out_kernel(
    tokens_all, out_ref, gx_ref, win_ref, wo_ref, wup_ref, wdown_ref, sums_ref, *results
):
    for src, dst in zip((out_ref, gx_ref, win_ref, wo_ref, wup_ref, wdown_ref), results[:6]):
        dst[...] = src[...]
    named = dict(zip(("query", "value", "output", "up", "down"), results[6:11]))
    for name, ref in named.items():
        ref[...] = sums_ref[BIASES.index(name), 0 : ref.shape[0]]
    results[11][...] = sums_ref[SCALARS, 3:5]
    results[12][...] = jnp.sqrt(sums_ref[SCALARS, 0:3] * (1.0 / tokens_all))


def call(kernel, out_shape, in_specs, out_specs, scratch, collective=None):
    return pl.pallas_call(
        kernel,
        out_shape=out_shape,
        in_specs=in_specs,
        out_specs=out_specs,
        scratch_shapes=scratch,
        compiler_params=pltpu.CompilerParams(
            collective_id=collective,
            has_side_effects=collective is not None,
            vmem_limit_bytes=VMEM_BYTES,
        ),
    )


def local(
    layer_input,
    segments,
    input_weight,
    output_weight,
    up_weight,
    down_weight,
    query_bias,
    value_bias,
    output_bias,
    up_bias,
    down_bias,
    alphas,
    out_grad,
):
    heads, blocks = lax.axis_size("head"), lax.axis_size("blk")
    depth, devices = blocks // 2, heads * blocks
    seqs, rows, width = layer_input.shape
    hidden = up_weight.shape[1]
    seq_len = rows * devices
    assert heads == 4 and seqs * HEADS == GROUP and rows == LANES
    longest = 16 * math.isqrt(seq_len)
    window, parts = longest // rows, devices // GROUP
    docs = 2 * seq_len // longest
    assert window <= GROUP and window % 2 == 0
    span = window + GROUP

    def shape(*dims, dtype=BF16):
        return jax.ShapeDtypeStruct(dims, dtype)

    vmem, smem = pl.BlockSpec(memory_space=VMEM), pl.BlockSpec(memory_space=pltpu.SMEM)
    dma = pltpu.SemaphoreType.DMA
    lead = (2, 2, depth, 2)
    in_rows, up_rows = input_weight.shape[0], down_weight.shape[0]
    gather_sems = Gather.semaphores(depth)
    reduced = (
        (in_rows, width, BF16),
        (in_rows, hidden, BF16),
        (up_rows, width, BF16),
        (in_rows, 2 * width, BF16),
        (in_rows, width, BF16),
        (8, LANES, F32),
    )
    tokens = seqs * rows
    results = (
        shape(seqs, rows, width),
        shape(seqs, rows, width),
        shape(in_rows, 3 * width, dtype=F32),
        shape(in_rows, width, dtype=F32),
        shape(in_rows, hidden, dtype=F32),
        shape(up_rows, width, dtype=F32),
    )
    carried = call(
        functools.partial(layer_kernel, blocks, parts, window, docs),
        results + (shape(8, LANES, dtype=F32),),
        [vmem] * 6 + [(vmem,) * 5] + [smem, vmem],
        (vmem,) * 7,
        [
            [
                VMEM((*lead, in_rows, 3 * width), BF16),
                VMEM((*lead, in_rows, width), BF16),
                VMEM((*lead, in_rows, hidden), BF16),
                VMEM((*lead, up_rows, width), BF16),
                VMEM((*lead, 8, LANES), F32),
            ],
            [dma((gather_sems,))] * 12,
            dma((6,)),
            [Reduce.scratch(depth, *sizes) for sizes in reduced],
            [dma((GROUP,))] * 14,
            [dma((1,)), dma((1,)), dma((window,)), dma((window,)), dma((1,)), dma((1,))],
            VMEM((span, 16, LANES), BF16),
            VMEM((16, LANES), BF16),
            VMEM((8, LANES), F32),
            VMEM((GROUP, HD, LANES), BF16),
            VMEM((GROUP, LANES, LANES), BF16),
            VMEM((GROUP, HD, LANES), BF16),
            VMEM((span, LANES, LANES), BF16),
            VMEM((span, LANES, LANES), BF16),
            VMEM((GROUP, LANES), jnp.int32),
            VMEM((GROUP, HD, LANES), BF16),
            VMEM((GROUP, HD, LANES), F32),
            VMEM((GROUP, LANES), F32),
            VMEM((GROUP, HD, LANES), BF16),
            VMEM((GROUP, HD, LANES), BF16),
            VMEM((GROUP, HD, LANES), BF16),
            VMEM((tokens, hidden), BF16),
            VMEM((tokens, hidden), BF16),
            VMEM((tokens, width), F32),
            VMEM((span, LANES, LANES), F32),
            VMEM((GROUP, HD, LANES), BF16),
            VMEM((GROUP, LANES, LANES), BF16),
            VMEM((GROUP, HD, LANES), BF16),
            VMEM((GROUP, LANES, LANES), BF16),
            VMEM((window, LANES, LANES), BF16),
            VMEM((window, LANES, LANES), BF16),
            VMEM((tokens, 3 * width), BF16),
            [
                [
                    VMEM((*lead, in_rows, width), BF16),
                    VMEM((*lead, in_rows, 2 * width), BF16),
                ],
                VMEM((*lead, in_rows, width), BF16),
                VMEM((*lead, in_rows, hidden), BF16),
                VMEM((*lead, up_rows, width), BF16),
                VMEM((*lead, 8, LANES), F32),
            ],
        ],
        collective=0,
    )(
        layer_input,
        segments,
        input_weight,
        output_weight,
        up_weight,
        down_weight,
        (query_bias, value_bias, output_bias, down_bias, up_bias),
        alphas,
        out_grad,
    )
    per, per_up = width // devices, hidden // devices
    return call(
        functools.partial(hand_out_kernel, seqs * seq_len * width),
        results
        + tuple(
            shape(size, dtype=F32) for size in (per, per, per, per_up, per, 2, 3)
        ),
        [vmem] * 7,
        (vmem,) * 13,
        [],
    )(*carried)


def solution(mesh):
    tokens = P(None, ("head", "blk"), None)
    rows, flat = P(("head", "blk"), None), P(("head", "blk"))
    return jax.shard_map(
        local,
        mesh=mesh,
        in_specs=(
            tokens,
            P(None, ("head", "blk")),
            rows,
            rows,
            rows,
            rows,
            flat,
            flat,
            flat,
            flat,
            flat,
            P(),
            tokens,
        ),
        out_specs=(
            tokens,
            tokens,
            rows,
            rows,
            rows,
            rows,
            flat,
            flat,
            flat,
            flat,
            flat,
            P(),
            P(),
        ),
        check_vma=False,
    )
```

```python
import functools
import math

import jax
import jax.numpy as jnp
from jax import lax
from jax.experimental import pallas as pl
from jax.experimental.pallas import tpu as pltpu
from jax.sharding import PartitionSpec as P

HEADS = 8
HD = 64
LANES = 128
GROUP = 16
BLOCK = 256
VMEM_BYTES = 60 * 1024 * 1024
F32 = jnp.float32
BF16 = jnp.bfloat16
VMEM = pltpu.VMEM
NEG = -1e30
MOST = 2


class Place:
    def __init__(self, blocks):
        self.blocks = blocks
        self.depth = blocks // 2
        head = lax.axis_index("head")
        block = lax.axis_index("blk")
        self.x, self.core = lax.div(head, 2), lax.rem(head, 2)
        self.z, self.y = lax.div(block, 2), lax.rem(block, 2)
        flat = head * blocks + block
        self.part, self.slot = lax.div(flat, GROUP), lax.rem(flat, GROUP)

    def at(self, x=None, core=None, z=None, y=None):
        x = self.x if x is None else x
        core = self.core if core is None else core
        z = self.z if z is None else z
        y = self.y if y is None else y
        return (x * 2 + core, z * 2 + y)

    def deeper(self, offset):
        return lax.rem(self.z + offset + self.depth, self.depth)

    def member(self, slot, part=None):
        part = self.part if part is None else part
        flat = part * GROUP + slot
        return (lax.div(flat, self.blocks), lax.rem(flat, self.blocks))

    def other_slot(self, offset):
        return lax.rem(self.slot + offset + GROUP, GROUP)


def remote(src, dst, send, recv, device):
    return pltpu.make_async_remote_copy(
        src_ref=src,
        dst_ref=dst,
        send_sem=send,
        recv_sem=recv,
        device_id=device,
        device_id_type=pl.DeviceIdType.MESH,
    )


def greet(place, parts, tree):
    barrier = pltpu.get_barrier_semaphore()

    def hello(device):
        pl.semaphore_signal(barrier, inc=1, device_id=device, device_id_type=pl.DeviceIdType.MESH)

    def group(offset, carry):
        hello(place.member(place.other_slot(offset)))
        return carry

    lax.fori_loop(1, GROUP, group, 0)
    total = GROUP - 1
    if tree:

        def line(offset, carry):
            hello(place.at(z=place.deeper(offset)))
            return carry

        lax.fori_loop(1, place.depth, line, 0)
        hello(place.at(x=1 - place.x))
        hello(place.at(y=1 - place.y))
        hello(place.at(x=1 - place.x, y=1 - place.y))
        hello(place.at(core=1 - place.core))
        total += place.depth + 3
    if parts > 1 and tree:

        @pl.when(place.part > 0)
        def _():
            hello(place.member(place.slot, place.part - 1))

        @pl.when(place.part < parts - 1)
        def _():
            hello(place.member(place.slot, place.part + 1))

        total += jnp.where(place.part > 0, 1, 0) + jnp.where(place.part < parts - 1, 1, 0)
    pl.semaphore_wait(barrier, total)


def halves_of(columns):
    if columns < 2 * LANES:
        return ((0, columns, "yx"),)
    most = max(columns // 2, columns * MOST // 4)
    return ((0, most, "yx"), (most, columns - most, "xy"))


def wait_received(place, dst, sem):
    remote(dst, dst, sem, sem, place.at(core=1 - place.core)).wait_recv()


def wait_sent(place, src, sem):
    remote(src, src, sem, sem, place.at(core=1 - place.core)).wait_send()


class Gather:
    COUNT = 9

    def __init__(self, place, src, dst, sems, cols=None):
        self.place, self.src, self.dst, self.sems = place, src, dst, sems
        start, width = cols or (0, dst.shape[-1])
        self.cols = pl.ds(start, width)

    def part(self, *index):
        return self.dst.at[index + (slice(None), self.cols)]

    def column(self, core, x, y):
        return self.part(x, core, slice(None), y)

    def others(self):
        place = self.place
        return ((1 - place.x, place.y), (place.x, 1 - place.y), (1 - place.x, 1 - place.y))

    def own(self):
        place = self.place
        mine = self.part(place.x, place.core, place.z, place.y)
        return pltpu.make_async_copy(self.src.at[:, self.cols], mine, self.sems.at[0])

    def start_line(self):
        place = self.place
        for offset in range(1, place.depth):
            remote(
                self.src.at[:, self.cols],
                self.part(place.x, place.core, place.z, place.y),
                self.sems.at[1],
                self.sems.at[2],
                place.at(z=place.deeper(offset)),
            ).start()
        self.own().start()

    def lines(self):
        return self.part(0, 0, pl.ds(0, self.place.depth - 1), 0)

    def hand(self, x, y):
        place = self.place
        column = self.column(place.core, x, y)
        remote(
            column, column, self.sems.at[7], self.sems.at[8], place.at(core=1 - place.core)
        ).start()

    def start_columns(self):
        place = self.place
        self.own().wait()
        wait_received(place, self.lines(), self.sems.at[2])
        mine = self.column(place.core, place.x, place.y)
        for number, (x, y) in enumerate(self.others()):
            remote(
                mine, mine, self.sems.at[3], self.sems.at[4 + number], place.at(x=x, y=y)
            ).start()
        self.hand(place.x, place.y)

    def start_hands(self):
        for number, (x, y) in enumerate(self.others()):
            wait_received(
                self.place, self.column(self.place.core, x, y), self.sems.at[4 + number]
            )
            self.hand(x, y)

    def finish(self):
        every = slice(None)
        region = self.part(every, 1 - self.place.core, every, every)
        wait_received(self.place, region, self.sems.at[8])

    def drain(self):
        place = self.place
        wait_sent(place, self.lines(), self.sems.at[1])
        every = slice(None)
        wait_sent(
            place, self.part(every, every, pl.ds(0, 3 * place.depth // 4), 0), self.sems.at[3]
        )
        wait_sent(place, self.part(every, 0, every, every), self.sems.at[7])


def halves_of(columns):
    if columns < 2 * LANES:
        return ((0, columns, "yx"),)
    most = max(columns // 2, columns * MOST // 4)
    return ((0, most, "yx"), (most, columns - most, "xy"))


class TreeGather:
    COUNT = 13

    def __init__(self, place, src, dst, sems):
        self.place, self.src, self.dst, self.sems = place, src, dst, sems
        self.halves = halves_of(dst.shape[-1])

    def cut(self, half, *index):
        start, width, _ = half
        return self.dst.at[index + (slice(None), pl.ds(start, width))]

    def across(self, half, first):
        place = self.place
        if (half[2] == "yx") == first:
            return place.x, 1 - place.y
        return 1 - place.x, place.y

    def region(self, half, first, core, x, y):
        every = slice(None)
        if first:
            return self.cut(half, x, core, every, y)
        if half[2] == "yx":
            return self.cut(half, x, core, every, every)
        return self.cut(half, every, core, every, y)

    def own(self):
        place = self.place
        mine = self.dst.at[place.x, place.core, place.z, place.y]
        return pltpu.make_async_copy(self.src, mine, self.sems.at[0])

    def start_line(self):
        place = self.place
        for offset in range(1, place.depth):
            remote(
                self.src,
                self.dst.at[place.x, place.core, place.z, place.y],
                self.sems.at[1],
                self.sems.at[2],
                place.at(z=place.deeper(offset)),
            ).start()
        self.own().start()

    def lines(self):
        return self.dst.at[0, 0, pl.ds(0, self.place.depth - 1), 0]

    def exchange(self, number, first):
        place, half = self.place, self.halves[number]
        x, y = self.across(half, first)
        mine = self.region(half, first, place.core, place.x, place.y)
        base = 0 if first else 2
        return remote(
            mine,
            mine,
            self.sems.at[3 + base + number],
            self.sems.at[9 + base + number],
            place.at(x=x, y=y),
        )

    def received(self, number, first):
        half = self.halves[number]
        x, y = self.across(half, first)
        region = self.region(half, first, self.place.core, x, y)
        wait_received(self.place, region, self.sems.at[(9 if first else 11) + number])
        return region

    def hand(self, region):
        place = self.place
        remote(
            region, region, self.sems.at[7], self.sems.at[8], place.at(core=1 - place.core)
        ).start()

    def start_first(self):
        place = self.place
        self.own().wait()
        wait_received(place, self.lines(), self.sems.at[2])
        for number in range(len(self.halves)):
            self.exchange(number, True).start()
        self.hand(self.dst.at[place.x, place.core, slice(None), place.y])

    def start_second(self):
        for number in range(len(self.halves)):
            region = self.received(number, True)
            self.exchange(number, False).start()
            self.hand(region)

    def start_hands(self):
        for number in range(len(self.halves)):
            self.hand(self.received(number, False))

    def finish(self):
        wait_received(self.place, self.dst.at[:, 1 - self.place.core], self.sems.at[8])

    def drain(self):
        for number in range(len(self.halves)):
            self.exchange(number, True).wait_send()
            self.exchange(number, False).wait_send()
        wait_sent(self.place, self.lines(), self.sems.at[1])
        wait_sent(self.place, self.dst.at[:, 0], self.sems.at[7])


class Reduce:
    COUNT = 8

    def __init__(self, place, part, out, rc, total, rn, rz, sems):
        self.place, self.part, self.out = place, part, out
        self.rc, self.total, self.rn, self.rz, self.sems = rc, total, rn, rz, sems

    @staticmethod
    def scratch(depth, rows, cols, dtype):
        return [
            VMEM((2, depth, 2, rows, cols), dtype),
            VMEM((2, depth, 2, rows, cols), dtype),
            VMEM((3, depth, rows, cols), dtype),
            VMEM((depth - 1, rows, cols), dtype),
            pltpu.SemaphoreType.DMA((Reduce.COUNT,)),
        ]

    def others(self):
        place = self.place
        return ((1 - place.x, place.y), (place.x, 1 - place.y), (1 - place.x, 1 - place.y))

    def core(self):
        place = self.place
        return remote(
            self.part.at[:, 1 - place.core],
            self.rc,
            self.sems.at[0],
            self.sems.at[1],
            place.at(core=1 - place.core),
        )

    def columns(self):
        place = self.place
        for number, (x, y) in enumerate(self.others()):
            yield remote(
                self.total.at[x, :, y],
                self.rn.at[number],
                self.sems.at[2],
                self.sems.at[3 + number],
                place.at(x=x, y=y),
            )

    def line(self, offset):
        place = self.place
        return remote(
            self.total.at[place.x, place.deeper(offset), place.y],
            self.rz.at[offset - 1],
            self.sems.at[6],
            self.sems.at[7],
            place.at(z=place.deeper(offset)),
        )

    def start_core(self):
        self.core().start()

    def add_core(self, x, z, y):
        place = self.place
        self.total[x, z, y] = (
            self.part[x, place.core, z, y].astype(F32) + self.rc[x, z, y].astype(F32)
        ).astype(self.total.dtype)

    def start_columns(self):
        place = self.place
        self.core().wait_recv()
        for copy, (x, y) in zip(self.columns(), self.others()):

            def add(z, carry):
                self.add_core(x, z, y)
                return carry

            lax.fori_loop(0, place.depth, add, 0)
            copy.start()

        def add(z, carry):
            self.add_core(place.x, z, place.y)
            return carry

        lax.fori_loop(0, place.depth, add, 0)

    def start_line(self):
        place = self.place
        for copy in self.columns():
            copy.wait_recv()
        here = (place.x, slice(None), place.y)
        total = self.total[here].astype(F32)
        for number in range(3):
            total = total + self.rn[number].astype(F32)
        self.total[here] = total.astype(self.total.dtype)
        for offset in range(1, place.depth):
            self.line(offset).start()

    def finish(self):
        place = self.place
        wait_received(place, self.rz, self.sems.at[7])
        result = self.total[place.x, place.z, place.y].astype(F32)
        for offset in range(1, place.depth):
            result = result + self.rz[offset - 1].astype(F32)
        self.out[...] = result

    def drain(self):
        place = self.place
        self.core().wait_send()
        wait_sent(place, self.rn, self.sems.at[2])
        wait_sent(place, self.rz, self.sems.at[6])


class TreeReduce:
    COUNT = 12

    def __init__(self, place, part, out, rc, total, ra, rb, fa, fb, rz, sems):
        self.place, self.part, self.out = place, part, out
        self.rc, self.total, self.rz = rc, total, rz
        self.second, self.first = (ra, rb), (fa, fb)
        self.sems = sems
        self.halves = halves_of(part.shape[-1])

    @staticmethod
    def scratch(depth, rows, cols, dtype):
        wide, narrow = [half[1] for half in halves_of(cols)]
        return [
            VMEM((2, depth, 2, rows, cols), dtype),
            VMEM((2, depth, 2, rows, cols), dtype),
            VMEM((depth, 2, rows, wide), dtype),
            VMEM((2, depth, rows, narrow), dtype),
            VMEM((depth, rows, wide), dtype),
            VMEM((depth, rows, narrow), dtype),
            VMEM((depth - 1, rows, cols), dtype),
            pltpu.SemaphoreType.DMA((TreeReduce.COUNT,)),
        ]

    core, line, start_core, add_core = Reduce.core, Reduce.line, Reduce.start_core, Reduce.add_core
    finish = Reduce.finish

    def cut(self, half, *index):
        start, width, _ = half
        return index + (slice(None), pl.ds(start, width))

    def exchange(self, number, second):
        place, every = self.place, slice(None)
        half = self.halves[number]
        slot = (2 if second else 8) + number
        over_x = (half[2] == "yx") == second
        device = place.at(x=1 - place.x) if over_x else place.at(y=1 - place.y)
        if second:
            index = (1 - place.x, every, every) if over_x else (every, every, 1 - place.y)
            landing = self.second[number]
        else:
            index = (1 - place.x, every, place.y) if over_x else (place.x, every, 1 - place.y)
            landing = self.first[number]
        return remote(
            self.total.at[self.cut(half, *index)],
            landing,
            self.sems.at[slot],
            self.sems.at[slot + 2],
            device,
        )

    def start_second(self):
        self.core().wait_recv()

        def add(z, carry):
            for x in range(2):
                for y in range(2):
                    self.add_core(x, z, y)
            return carry

        lax.fori_loop(0, self.place.depth, add, 0)
        for number in range(len(self.halves)):
            self.exchange(number, True).start()

    def accumulate(self, index, value):
        self.total[index] = (self.total[index].astype(F32) + value.astype(F32)).astype(
            self.total.dtype
        )

    def start_first(self):
        place = self.place
        for number, half in enumerate(self.halves):
            self.exchange(number, True).wait_recv()
            landed = self.second[number]

            def add(z, carry):
                for other in range(2):
                    if half[2] == "yx":
                        self.accumulate(self.cut(half, place.x, z, other), landed[z, other])
                    else:
                        self.accumulate(self.cut(half, other, z, place.y), landed[other, z])
                return carry

            lax.fori_loop(0, place.depth, add, 0)
            self.exchange(number, False).start()

    def start_line(self):
        place = self.place
        for number, half in enumerate(self.halves):
            self.exchange(number, False).wait_recv()
            landed = self.first[number]

            def add(z, carry):
                self.accumulate(self.cut(half, place.x, z, place.y), landed[z])
                return carry

            lax.fori_loop(0, place.depth, add, 0)
        for offset in range(1, place.depth):
            self.line(offset).start()

    def drain(self):
        self.core().wait_send()
        for number in range(len(self.halves)):
            self.exchange(number, True).wait_send()
            self.exchange(number, False).wait_send()
        wait_sent(self.place, self.rz, self.sems.at[6])


def iota(shape, dim):
    return lax.broadcasted_iota(jnp.int32, shape, dim)


def dot(left, right):
    return lax.dot_general(left, right, (((1,), (0,)), ((), ())), preferred_element_type=F32)


def dot_nt(left, right):
    return lax.dot_general(left, right, (((1,), (1,)), ((), ())), preferred_element_type=F32)


def dot_tn(left, right):
    return lax.dot_general(left, right, (((0,), (0,)), ((), ())), preferred_element_type=F32)


def shift_of(size):
    assert size & (size - 1) == 0
    return size.bit_length() - 1


BIASES = ("query", "value", "output", "down", "up")
SCALARS = len(BIASES)


def spread_bias(gathered, name, per, total):
    rows = gathered.shape[0]
    pick = iota((LANES, total), 0) == (iota((LANES, total), 1) & (per - 1))
    spread = dot(gathered.astype(BF16), pick.astype(BF16))
    owner = jnp.right_shift(iota((rows, total), 1), shift_of(per)) * 8 + BIASES.index(name)
    return jnp.sum(jnp.where(iota((rows, total), 0) == owner, spread, 0.0), axis=0, keepdims=True)


def fold_bias(row, rows, name, per):
    total = row.shape[1]
    owner = jnp.right_shift(iota((rows, total), 1), shift_of(per)) * 8 + BIASES.index(name)
    chosen = jnp.where(iota((rows, total), 0) == owner, row, 0.0)
    put = iota((total, LANES), 1) == (iota((total, LANES), 0) & (per - 1))
    return lax.dot_general(
        chosen,
        put.astype(F32),
        (((1,), (0,)), ((), ())),
        precision=lax.Precision.HIGHEST,
        preferred_element_type=F32,
    )


def layer_kernel(
    blocks,
    parts,
    window,
    docs,
    x_ref,
    seg_ref,
    win_ref,
    wo_ref,
    wup_ref,
    wdown_ref,
    bias_refs,
    alphas_ref,
    grad_ref,
    out_ref,
    gx_ref,
    r_win,
    r_out,
    r_up,
    r_down,
    r_aux,
    gathered,
    gather_sems,
    trees,
    exchange_sems,
    halo_sems,
    segs,
    tile,
    aux_ref,
    qs,
    ks,
    qt_ref,
    kv_ref,
    kvt,
    starts_ref,
    ot_ref,
    of_ref,
    lse_ref,
    mixed_t,
    dos,
    doct_ref,
    act_s,
    gpre_s,
    gres_ref,
    acc,
    dqt_ref,
    dkv_sum,
    dq_in,
    dkv_in,
    halo_out,
    halo_in,
    gp,
    partials,
):
    place = Place(blocks)
    depth, devices = place.depth, 4 * blocks
    gwin, gwo, gwup, gwdown, gaux = gathered
    p_win, p_out, p_up, p_down, p_aux = partials
    width, hidden = gwin.shape[-1] // 3, gwup.shape[-1]
    per, per_up = width // devices, hidden // devices
    span, pairs_of_chunks, reach = window + GROUP, GROUP // 2, window // 2
    free = pairs_of_chunks - reach

    def loop(call, low=1, high=GROUP):
        def step(number, carry):
            call(number)
            return carry

        lax.fori_loop(low, high, step, 0)

    def exchange(src, dst, sems, each=False):
        def copy(offset, come=False):
            landing = place.other_slot(-offset) if come else place.slot
            target = place.other_slot(offset)
            return remote(
                src(target),
                dst(landing),
                sems.at[0],
                sems.at[offset if each else 1],
                place.member(target),
            )

        return copy

    def entry(ref, base=0):
        return lambda index: ref.at[base + index]

    seg_sems, k_sems, q_sems, o_sems, d_sems, dq_sems, dkv_sems = exchange_sems
    seg_copy = exchange(lambda target: tile, entry(segs, window), seg_sems)
    k_copy = exchange(entry(ks), entry(kv_ref, window), k_sems, True)
    q_copy = exchange(entry(qs), entry(qt_ref), q_sems)
    o_copy = exchange(entry(ot_ref), entry(mixed_t), o_sems)
    d_copy = exchange(entry(dos), entry(doct_ref), d_sems, True)
    dq_copy = exchange(entry(dqt_ref), entry(dq_in), dq_sems)
    dkv_copy = exchange(entry(dkv_sum), entry(dkv_in), dkv_sems)
    seg_hs, seg_hr, kv_hs, kv_hr, back_hs, back_hr = halo_sems

    def all_here(ref, sems):
        wait_received(place, ref.at[pl.ds(0, GROUP - 1)], sems.at[1])

    def all_sent(ref, sems):
        wait_sent(place, ref.at[pl.ds(0, GROUP - 1)], sems.at[0])

    def send_to(copy, target):
        offset = lax.rem(target - place.slot + GROUP, GROUP)

        @pl.when(offset != 0)
        def _():
            copy(offset).start()

    def await_from(copy, source):
        offset = lax.rem(place.slot - source + GROUP, GROUP)

        @pl.when(offset != 0)
        def _():
            copy(offset, True).wait_recv()

    greet(place, parts, True)

    row = iota((16, LANES), 0)
    numbers = seg_ref[...].astype(F32)
    tile[...] = jnp.where(row == 0, numbers[0:1], numbers[1:2]).astype(BF16)
    segs[window + place.slot] = tile[...]
    aux_ref[...] = jnp.zeros_like(aux_ref)
    for index, ref in enumerate(bias_refs):
        aux_ref[index : index + 1, 0 : ref.shape[-1]] = ref[...].astype(F32).reshape(1, ref.shape[-1])
    if window:

        @pl.when(place.part == 0)
        def _():
            kv_ref[pl.ds(0, window)] = jnp.zeros((window, LANES, LANES), BF16)

    plan = (
        (aux_ref, gaux, None),
        (win_ref, gwin, (width, 2 * width)),
        (win_ref, gwin, (0, width)),
    )
    g_aux, g_kv, g_q = [
        Gather(place, src, dst, sems, cols)
        for (src, dst, cols), sems in zip(plan, gather_sems[:3])
    ]
    rest = [
        TreeGather(place, src, dst, sems)
        for (src, dst), sems in zip(
            ((wo_ref, gwo), (wup_ref, gwup), (wdown_ref, gwdown)), gather_sems[3:]
        )
    ]
    g_kv.start_line()
    g_aux.start_line()
    g_q.start_line()
    loop(lambda offset: seg_copy(offset).start())
    g_kv.start_columns()
    g_aux.start_columns()
    g_q.start_columns()
    for gather in rest:
        gather.start_line()

    wait_received(place, segs.at[pl.ds(0, GROUP - 1)], seg_sems.at[1])

    def seg_halo(part):
        return remote(
            segs.at[pl.ds(GROUP, window)],
            segs.at[pl.ds(0, window)],
            seg_hs.at[0],
            seg_hr.at[0],
            place.member(place.slot, part),
        )

    if parts > 1:

        @pl.when(place.part < parts - 1)
        def _():
            seg_halo(place.part + 1).start()

    g_kv.start_hands()
    g_aux.start_hands()
    g_q.start_hands()
    g_aux.finish()
    g_kv.finish()

    aux = gaux[...].reshape(devices * 8, LANES)
    bias_q = spread_bias(aux, "query", per, width)
    bias_v = spread_bias(aux, "value", per, width)
    tokens = x_ref[...].reshape(2 * LANES, width)
    low_lane = iota((LANES, LANES), 1) < HD
    wide = 2 * LANES

    def column(kind, t):
        weight = gwin[:, :, :, :, :, pl.ds(kind * width + t * wide, wide)]
        return dot(tokens, weight.reshape(width, wide))

    def corners(t):
        for s in range(2):
            for u in range(2):
                at = (slice(s * LANES, (s + 1) * LANES), slice(u * LANES, (u + 1) * LANES))
                yield s * HEADS + t * 4 + u * 2, at

    for t in range(width // wide):
        k = column(1, t).astype(BF16).astype(F32)
        v = (column(2, t) + bias_v[:, t * wide : (t + 1) * wide]).astype(BF16).astype(F32)
        for head, at in corners(t):
            k_at, v_at = k[at], v[at]
            ks[head] = jnp.where(low_lane, k_at, pltpu.roll(v_at, HD, 1)).astype(BF16)
            ks[head + 1] = jnp.where(low_lane, pltpu.roll(k_at, HD, 1), v_at).astype(BF16)
    loop(lambda offset: k_copy(offset).start())
    kv_ref[window + place.slot] = ks[place.slot]
    g_q.finish()
    for t in range(width // wide):
        q = (column(0, t) + bias_q[:, t * wide : (t + 1) * wide]).astype(BF16).astype(F32) * 0.125
        for head, at in corners(t):
            turned = q[at].T.astype(BF16)
            qs[head] = turned[:HD]
            qs[head + 1] = turned[HD:]
    loop(lambda offset: q_copy(offset).start())
    qt_ref[place.slot] = qs[place.slot]

    for gather in rest:
        gather.start_first()

    if parts > 1:

        @pl.when(place.part < parts - 1)
        def _():
            seg_halo(place.part + 1).wait_send()

        @pl.when(place.part > 0)
        def _():
            seg_halo(place.part - 1).wait_recv()

    sequence = lax.div(place.slot, HEADS)
    chosen = jnp.where(iota((span, 16, LANES), 1) == sequence, segs[...].astype(F32), 0.0)
    seen = jnp.sum(chosen, axis=1)
    outside = (iota((span, LANES), 0) < window) & (place.part == 0)
    seen = jnp.where(outside, -1.0, seen)
    own = seen[window:]
    start = jnp.zeros((GROUP, LANES), F32)
    for number in range(docs):
        count = jnp.sum(jnp.where(seen == number - 1, 1.0, 0.0), axis=0, keepdims=True)
        count = jnp.sum(count, axis=1, keepdims=True)
        start = start + jnp.where(own >= number, count, 0.0)
    starts_ref[...] = start.astype(jnp.int32)

    for gather in rest:
        gather.start_second()

    def kv_halo(number, part):
        return remote(
            kv_ref.at[GROUP + number],
            kv_ref.at[number],
            kv_hs.at[number],
            kv_hr.at[number],
            place.member(place.slot, part),
        )

    def arrived(source):
        kvt[window + source] = kv_ref[window + source].T
        if parts > 1:

            @pl.when((place.part < parts - 1) & (source >= GROUP - window))
            def _():
                kv_halo(source - (GROUP - window), place.part + 1).start()

    arrived(place.slot)

    def kv_wait(offset):
        k_copy(offset, True).wait_recv()
        arrived(place.other_slot(-offset))

    loop(kv_wait)
    all_here(qt_ref, q_sems)

    many = window + 2
    older = window * LANES

    def q_rows_of(ref, m):
        return jnp.concatenate([ref[pl.ds(2 * m, 1)], ref[pl.ds(2 * m + 1, 1)]], axis=1)

    def turned_window(m):
        return jnp.concatenate([kvt[2 * m + i] for i in range(many)], axis=1)

    def masked(scores, start, q_place, block, base):
        k_place = base + block * BLOCK + iota((BLOCK, BLOCK), 0)
        visible = k_place >= start
        if block == reach:
            visible = visible & (k_place <= q_place)
        return jnp.where(visible, scores, NEG)

    blank = jnp.zeros((HD, BLOCK), BF16)

    def attend(step, carry):
        for number, gather in enumerate(rest):

            @pl.when(step == 1 + 2 * number)
            def _():
                gather.start_hands()

        if parts > 1:

            @pl.when((step == free) & (place.part > 0))
            def _():
                loop(lambda number: kv_halo(number, place.part - 1).wait_recv(), 0, window)

        @pl.when(step == free)
        def _():
            def turn(number):
                kvt[number] = kv_ref[number].T

            loop(turn, 0, window)

        turnover = place.slot
        late = lax.rem(step - free + GROUP + turnover, reach)
        if free:
            m = jnp.where(step < free, reach + lax.rem(step + turnover, free), late)
        else:
            m = late
        q_wide = jnp.concatenate([two(qt_ref, 2 * m), blank], axis=0)
        start = q_rows_of(starts_ref, m)
        base = m * BLOCK
        q_place = base + older + iota((1, BLOCK), 1)
        scores = [
            masked(
                dot(kv_ref[pl.ds(2 * (m + block), 2)].reshape(BLOCK, LANES), q_wide),
                start,
                q_place,
                block,
                base,
            )
            for block in range(reach + 1)
        ]
        peak = functools.reduce(jnp.maximum, scores)
        peak = jnp.max(peak, axis=0, keepdims=True)
        weights = [jnp.exp(score - peak) for score in scores]
        total = functools.reduce(jnp.add, weights)
        total = jnp.sum(total, axis=0, keepdims=True)
        weights = jnp.concatenate([weight.astype(BF16) for weight in weights], axis=0)
        out = dot(turned_window(m)[HD:], weights) / total
        lse = peak + jnp.log(total)
        for side in range(2):
            lanes = slice(side * LANES, (side + 1) * LANES)
            of_ref[2 * m + side] = out[:, lanes]
            ot_ref[2 * m + side] = out[:, lanes].astype(BF16)
            lse_ref[pl.ds(2 * m + side, 1)] = lse[:, lanes]
            send_to(o_copy, 2 * m + side)
        return carry

    lax.fori_loop(0, pairs_of_chunks, attend, 0)
    mixed_t[place.slot] = ot_ref[place.slot]

    a0, a1 = alphas_ref[0], alphas_ref[1]
    bias_out = spread_bias(aux, "output", per, width)
    bias_down = spread_bias(aux, "down", per, width)
    bias_up = spread_bias(aux, "up", per_up, hidden)
    rows = 2 * LANES
    wide_tokens = tokens.astype(F32)
    grads = grad_ref[...].reshape(rows, width).astype(F32)
    grad_ffn = (a1 * grads).astype(BF16)
    for gather in rest:
        gather.finish()
    full_out = gwo[...].reshape(width, width)

    all_here(mixed_t, o_sems)
    mixed_turned = mixed_t[...].reshape(2, width, LANES)
    mixed = jnp.concatenate([mixed_turned[0].T, mixed_turned[1].T], axis=0)
    branch = dot(mixed, full_out) + bias_out
    attn_term = a0 * branch
    residual = wide_tokens + attn_term
    hidden_in = residual.astype(BF16)

    ffn = jnp.zeros((rows, width), F32) + bias_down
    grad_res = grads
    tile_up = 512
    whole_up = gwup.reshape(width, hidden)
    whole_down = gwdown.reshape(hidden, width)
    for t in range(hidden // tile_up):
        cols = pl.ds(t * tile_up, tile_up)
        w_up = whole_up[:, cols]
        w_down = whole_down[cols, :]
        pre = dot(hidden_in, w_up) + bias_up[:, t * tile_up : (t + 1) * tile_up]
        phi = 0.5 * (1.0 + lax.erf(pre * (1.0 / math.sqrt(2.0))))
        act = (pre * phi).astype(BF16)
        act_s[:, cols] = act
        ffn = ffn + dot(act, w_down)
        slope = phi + pre * jnp.exp(-0.5 * pre * pre) * (1.0 / math.sqrt(2.0 * math.pi))
        gpre = (dot_nt(grad_ffn, w_down) * slope).astype(BF16)
        gpre_s[:, cols] = gpre
        grad_res = grad_res + dot_nt(gpre, w_up)
    gres_ref[...] = grad_res
    grad_branch = (a0 * grad_res).astype(BF16)
    grad_mixed = dot_nt(grad_branch, full_out).astype(BF16).astype(F32)
    for s in range(2):
        turned = grad_mixed[s * LANES : (s + 1) * LANES].T.astype(BF16)
        dos[pl.ds(s * HEADS, HEADS)] = turned.reshape(HEADS, HD, LANES)
    loop(lambda offset: d_copy(offset).start())
    doct_ref[place.slot] = dos[place.slot]

    kinds = (TreeReduce, TreeReduce, TreeReduce, Reduce, Reduce, Reduce)
    t_out, t_up, t_down, t_kv, t_q, t_aux = [
        kind(place, part, out, *scratch)
        for kind, (part, out), scratch in zip(
            kinds,
            (
                (p_out, r_out),
                (p_up, r_up),
                (p_down, r_down),
                (p_win[1], r_win.at[:, pl.ds(width, 2 * width)]),
                (p_win[0], r_win.at[:, pl.ds(0, width)]),
                (p_aux, r_aux),
            ),
            trees,
        )
    ]
    lead = (2, 2, depth, 2)
    for t in range(hidden // tile_up):
        cols = pl.ds(t * tile_up, tile_up)
        block = dot_tn(act_s[:, cols], grad_ffn).astype(BF16)
        p_down.reshape(hidden, width)[cols, :] = block
    t_down.start_core()
    for t in range(hidden // tile_up):
        cols = pl.ds(t * tile_up, tile_up)
        block = dot_tn(hidden_in, gpre_s[:, cols]).astype(BF16)
        p_up.reshape(width, hidden)[:, cols] = block
    t_up.start_core()
    p_out.reshape(width, width)[...] = dot(
        jnp.concatenate([mixed_turned[0], mixed_turned[1]], axis=1), grad_branch
    ).astype(BF16)
    t_out.start_core()

    ffn_term = a1 * ffn
    stream = residual + ffn_term
    out_ref[...] = stream.astype(BF16).reshape(2, LANES, width)

    def whole(values):
        return jnp.sum(jnp.sum(values, axis=0, keepdims=True), axis=1, keepdims=True)

    sums = (
        whole(stream * stream),
        whole(attn_term * attn_term),
        whole(ffn_term * ffn_term),
        whole(grad_res * branch),
        whole(grads * ffn),
    )
    lane = iota((devices * 8, LANES), 1)
    scalars = jnp.zeros((devices * 8, LANES), F32)
    for number, value in enumerate(sums):
        scalars = scalars + jnp.where(lane == number, value, 0.0)
    up_row = jnp.sum(gpre_s[...].astype(F32), axis=0, keepdims=True)
    down_row = jnp.sum(grad_ffn.astype(F32), axis=0, keepdims=True)
    out_row = jnp.sum(grad_branch.astype(F32), axis=0, keepdims=True)
    folded = (
        fold_bias(out_row, devices * 8, "output", per)
        + fold_bias(down_row, devices * 8, "down", per)
        + fold_bias(up_row, devices * 8, "up", per_up)
        + jnp.where((iota((devices * 8, LANES), 0) & 7) == SCALARS, scalars, 0.0)
    )
    p_aux[...] = folded.reshape(*lead, 8, LANES)

    early = (t_down, t_up, t_out)
    low_block = iota((BLOCK, LANES), 1) < HD

    def clear(number):
        acc[number] = jnp.zeros((LANES, LANES), F32)

    loop(clear, 0, span)

    def back_halo(part):
        return remote(
            halo_out, halo_in, back_hs.at[0], back_hr.at[0], place.member(place.slot, part)
        )

    def settle(number):
        dkv_sum[number] = acc[window + number].astype(BF16)

    def attend_back(m, carry):
        for number, tree in enumerate(early):

            @pl.when(m == 1 + number)
            def _():
                tree.start_second()

        await_from(d_copy, 2 * m)
        await_from(d_copy, 2 * m + 1)
        qt, dt = two(qt_ref, 2 * m), two(doct_ref, 2 * m)
        q_wide = jnp.concatenate([qt, blank], axis=0)
        d_wide = jnp.concatenate([blank, dt], axis=0)
        both = jnp.concatenate([qt, dt], axis=0).astype(F32).T
        q_and_d = jnp.concatenate(
            [jnp.where(low_block, both, 0.0), jnp.where(low_block, 0.0, both)], axis=0
        ).astype(BF16)
        start = q_rows_of(starts_ref, m)
        lse = q_rows_of(lse_ref, m)
        delta = jnp.sum(dt.astype(F32) * two(of_ref, 2 * m), axis=0, keepdims=True)
        base = m * BLOCK
        q_place = base + older + iota((1, BLOCK), 1)
        grad_scores = []
        for block in range(reach + 1):
            here = pl.ds(2 * (m + block), 2)
            kv = kv_ref[here].reshape(BLOCK, LANES)
            scores = masked(dot(kv, q_wide), start, q_place, block, base)
            probs = jnp.exp(scores - lse)
            grad_score = (probs * (dot(kv, d_wide) - delta)).astype(BF16)
            grad_scores.append(grad_score)
            both_scores = jnp.concatenate([grad_score, probs.astype(BF16)], axis=1)
            acc[here] += dot(both_scores, q_and_d).reshape(2, LANES, LANES)
        dq = dot(turned_window(m)[:HD], jnp.concatenate(grad_scores, axis=0)) * 0.125
        for side in range(2):
            dqt_ref[2 * m + side] = dq[:, side * LANES : (side + 1) * LANES].astype(BF16)
            send_to(dq_copy, 2 * m + side)
        if parts > 1:

            @pl.when((m == reach - 1) & (place.part > 0))
            def _():
                def put(number):
                    halo_out[number] = acc[number].astype(BF16)

                loop(put, 0, window)
                back_halo(place.part - 1).start()

        if free:

            @pl.when(m >= reach)
            def _():
                for side in range(2):
                    chunk = 2 * (m - reach) + side
                    settle(chunk)
                    send_to(dkv_copy, chunk)

        return carry

    lax.fori_loop(0, pairs_of_chunks, attend_back, 0)
    dq_in[place.slot] = dqt_ref[place.slot]
    loop(settle, GROUP - window, GROUP)
    if parts > 1:

        @pl.when(place.part < parts - 1)
        def _():
            back_halo(place.part + 1).wait_recv()

            def add(number):
                chunk = GROUP - window + number
                total = acc[window + chunk] + halo_in[number].astype(F32)
                dkv_sum[chunk] = total.astype(BF16)

            loop(add, 0, window)

    def late(offset):
        @pl.when(place.other_slot(offset) >= GROUP - window)
        def _():
            dkv_copy(offset).start()

    loop(late)
    dkv_in[place.slot] = dkv_sum[place.slot]
    for tree in early:
        tree.start_first()

    tokens_turned = tokens.T
    all_here(dq_in, dq_sems)
    for s in range(2):
        turned = dq_in[pl.ds(s * HEADS, HEADS)].reshape(width, LANES).astype(F32)
        gp[s * LANES : (s + 1) * LANES, 0:width] = turned.T.astype(BF16)
    query_row = jnp.sum(gp[:, 0:width].astype(F32), axis=0, keepdims=True)
    p_win[0][...] = (
        dot(tokens_turned, gp[:, 0:width])
        .astype(BF16)
        .reshape(*lead, width // devices, width)
    )
    t_q.start_core()
    full_in = gwin.reshape(width, 3 * width)
    gx = gres_ref[...] + dot_nt(gp[:, 0:width], full_in[:, 0:width])
    t_q.start_columns()

    all_here(dkv_in, dkv_sems)
    for s in range(2):
        at_rows = slice(s * LANES, (s + 1) * LANES)
        for pair in range(HEADS // 2):
            even = dkv_in[s * HEADS + 2 * pair].astype(F32)
            odd = dkv_in[s * HEADS + 2 * pair + 1].astype(F32)
            keys = jnp.where(low_lane, even, pltpu.roll(odd, HD, 1))
            values = jnp.where(low_lane, pltpu.roll(even, HD, 1), odd)
            at = width + pair * LANES
            gp[at_rows, at : at + LANES] = keys.astype(BF16)
            gp[at_rows, width + at : width + at + LANES] = values.astype(BF16)
    for t in range(2):
        part = dot(tokens_turned, gp[:, (1 + t) * width : (2 + t) * width]).astype(BF16)
        p_win[1][:, :, :, :, :, t * width : (t + 1) * width] = part.reshape(
            *lead, width // devices, width
        )
    t_kv.start_core()
    for tree in early:
        tree.start_line()
    value_row = jnp.sum(gp[:, 2 * width :].astype(F32), axis=0, keepdims=True)
    folded = fold_bias(query_row, devices * 8, "query", per) + fold_bias(
        value_row, devices * 8, "value", per
    )
    p_aux[...] += folded.reshape(*lead, 8, LANES)
    t_aux.start_core()
    t_q.start_line()
    t_kv.start_columns()
    t_aux.start_columns()
    for t in range(1, 3):
        cols = slice(t * width, (t + 1) * width)
        gx = gx + dot_nt(gp[:, cols], full_in[:, cols])
    gx_ref[...] = gx.astype(BF16).reshape(2, LANES, width)
    t_aux.start_line()
    t_kv.start_line()
    for tree in early:
        tree.finish()
    t_q.finish()
    t_aux.finish()
    t_kv.finish()

    all_sent(segs, seg_sems)
    all_sent(ks, k_sems)
    all_sent(qs, q_sems)
    all_sent(ot_ref, o_sems)
    all_sent(dos, d_sems)
    all_sent(dqt_ref, dq_sems)
    all_sent(dkv_sum, dkv_sems)
    if parts > 1:

        @pl.when(place.part < parts - 1)
        def _():
            loop(lambda number: kv_halo(number, place.part + 1).wait_send(), 0, window)

        @pl.when(place.part > 0)
        def _():
            back_halo(place.part - 1).wait_send()

    for gather in (g_aux, g_kv, g_q, *rest):
        gather.drain()
    for tree in early + (t_q, t_kv, t_aux):
        tree.drain()


def two(ref, index):
    return jnp.concatenate([ref[index], ref[index + 1]], axis=1)


def hand_out_kernel(
    tokens_all, out_ref, gx_ref, win_ref, wo_ref, wup_ref, wdown_ref, sums_ref, *results
):
    for src, dst in zip((out_ref, gx_ref, win_ref, wo_ref, wup_ref, wdown_ref), results[:6]):
        dst[...] = src[...]
    named = dict(zip(("query", "value", "output", "up", "down"), results[6:11]))
    for name, ref in named.items():
        ref[...] = sums_ref[BIASES.index(name), 0 : ref.shape[0]]
    results[11][...] = sums_ref[SCALARS, 3:5]
    results[12][...] = jnp.sqrt(sums_ref[SCALARS, 0:3] * (1.0 / tokens_all))


def call(kernel, out_shape, in_specs, out_specs, scratch, collective=None):
    return pl.pallas_call(
        kernel,
        out_shape=out_shape,
        in_specs=in_specs,
        out_specs=out_specs,
        scratch_shapes=scratch,
        compiler_params=pltpu.CompilerParams(
            collective_id=collective,
            has_side_effects=collective is not None,
            vmem_limit_bytes=VMEM_BYTES,
        ),
    )


def local(
    layer_input,
    segments,
    input_weight,
    output_weight,
    up_weight,
    down_weight,
    query_bias,
    value_bias,
    output_bias,
    up_bias,
    down_bias,
    alphas,
    out_grad,
):
    heads, blocks = lax.axis_size("head"), lax.axis_size("blk")
    depth, devices = blocks // 2, heads * blocks
    seqs, rows, width = layer_input.shape
    hidden = up_weight.shape[1]
    seq_len = rows * devices
    assert heads == 4 and seqs * HEADS == GROUP and rows == LANES
    longest = 16 * math.isqrt(seq_len)
    window, parts = longest // rows, devices // GROUP
    docs = 2 * seq_len // longest
    assert window <= GROUP and window % 2 == 0
    span = window + GROUP

    def shape(*dims, dtype=BF16):
        return jax.ShapeDtypeStruct(dims, dtype)

    vmem, smem = pl.BlockSpec(memory_space=VMEM), pl.BlockSpec(memory_space=pltpu.SMEM)
    dma = pltpu.SemaphoreType.DMA
    lead = (2, 2, depth, 2)
    in_rows, up_rows = input_weight.shape[0], down_weight.shape[0]
    reduced = (
        (in_rows, width, BF16),
        (in_rows, hidden, BF16),
        (up_rows, width, BF16),
        (in_rows, 2 * width, BF16),
        (in_rows, width, BF16),
        (8, LANES, F32),
    )
    tokens = seqs * rows
    results = (
        shape(seqs, rows, width),
        shape(seqs, rows, width),
        shape(in_rows, 3 * width, dtype=F32),
        shape(in_rows, width, dtype=F32),
        shape(in_rows, hidden, dtype=F32),
        shape(up_rows, width, dtype=F32),
    )
    carried = call(
        functools.partial(layer_kernel, blocks, parts, window, docs),
        results + (shape(8, LANES, dtype=F32),),
        [vmem] * 6 + [(vmem,) * 5] + [smem, vmem],
        (vmem,) * 7,
        [
            [
                VMEM((*lead, in_rows, 3 * width), BF16),
                VMEM((*lead, in_rows, width), BF16),
                VMEM((*lead, in_rows, hidden), BF16),
                VMEM((*lead, up_rows, width), BF16),
                VMEM((*lead, 8, LANES), F32),
            ],
            [dma((Gather.COUNT,))] * 3 + [dma((TreeGather.COUNT,))] * 3,
            [TreeReduce.scratch(depth, *sizes) for sizes in reduced[:3]]
            + [Reduce.scratch(depth, *sizes) for sizes in reduced[3:]],
            [dma((2,)), dma((GROUP,)), dma((2,)), dma((2,)), dma((GROUP,)), dma((2,)), dma((2,))],
            [dma((1,)), dma((1,)), dma((window,)), dma((window,)), dma((1,)), dma((1,))],
            VMEM((span, 16, LANES), BF16),
            VMEM((16, LANES), BF16),
            VMEM((8, LANES), F32),
            VMEM((GROUP, HD, LANES), BF16),
            VMEM((GROUP, LANES, LANES), BF16),
            VMEM((GROUP, HD, LANES), BF16),
            VMEM((span, LANES, LANES), BF16),
            VMEM((span, LANES, LANES), BF16),
            VMEM((GROUP, LANES), jnp.int32),
            VMEM((GROUP, HD, LANES), BF16),
            VMEM((GROUP, HD, LANES), F32),
            VMEM((GROUP, LANES), F32),
            VMEM((GROUP, HD, LANES), BF16),
            VMEM((GROUP, HD, LANES), BF16),
            VMEM((GROUP, HD, LANES), BF16),
            VMEM((tokens, hidden), BF16),
            VMEM((tokens, hidden), BF16),
            VMEM((tokens, width), F32),
            VMEM((span, LANES, LANES), F32),
            VMEM((GROUP, HD, LANES), BF16),
            VMEM((GROUP, LANES, LANES), BF16),
            VMEM((GROUP, HD, LANES), BF16),
            VMEM((GROUP, LANES, LANES), BF16),
            VMEM((window, LANES, LANES), BF16),
            VMEM((window, LANES, LANES), BF16),
            VMEM((tokens, 3 * width), BF16),
            [
                [
                    VMEM((*lead, in_rows, width), BF16),
                    VMEM((*lead, in_rows, 2 * width), BF16),
                ],
                VMEM((*lead, in_rows, width), BF16),
                VMEM((*lead, in_rows, hidden), BF16),
                VMEM((*lead, up_rows, width), BF16),
                VMEM((*lead, 8, LANES), F32),
            ],
        ],
        collective=0,
    )(
        layer_input,
        segments,
        input_weight,
        output_weight,
        up_weight,
        down_weight,
        (query_bias, value_bias, output_bias, down_bias, up_bias),
        alphas,
        out_grad,
    )
    per, per_up = width // devices, hidden // devices
    return call(
        functools.partial(hand_out_kernel, seqs * seq_len * width),
        results
        + tuple(
            shape(size, dtype=F32) for size in (per, per, per, per_up, per, 2, 3)
        ),
        [vmem] * 7,
        (vmem,) * 13,
        [],
    )(*carried)


def solution(mesh):
    tokens = P(None, ("head", "blk"), None)
    rows, flat = P(("head", "blk"), None), P(("head", "blk"))
    return jax.shard_map(
        local,
        mesh=mesh,
        in_specs=(
            tokens,
            P(None, ("head", "blk")),
            rows,
            rows,
            rows,
            rows,
            flat,
            flat,
            flat,
            flat,
            flat,
            P(),
            tokens,
        ),
        out_specs=(
            tokens,
            tokens,
            rows,
            rows,
            rows,
            rows,
            flat,
            flat,
            flat,
            flat,
            flat,
            P(),
            P(),
        ),
        check_vma=False,
    )
```

```python
import functools
import math

import jax
import jax.numpy as jnp
from jax import lax
from jax.experimental import pallas as pl
from jax.experimental.pallas import tpu as pltpu
from jax.sharding import PartitionSpec as P

HEADS = 8
HD = 64
LANES = 128
GROUP = 16
BLOCK = 256
VMEM_BYTES = 60 * 1024 * 1024
F32 = jnp.float32
BF16 = jnp.bfloat16
VMEM = pltpu.VMEM
NEG = -1e30


def column_of(kind, pair, width):
    if kind == "q":
        return 2 * width + pair * LANES
    first = (pair % 2) * width + (pair // 2) * LANES
    return first + (width // 2 if kind == "v" else 0)


def columns_between(width):
    for number, kind in enumerate("qkv"):
        for pair in range(width // LANES):
            yield number * width + pair * LANES, column_of(kind, pair, width)


class Place:
    def __init__(self, blocks):
        self.blocks = blocks
        self.depth = blocks // 2
        head = lax.axis_index("head")
        block = lax.axis_index("blk")
        self.x, self.core = lax.div(head, 2), lax.rem(head, 2)
        self.z, self.y = lax.div(block, 2), lax.rem(block, 2)
        flat = head * blocks + block
        self.part, self.slot = lax.div(flat, GROUP), lax.rem(flat, GROUP)

    def at(self, x=None, core=None, z=None, y=None):
        x = self.x if x is None else x
        core = self.core if core is None else core
        z = self.z if z is None else z
        y = self.y if y is None else y
        return (x * 2 + core, z * 2 + y)

    def deeper(self, offset):
        return lax.rem(self.z + offset + self.depth, self.depth)

    def bits(self):
        bit = self.depth // 2
        while bit:
            yield bit
            bit //= 2

    def flipped(self, bits):
        z = self.z
        for bit in self.bits():
            if bits & bit:
                z = z + bit - 2 * bit * lax.rem(lax.div(self.z, bit), 2)
        return z

    def member(self, slot, part=None):
        part = self.part if part is None else part
        flat = part * GROUP + slot
        return (lax.div(flat, self.blocks), lax.rem(flat, self.blocks))

    def other_slot(self, offset):
        return lax.rem(self.slot + offset + GROUP, GROUP)


def remote(src, dst, send, recv, device):
    return pltpu.make_async_remote_copy(
        src_ref=src,
        dst_ref=dst,
        send_sem=send,
        recv_sem=recv,
        device_id=device,
        device_id_type=pl.DeviceIdType.MESH,
    )


def greet(place, parts, tree):
    barrier = pltpu.get_barrier_semaphore()

    def hello(device):
        pl.semaphore_signal(barrier, inc=1, device_id=device, device_id_type=pl.DeviceIdType.MESH)

    def group(offset, carry):
        hello(place.member(place.other_slot(offset)))
        return carry

    lax.fori_loop(1, GROUP, group, 0)
    total = GROUP - 1
    if tree:

        def line(offset, carry):
            hello(place.at(z=place.deeper(offset)))
            return carry

        lax.fori_loop(1, place.depth, line, 0)
        hello(place.at(x=1 - place.x))
        hello(place.at(y=1 - place.y))
        hello(place.at(x=1 - place.x, y=1 - place.y))
        hello(place.at(core=1 - place.core))
        total += place.depth + 3
    if parts > 1 and tree:

        @pl.when(place.part > 0)
        def _():
            hello(place.member(place.slot, place.part - 1))

        @pl.when(place.part < parts - 1)
        def _():
            hello(place.member(place.slot, place.part + 1))

        total += jnp.where(place.part > 0, 1, 0) + jnp.where(place.part < parts - 1, 1, 0)
    pl.semaphore_wait(barrier, total)


def halves_of(columns):
    if columns < 2 * LANES:
        return ((0, columns, "yx"),)
    most = columns // 2
    return ((0, most, "yx"), (most, columns - most, "xy"))


def wait_received(place, dst, sem):
    remote(dst, dst, sem, sem, place.at(core=1 - place.core)).wait_recv()


def wait_sent(place, src, sem):
    remote(src, src, sem, sem, place.at(core=1 - place.core)).wait_send()


class Gather:
    COUNT = 9

    def __init__(self, place, src, dst, sems, cols=None):
        self.place, self.src, self.dst, self.sems = place, src, dst, sems
        start, width = cols or (0, dst.shape[-1])
        self.cols = pl.ds(start, width)

    def part(self, *index):
        return self.dst.at[index + (slice(None), self.cols)]

    def column(self, core, x, y):
        return self.part(x, core, slice(None), y)

    def others(self):
        place = self.place
        return ((1 - place.x, place.y), (place.x, 1 - place.y), (1 - place.x, 1 - place.y))

    def own(self):
        place = self.place
        mine = self.part(place.x, place.core, place.z, place.y)
        return pltpu.make_async_copy(self.src.at[:, self.cols], mine, self.sems.at[0])

    def start_line(self):
        place = self.place
        for offset in range(1, place.depth):
            remote(
                self.src.at[:, self.cols],
                self.part(place.x, place.core, place.z, place.y),
                self.sems.at[1],
                self.sems.at[2],
                place.at(z=place.deeper(offset)),
            ).start()
        self.own().start()

    def lines(self):
        return self.part(0, 0, pl.ds(0, self.place.depth - 1), 0)

    def hand(self, x, y):
        place = self.place
        column = self.column(place.core, x, y)
        remote(
            column, column, self.sems.at[7], self.sems.at[8], place.at(core=1 - place.core)
        ).start()

    def start_columns(self):
        place = self.place
        self.own().wait()
        wait_received(place, self.lines(), self.sems.at[2])
        mine = self.column(place.core, place.x, place.y)
        for number, (x, y) in enumerate(self.others()):
            remote(
                mine, mine, self.sems.at[3], self.sems.at[4 + number], place.at(x=x, y=y)
            ).start()
        self.hand(place.x, place.y)

    def start_hands(self):
        for number, (x, y) in enumerate(self.others()):
            wait_received(
                self.place, self.column(self.place.core, x, y), self.sems.at[4 + number]
            )
            self.hand(x, y)

    def finish(self):
        every = slice(None)
        region = self.part(every, 1 - self.place.core, every, every)
        wait_received(self.place, region, self.sems.at[8])

    def drain(self):
        place = self.place
        wait_sent(place, self.lines(), self.sems.at[1])
        every = slice(None)
        wait_sent(
            place, self.part(every, every, pl.ds(0, 3 * place.depth // 4), 0), self.sems.at[3]
        )
        wait_sent(place, self.part(every, 0, every, every), self.sems.at[7])


def halves_of(columns):
    if columns < 2 * LANES:
        return ((0, columns, "yx"),)
    most = columns // 2
    return ((0, most, "yx"), (most, columns - most, "xy"))


class TreeGather:
    COUNT = 12

    def __init__(self, place, src, dst, sems, cols=None):
        self.place, self.src, self.dst, self.sems = place, src, dst, sems
        self.start, self.width = cols or (0, dst.shape[-1])
        self.halves = halves_of(self.width)
        self.cols = pl.ds(self.start, self.width)

    def part(self, *index):
        return self.dst.at[index + (slice(None), self.cols)]

    def cut(self, half, *index):
        start, width, _ = half
        return self.dst.at[index + (slice(None), pl.ds(self.start + start, width))]

    def across(self, half, first):
        place = self.place
        if (half[2] == "yx") == first:
            return place.x, 1 - place.y
        return 1 - place.x, place.y

    def region(self, half, first, core, x, y):
        every = slice(None)
        if first:
            return self.cut(half, x, core, every, y)
        if half[2] == "yx":
            return self.cut(half, x, core, every, every)
        return self.cut(half, every, core, every, y)

    def own(self):
        place = self.place
        mine = self.part(place.x, place.core, place.z, place.y)
        return pltpu.make_async_copy(self.src.at[:, self.cols], mine, self.sems.at[0])

    def send_piece(self, bits, bit):
        place = self.place
        piece = self.part(place.x, place.core, place.flipped(bits), place.y)
        remote(
            piece if bits else self.src.at[:, self.cols],
            piece,
            self.sems.at[1],
            self.sems.at[11 + (bits | bit)],
            place.at(z=place.flipped(bit)),
        ).start()

    def await_piece(self, bits):
        place = self.place
        piece = self.part(place.x, place.core, place.flipped(bits), place.y)
        wait_received(place, piece, self.sems.at[11 + bits])

    def start_line(self):
        for bit in self.place.bits():
            self.send_piece(0, bit)
        self.own().start()

    def start_step(self):
        known = [0]
        for bit in self.place.bits():
            for bits in known[1:]:
                self.send_piece(bits, bit)
            known += [bits | bit for bits in known]
            if bit > 1:
                for bits in known[len(known) // 2 :]:
                    self.await_piece(bits)

    def lines(self):
        return self.part(0, 0, pl.ds(0, self.place.depth - 1), 0)

    def exchange(self, number, first):
        place, half = self.place, self.halves[number]
        x, y = self.across(half, first)
        mine = self.region(half, first, place.core, place.x, place.y)
        base = 0 if first else 2
        return remote(
            mine,
            mine,
            self.sems.at[3 + base + number],
            self.sems.at[8 + base + number],
            place.at(x=x, y=y),
        )

    def received(self, number, first):
        half = self.halves[number]
        x, y = self.across(half, first)
        region = self.region(half, first, self.place.core, x, y)
        wait_received(self.place, region, self.sems.at[(8 if first else 10) + number])
        return region

    def hand(self, region):
        place = self.place
        remote(
            region, region, self.sems.at[7], self.sems.at[2], place.at(core=1 - place.core)
        ).start()

    def start_first(self):
        place = self.place
        self.own().wait()
        for bits in range(1, place.depth, 2):
            self.await_piece(bits)
        for number in range(len(self.halves)):
            self.exchange(number, True).start()
        self.hand(self.part(place.x, place.core, slice(None), place.y))

    def start_second(self):
        for number in range(len(self.halves)):
            region = self.received(number, True)
            self.exchange(number, False).start()
            self.hand(region)

    def start_hands(self):
        for number in range(len(self.halves)):
            self.hand(self.received(number, False))

    def finish(self):
        every = slice(None)
        region = self.part(every, 1 - self.place.core, every, every)
        wait_received(self.place, region, self.sems.at[2])

    def drain(self):
        for number in range(len(self.halves)):
            self.exchange(number, True).wait_send()
            self.exchange(number, False).wait_send()
        wait_sent(self.place, self.lines(), self.sems.at[1])
        every = slice(None)
        wait_sent(self.place, self.part(every, 0, every, every), self.sems.at[7])


class Reduce:
    COUNT = 8

    def __init__(self, place, part, out, rc, total, rn, rz, sems, cols=None):
        self.place, self.part = place, part
        self.cols = pl.ds(*(cols or (0, part.shape[-1])))
        self.out = out.at[:, self.cols]
        self.rc, self.total, self.rn, self.rz, self.sems = rc, total, rn, rz, sems

    @staticmethod
    def scratch(depth, rows, cols, dtype):
        return [
            VMEM((2, depth, 2, rows, cols), dtype),
            VMEM((2, depth, 2, rows, cols), dtype),
            VMEM((3, depth, rows, cols), dtype),
            VMEM((depth - 1, rows, cols), dtype),
            pltpu.SemaphoreType.DMA((Reduce.COUNT,)),
        ]

    def others(self):
        place = self.place
        return ((1 - place.x, place.y), (place.x, 1 - place.y), (1 - place.x, 1 - place.y))

    def core(self):
        place = self.place
        return remote(
            self.part.at[:, 1 - place.core, :, :, :, self.cols],
            self.rc,
            self.sems.at[0],
            self.sems.at[1],
            place.at(core=1 - place.core),
        )

    def columns(self):
        place = self.place
        for number, (x, y) in enumerate(self.others()):
            yield remote(
                self.total.at[x, :, y],
                self.rn.at[number],
                self.sems.at[2],
                self.sems.at[3 + number],
                place.at(x=x, y=y),
            )

    def line(self, offset):
        place = self.place
        return remote(
            self.total.at[place.x, place.deeper(offset), place.y],
            self.rz.at[offset - 1],
            self.sems.at[6],
            self.sems.at[7],
            place.at(z=place.deeper(offset)),
        )

    def start_core(self):
        self.core().start()

    def add_core(self, x, z, y):
        place = self.place
        self.total[x, z, y] = self.part[x, place.core, z, y, :, self.cols] + self.rc[x, z, y]

    def start_columns(self):
        place = self.place
        self.core().wait_recv()
        for copy, (x, y) in zip(self.columns(), self.others()):

            def add(z, carry):
                self.add_core(x, z, y)
                return carry

            lax.fori_loop(0, place.depth, add, 0)
            copy.start()

        def add(z, carry):
            self.add_core(place.x, z, place.y)
            return carry

        lax.fori_loop(0, place.depth, add, 0)

    def start_line(self):
        place = self.place
        for copy in self.columns():
            copy.wait_recv()
        here = (place.x, slice(None), place.y)
        total = self.total[here].astype(F32)
        for number in range(3):
            total = total + self.rn[number].astype(F32)
        self.total[here] = total.astype(self.total.dtype)
        for offset in range(1, place.depth):
            self.line(offset).start()

    def finish(self):
        place = self.place
        wait_received(place, self.rz, self.sems.at[7])
        result = self.total[place.x, place.z, place.y].astype(F32)
        for offset in range(1, place.depth):
            result = result + self.rz[offset - 1].astype(F32)
        self.out[...] = result

    def drain(self):
        place = self.place
        self.core().wait_send()
        wait_sent(place, self.rn, self.sems.at[2])
        wait_sent(place, self.rz, self.sems.at[6])


class TreeReduce:
    COUNT = 12

    def __init__(self, place, part, out, rc, total, ra, rb, fa, fb, rz, sems, cols=None):
        self.place, self.part = place, part
        self.cols = pl.ds(*(cols or (0, part.shape[-1])))
        self.out = out.at[:, self.cols]
        self.rc, self.total, self.rz = rc, total, rz
        self.second, self.first = (ra, rb), (fa, fb)
        self.sems = sems
        self.halves = halves_of(total.shape[-1])

    @staticmethod
    def scratch(depth, rows, cols, dtype):
        wide, narrow = [half[1] for half in halves_of(cols)]
        return [
            VMEM((2, depth, 2, rows, cols), dtype),
            VMEM((2, depth, 2, rows, cols), dtype),
            VMEM((depth, 2, rows, wide), dtype),
            VMEM((2, depth, rows, narrow), dtype),
            VMEM((depth, rows, wide), dtype),
            VMEM((depth, rows, narrow), dtype),
            VMEM((depth - 1, rows, cols), dtype),
            pltpu.SemaphoreType.DMA((TreeReduce.COUNT + depth - 1,)),
        ]

    core, start_core, add_core = Reduce.core, Reduce.start_core, Reduce.add_core

    def cut(self, half, *index):
        start, width, _ = half
        return index + (slice(None), pl.ds(start, width))

    def exchange(self, number, second):
        place, every = self.place, slice(None)
        half = self.halves[number]
        slot = (2 if second else 8) + number
        over_x = (half[2] == "yx") == second
        device = place.at(x=1 - place.x) if over_x else place.at(y=1 - place.y)
        if second:
            index = (1 - place.x, every, every) if over_x else (every, every, 1 - place.y)
            landing = self.second[number]
        else:
            index = (1 - place.x, every, place.y) if over_x else (place.x, every, 1 - place.y)
            landing = self.first[number]
        return remote(
            self.total.at[self.cut(half, *index)],
            landing,
            self.sems.at[slot],
            self.sems.at[slot + 2],
            device,
        )

    def start_second(self):
        self.core().wait_recv()

        def add(z, carry):
            for x in range(2):
                for y in range(2):
                    self.add_core(x, z, y)
            return carry

        lax.fori_loop(0, self.place.depth, add, 0)
        for number in range(len(self.halves)):
            self.exchange(number, True).start()

    def accumulate(self, index, value):
        self.total[index] = self.total[index] + value

    def start_first(self):
        place = self.place
        for number, half in enumerate(self.halves):
            self.exchange(number, True).wait_recv()
            landed = self.second[number]

            def add(z, carry):
                for other in range(2):
                    if half[2] == "yx":
                        self.accumulate(self.cut(half, place.x, z, other), landed[z, other])
                    else:
                        self.accumulate(self.cut(half, other, z, place.y), landed[other, z])
                return carry

            lax.fori_loop(0, place.depth, add, 0)
            self.exchange(number, False).start()

    def start_line(self):
        place = self.place
        for number, half in enumerate(self.halves):
            self.exchange(number, False).wait_recv()
            landed = self.first[number]

            def add(z, carry):
                self.accumulate(self.cut(half, place.x, z, place.y), landed[z])
                return carry

            lax.fori_loop(0, place.depth, add, 0)
        self.send_over(1)

    def offsets(self, bit):
        return range(bit, self.place.depth, 2 * bit)

    def send_over(self, bit):
        place = self.place
        for bits in self.offsets(bit):
            remote(
                self.total.at[place.x, place.flipped(bits), place.y],
                self.rz.at[bits - 1],
                self.sems.at[6],
                self.sems.at[11 + bits],
                place.at(z=place.flipped(bit)),
            ).start()

    def start_step(self):
        place = self.place
        bit = 1
        while 2 * bit < place.depth:
            for bits in self.offsets(bit):
                wait_received(place, self.rz.at[bits - 1], self.sems.at[11 + bits])
                here = (place.x, place.flipped(bits - bit), place.y)
                self.total[here] = self.total[here] + self.rz[bits - 1]
            bit *= 2
            self.send_over(bit)

    def finish(self):
        place = self.place
        last = place.depth // 2
        wait_received(place, self.rz.at[last - 1], self.sems.at[11 + last])
        total = self.total[place.x, place.z, place.y].astype(F32)
        self.out[...] = total + self.rz[last - 1].astype(F32)

    def drain(self):
        self.core().wait_send()
        for number in range(len(self.halves)):
            self.exchange(number, True).wait_send()
            self.exchange(number, False).wait_send()
        wait_sent(self.place, self.rz, self.sems.at[6])


def iota(shape, dim):
    return lax.broadcasted_iota(jnp.int32, shape, dim)


def dot(left, right):
    return lax.dot_general(left, right, (((1,), (0,)), ((), ())), preferred_element_type=F32)


def dot_nt(left, right):
    return lax.dot_general(left, right, (((1,), (1,)), ((), ())), preferred_element_type=F32)


def dot_tn(left, right):
    return lax.dot_general(left, right, (((0,), (0,)), ((), ())), preferred_element_type=F32)


def shift_of(size):
    assert size & (size - 1) == 0
    return size.bit_length() - 1


BIASES = ("query", "value", "output", "down", "up")
SCALARS = len(BIASES)


def spread_bias(gathered, name, per, total):
    rows = gathered.shape[0]
    pick = iota((LANES, total), 0) == (iota((LANES, total), 1) & (per - 1))
    spread = dot(gathered.astype(BF16), pick.astype(BF16))
    owner = jnp.right_shift(iota((rows, total), 1), shift_of(per)) * 8 + BIASES.index(name)
    return jnp.sum(jnp.where(iota((rows, total), 0) == owner, spread, 0.0), axis=0, keepdims=True)


def fold_bias(row, rows, name, per):
    total = row.shape[1]
    owner = jnp.right_shift(iota((rows, total), 1), shift_of(per)) * 8 + BIASES.index(name)
    chosen = jnp.where(iota((rows, total), 0) == owner, row, 0.0)
    put = iota((total, LANES), 1) == (iota((total, LANES), 0) & (per - 1))
    return lax.dot_general(
        chosen,
        put.astype(F32),
        (((1,), (0,)), ((), ())),
        precision=lax.Precision.HIGHEST,
        preferred_element_type=F32,
    )


def layer_kernel(
    blocks,
    parts,
    window,
    docs,
    x_ref,
    seg_ref,
    win_ref,
    wo_ref,
    wup_ref,
    wdown_ref,
    bias_refs,
    alphas_ref,
    grad_ref,
    out_ref,
    gx_ref,
    r_win,
    r_out,
    r_up,
    r_down,
    r_aux,
    gathered,
    gather_sems,
    trees,
    exchange_sems,
    halo_sems,
    segs,
    tile,
    aux_ref,
    qs,
    ks,
    qt_ref,
    kv_ref,
    kvt,
    starts_ref,
    ot_ref,
    of_ref,
    lse_ref,
    mixed_t,
    dos,
    doct_ref,
    act_s,
    slope_s,
    gpre_s,
    gres_ref,
    q_rows_s,
    d_rows_s,
    delta_ref,
    dq_s,
    grad_s,
    dqt_ref,
    dkv_sum,
    dq_in,
    dkv_in,
    halo_out,
    halo_in,
    gp,
    win_s,
    r_win_s,
    partials,
):
    place = Place(blocks)
    depth, devices = place.depth, 4 * blocks
    gwin, gwo, gwup, gwdown, gaux = gathered
    p_win, p_out, p_up, p_down, p_aux = partials
    width, hidden = gwin.shape[-1] // 3, gwup.shape[-1]
    per, per_up = width // devices, hidden // devices
    span, pairs_of_chunks, reach = window + GROUP, GROUP // 2, window // 2
    free = pairs_of_chunks - reach

    def loop(call, low=1, high=GROUP):
        def step(number, carry):
            call(number)
            return carry

        lax.fori_loop(low, high, step, 0)

    def exchange(src, dst, sems, each=False):
        def copy(offset, come=False):
            landing = place.other_slot(-offset) if come else place.slot
            target = place.other_slot(offset)
            return remote(
                src(target),
                dst(landing),
                sems.at[0],
                sems.at[offset if each else 1],
                place.member(target),
            )

        return copy

    def entry(ref, base=0):
        return lambda index: ref.at[base + index]

    seg_sems, k_sems, q_sems, o_sems, d_sems, dq_sems, dkv_sems = exchange_sems
    seg_copy = exchange(lambda target: tile, entry(segs, window), seg_sems)
    k_copy = exchange(entry(ks), entry(kv_ref, window), k_sems, True)
    q_copy = exchange(entry(qs), entry(qt_ref), q_sems)
    o_copy = exchange(entry(ot_ref), entry(mixed_t), o_sems)
    d_copy = exchange(entry(dos), entry(doct_ref), d_sems, True)
    dq_copy = exchange(entry(dqt_ref), entry(dq_in), dq_sems)
    dkv_copy = exchange(entry(dkv_sum), entry(dkv_in), dkv_sems)
    seg_hs, seg_hr, kv_hs, kv_hr, back_hs, back_hr = halo_sems

    def all_here(ref, sems):
        wait_received(place, ref.at[pl.ds(0, GROUP - 1)], sems.at[1])

    def all_sent(ref, sems):
        wait_sent(place, ref.at[pl.ds(0, GROUP - 1)], sems.at[0])

    def send_to(copy, target):
        offset = lax.rem(target - place.slot + GROUP, GROUP)

        @pl.when(offset != 0)
        def _():
            copy(offset).start()

    def await_from(copy, source):
        offset = lax.rem(place.slot - source + GROUP, GROUP)

        @pl.when(offset != 0)
        def _():
            copy(offset, True).wait_recv()

    greet(place, parts, True)

    row = iota((16, LANES), 0)
    numbers = seg_ref[...].astype(F32)
    tile[...] = jnp.where(row == 0, numbers[0:1], numbers[1:2]).astype(BF16)
    segs[window + place.slot] = tile[...]
    for source, target in columns_between(win_ref.shape[-1] // 3):
        win_s[:, target : target + LANES] = win_ref[:, source : source + LANES]
    aux_ref[...] = jnp.zeros_like(aux_ref)
    for index, ref in enumerate(bias_refs):
        aux_ref[index : index + 1, 0 : ref.shape[-1]] = ref[...].astype(F32).reshape(1, ref.shape[-1])
    if window:

        @pl.when(place.part == 0)
        def _():
            kv_ref[pl.ds(0, window)] = jnp.zeros((window, LANES, LANES), BF16)

    plan = (
        (aux_ref, gaux, None),
        (win_s, gwin, (0, width)),
        (win_s, gwin, (width, width)),
        (win_s, gwin, (2 * width, width)),
    )
    g_aux, g_even, g_odd, g_q = [
        Gather(place, src, dst, sems, cols)
        for (src, dst, cols), sems in zip(plan, gather_sems[:4])
    ]
    plan = (
        (wo_ref, gwo, None),
        (wup_ref, gwup, (0, hidden // 2)),
        (wup_ref, gwup, (hidden // 2, hidden // 2)),
        (wdown_ref, gwdown, (0, width // 2)),
        (wdown_ref, gwdown, (width // 2, width // 2)),
    )
    rest = [
        TreeGather(place, src, dst, sems, cols)
        for (src, dst, cols), sems in zip(plan, gather_sems[4:])
    ]
    g_wo, g_up0, g_up1, g_down0, g_down1 = rest
    g_even.start_line()
    g_aux.start_line()
    g_odd.start_line()
    g_q.start_line()
    loop(lambda offset: seg_copy(offset).start())
    g_wo.start_line()
    g_up0.start_line()
    g_up1.start_line()
    g_even.start_columns()
    g_aux.start_columns()
    g_odd.start_columns()
    g_q.start_columns()
    g_down0.start_line()
    g_down1.start_line()
    wait_received(place, segs.at[pl.ds(0, GROUP - 1)], seg_sems.at[1])

    def seg_halo(part):
        return remote(
            segs.at[pl.ds(GROUP, window)],
            segs.at[pl.ds(0, window)],
            seg_hs.at[0],
            seg_hr.at[0],
            place.member(place.slot, part),
        )

    if parts > 1:

        @pl.when(place.part < parts - 1)
        def _():
            seg_halo(place.part + 1).start()

    g_even.start_hands()
    g_wo.start_step()
    g_up0.start_step()
    g_up1.start_step()
    g_aux.start_hands()
    g_odd.start_hands()
    g_aux.finish()
    g_even.finish()

    aux = gaux[...].reshape(devices * 8, LANES)
    bias_q = spread_bias(aux, "query", per, width)
    bias_v = spread_bias(aux, "value", per, width)
    tokens = x_ref[...].reshape(2 * LANES, width)
    low_lane = iota((LANES, LANES), 1) < HD
    wide = 2 * LANES

    def column(at):
        return dot(tokens, gwin[:, :, :, :, :, pl.ds(at, wide)].reshape(width, wide))

    def corners():
        for s in range(2):
            for u in range(2):
                at = (slice(s * LANES, (s + 1) * LANES), slice(u * LANES, (u + 1) * LANES))
                yield s, u, at

    def project_pairs(odd):
        k = column(column_of("k", odd, width)).astype(BF16).astype(F32)
        v = column(column_of("v", odd, width))
        for s, u, at in corners():
            pair = odd + 2 * u
            head = s * HEADS + 2 * pair
            k_at = k[at]
            v_at = (v[at] + bias_v[:, pair * LANES : (pair + 1) * LANES]).astype(BF16).astype(F32)
            ks[head] = jnp.where(low_lane, k_at, pltpu.roll(v_at, HD, 1)).astype(BF16)
            ks[head + 1] = jnp.where(low_lane, pltpu.roll(k_at, HD, 1), v_at).astype(BF16)

        def start(offset):
            head = lax.rem(place.other_slot(offset), HEADS)

            @pl.when(lax.rem(lax.div(head, 2), 2) == odd)
            def _():
                k_copy(offset).start()

        loop(start)

    project_pairs(0)
    g_q.start_hands()
    g_wo.start_first()
    g_up0.start_first()
    g_up1.start_first()
    g_down0.start_step()
    g_down1.start_step()
    g_odd.finish()
    project_pairs(1)
    kv_ref[window + place.slot] = ks[place.slot]
    g_q.finish()
    for t in range(width // wide):
        q = column(column_of("q", 2 * t, width)) + bias_q[:, t * wide : (t + 1) * wide]
        q = q.astype(BF16).astype(F32) * 0.125
        for s, u, at in corners():
            turned = q[at].T.astype(BF16)
            head = s * HEADS + 4 * t + 2 * u
            qs[head] = turned[:HD]
            qs[head + 1] = turned[HD:]
    loop(lambda offset: q_copy(offset).start())
    qt_ref[place.slot] = qs[place.slot]
    g_wo.start_second()
    g_up0.start_second()
    g_up1.start_second()

    if parts > 1:

        @pl.when(place.part < parts - 1)
        def _():
            seg_halo(place.part + 1).wait_send()

        @pl.when(place.part > 0)
        def _():
            seg_halo(place.part - 1).wait_recv()

    sequence = lax.div(place.slot, HEADS)
    chosen = jnp.where(iota((span, 16, LANES), 1) == sequence, segs[...].astype(F32), 0.0)
    seen = jnp.sum(chosen, axis=1)
    outside = (iota((span, LANES), 0) < window) & (place.part == 0)
    seen = jnp.where(outside, -1.0, seen)
    own = seen[window:]
    start = jnp.zeros((GROUP, LANES), F32)
    for number in range(docs):
        count = jnp.sum(jnp.where(seen == number - 1, 1.0, 0.0), axis=0, keepdims=True)
        count = jnp.sum(count, axis=1, keepdims=True)
        start = start + jnp.where(own >= number, count, 0.0)
    starts_ref[...] = start.astype(jnp.int32)
    g_down0.start_first()
    g_down1.start_first()

    def kv_halo(number, part):
        return remote(
            kv_ref.at[GROUP + number],
            kv_ref.at[number],
            kv_hs.at[number],
            kv_hr.at[number],
            place.member(place.slot, part),
        )

    def arrived(source):
        kvt[window + source] = kv_ref[window + source].T
        if parts > 1:

            @pl.when((place.part < parts - 1) & (source >= GROUP - window))
            def _():
                kv_halo(source - (GROUP - window), place.part + 1).start()

    arrived(place.slot)

    def kv_wait(offset):
        k_copy(offset, True).wait_recv()
        arrived(place.other_slot(-offset))

    loop(kv_wait, 1, GROUP // 2)
    loop(kv_wait, GROUP // 2, GROUP)
    all_here(qt_ref, q_sems)
    g_wo.start_hands()
    g_up0.start_hands()
    g_up1.start_hands()

    many = window + 2
    older = window * LANES

    def q_rows_of(ref, m):
        return jnp.concatenate([ref[pl.ds(2 * m, 1)], ref[pl.ds(2 * m + 1, 1)]], axis=1)

    def turned_window(m):
        return jnp.concatenate([kvt[2 * m + i] for i in range(many)], axis=1)

    def masked(scores, start, q_place, block, base):
        k_place = base + block * BLOCK + iota((BLOCK, BLOCK), 0)
        visible = k_place >= start
        if block == reach:
            visible = visible & (k_place <= q_place)
        return jnp.where(visible, scores, NEG)

    blank = jnp.zeros((HD, BLOCK), BF16)

    def attend(step, carry):
        @pl.when(step == 1)
        def _():
            g_down0.start_second()

        @pl.when(step == 3)
        def _():
            g_down1.start_second()

        @pl.when(step == 6)
        def _():
            g_down0.start_hands()

        if parts > 1:

            @pl.when((step == free) & (place.part > 0))
            def _():
                loop(lambda number: kv_halo(number, place.part - 1).wait_recv(), 0, window)

        @pl.when(step == free)
        def _():
            def turn(number):
                kvt[number] = kv_ref[number].T

            loop(turn, 0, window)

        turnover = place.slot
        late = lax.rem(step - free + GROUP + turnover, reach)
        if free:
            m = jnp.where(step < free, reach + lax.rem(step + turnover, free), late)
        else:
            m = late
        q_wide = jnp.concatenate([two(qt_ref, 2 * m), blank], axis=0)
        start = q_rows_of(starts_ref, m)
        base = m * BLOCK
        q_place = base + older + iota((1, BLOCK), 1)
        scores = [
            masked(
                dot(kv_ref[pl.ds(2 * (m + block), 2)].reshape(BLOCK, LANES), q_wide),
                start,
                q_place,
                block,
                base,
            )
            for block in range(reach + 1)
        ]
        peak = functools.reduce(jnp.maximum, scores)
        peak = jnp.max(peak, axis=0, keepdims=True)
        weights = [jnp.exp(score - peak) for score in scores]
        total = functools.reduce(jnp.add, weights)
        total = jnp.sum(total, axis=0, keepdims=True)
        weights = jnp.concatenate([weight.astype(BF16) for weight in weights], axis=0)
        out = dot(turned_window(m)[HD:], weights) / total
        lse = peak + jnp.log(total)
        for side in range(2):
            lanes = slice(side * LANES, (side + 1) * LANES)
            of_ref[2 * m + side] = out[:, lanes]
            ot_ref[2 * m + side] = out[:, lanes].astype(BF16)
            lse_ref[pl.ds(2 * m + side, 1)] = lse[:, lanes]
            send_to(o_copy, 2 * m + side)
        return carry

    lax.fori_loop(0, pairs_of_chunks, attend, 0)
    mixed_t[place.slot] = ot_ref[place.slot]

    a0, a1 = alphas_ref[0], alphas_ref[1]
    bias_out = spread_bias(aux, "output", per, width)
    bias_down = spread_bias(aux, "down", per, width)
    bias_up = spread_bias(aux, "up", per_up, hidden)
    rows = 2 * LANES
    wide_tokens = tokens.astype(F32)
    grads = grad_ref[...].reshape(rows, width).astype(F32)
    grad_ffn = (a1 * grads).astype(BF16)
    g_down1.start_hands()
    g_wo.finish()
    full_out = gwo[...].reshape(width, width)

    all_here(mixed_t, o_sems)
    mixed_turned = mixed_t[...].reshape(2, width, LANES)
    mixed = jnp.concatenate([mixed_turned[0].T, mixed_turned[1].T], axis=0)
    branch = dot(mixed, full_out) + bias_out
    attn_term = a0 * branch
    residual = wide_tokens + attn_term
    hidden_in = residual.astype(BF16)

    ffn = jnp.zeros((rows, width), F32) + bias_down
    grad_res = grads
    tile_up = 512
    g_up0.finish()
    g_up1.finish()
    whole_up = gwup.reshape(width, hidden)
    whole_down = gwdown.reshape(hidden, width)
    for t in range(hidden // tile_up):
        cols = pl.ds(t * tile_up, tile_up)
        pre = dot(hidden_in, whole_up[:, cols]) + bias_up[:, t * tile_up : (t + 1) * tile_up]
        phi = 0.5 * (1.0 + lax.erf(pre * (1.0 / math.sqrt(2.0))))
        act_s[:, cols] = (pre * phi).astype(BF16)
        slope = phi + pre * jnp.exp(-0.5 * pre * pre) * (1.0 / math.sqrt(2.0 * math.pi))
        slope_s[:, cols] = slope
    g_down0.finish()
    g_down1.finish()
    for t in range(hidden // tile_up):
        cols = pl.ds(t * tile_up, tile_up)
        w_down = whole_down[cols, :]
        gpre = (dot_nt(grad_ffn, w_down) * slope_s[:, cols]).astype(BF16)
        gpre_s[:, cols] = gpre
        grad_res = grad_res + dot_nt(gpre, whole_up[:, cols])
    gres_ref[...] = grad_res
    grad_branch = (a0 * grad_res).astype(BF16)
    grad_mixed = dot_nt(grad_branch, full_out).astype(BF16).astype(F32)
    for s in range(2):
        turned = grad_mixed[s * LANES : (s + 1) * LANES].T.astype(BF16)
        dos[pl.ds(s * HEADS, HEADS)] = turned.reshape(HEADS, HD, LANES)
    loop(lambda offset: d_copy(offset).start())
    doct_ref[place.slot] = dos[place.slot]

    sources = [
        (TreeReduce, p_out, r_out, None),
        (TreeReduce, p_up, r_up, (0, hidden // 2)),
        (TreeReduce, p_up, r_up, (hidden // 2, hidden // 2)),
        (TreeReduce, p_down, r_down, (0, width // 2)),
        (TreeReduce, p_down, r_down, (width // 2, width // 2)),
        (Reduce, p_win, r_win_s, (0, width)),
        (Reduce, p_win, r_win_s, (width, width)),
        (Reduce, p_win, r_win_s, (2 * width, width)),
        (Reduce, p_aux, r_aux, None),
    ]
    t_out, t_up0, t_up1, t_down0, t_down1, t_even, t_odd, t_q, t_aux = [
        kind(place, part, out, *scratch, cols)
        for (kind, part, out, cols), scratch in zip(sources, trees)
    ]
    lead = (2, 2, depth, 2)
    flat_down, flat_up = p_down.reshape(hidden, width), p_up.reshape(width, hidden)
    for half, tree in enumerate((t_down0, t_down1)):
        at = slice(half * width // 2, (half + 1) * width // 2)
        for t in range(hidden // tile_up):
            cols = pl.ds(t * tile_up, tile_up)
            flat_down[cols, at] = dot_tn(act_s[:, cols], grad_ffn[:, at]).astype(BF16)
        tree.start_core()
    hidden_turned = hidden_in.T

    def up_part(half, tree):
        for t in range(hidden // tile_up // 2):
            cols = pl.ds(half * hidden // 2 + t * tile_up, tile_up)
            flat_up[:, cols] = dot(hidden_turned, gpre_s[:, cols]).astype(BF16)
        tree.start_core()

    up_part(0, t_up0)
    t_down0.start_second()
    up_part(1, t_up1)
    t_down1.start_second()
    p_out.reshape(width, width)[...] = dot(
        jnp.concatenate([mixed_turned[0], mixed_turned[1]], axis=1), grad_branch
    ).astype(BF16)
    t_out.start_core()
    t_up0.start_second()

    for t in range(hidden // tile_up):
        cols = pl.ds(t * tile_up, tile_up)
        ffn = ffn + dot(act_s[:, cols], whole_down[cols, :])
    ffn_term = a1 * ffn
    stream = residual + ffn_term
    out_ref[...] = stream.astype(BF16).reshape(2, LANES, width)

    def whole(values):
        return jnp.sum(jnp.sum(values, axis=0, keepdims=True), axis=1, keepdims=True)

    sums = (
        whole(stream * stream),
        whole(attn_term * attn_term),
        whole(ffn_term * ffn_term),
        whole(grad_res * branch),
        whole(grads * ffn),
    )
    lane = iota((devices * 8, LANES), 1)
    scalars = jnp.zeros((devices * 8, LANES), F32)
    for number, value in enumerate(sums):
        scalars = scalars + jnp.where(lane == number, value, 0.0)
    up_row = jnp.sum(gpre_s[...].astype(F32), axis=0, keepdims=True)
    down_row = jnp.sum(grad_ffn.astype(F32), axis=0, keepdims=True)
    out_row = jnp.sum(grad_branch.astype(F32), axis=0, keepdims=True)
    folded = (
        fold_bias(out_row, devices * 8, "output", per)
        + fold_bias(down_row, devices * 8, "down", per)
        + fold_bias(up_row, devices * 8, "up", per_up)
        + jnp.where((iota((devices * 8, LANES), 0) & 7) == SCALARS, scalars, 0.0)
    )
    p_aux[...] = folded.reshape(*lead, 8, LANES)

    t_up1.start_second()
    early = (t_down0, t_down1, t_up0, t_up1, t_out)
    low_block = iota((BLOCK, LANES), 1) < HD

    def clear(m):
        dq_s[m] = jnp.zeros((HD, BLOCK), F32)

    loop(clear, 0, pairs_of_chunks)

    def back_halo(u, part):
        pair = pl.ds(2 * u, 2)
        return remote(
            halo_out.at[pair],
            halo_in.at[pair],
            back_hs.at[u],
            back_hr.at[u],
            place.member(place.slot, part),
        )

    def ready(m):
        await_from(d_copy, 2 * m)
        await_from(d_copy, 2 * m + 1)
        qt, dt = two(qt_ref, 2 * m), two(doct_ref, 2 * m)
        both = jnp.concatenate([qt, dt], axis=0).astype(F32).T
        here = pl.ds(2 * m, 2)
        q_rows_s[here] = jnp.where(low_block, both, 0.0).astype(BF16).reshape(2, LANES, LANES)
        d_rows_s[here] = jnp.where(low_block, 0.0, both).astype(BF16).reshape(2, LANES, LANES)
        delta = jnp.sum(dt.astype(F32) * two(of_ref, 2 * m), axis=0, keepdims=True)
        delta_ref[pl.ds(2 * m, 1)] = delta[:, :LANES]
        delta_ref[pl.ds(2 * m + 1, 1)] = delta[:, LANES:]

    def key_block(u, low, count):
        kv = kv_ref[pl.ds(2 * u, 2)].reshape(BLOCK, LANES)
        keys_turned = two(kvt, 2 * u)[:HD]
        k_place = u * BLOCK + iota((BLOCK, BLOCK), 0)
        grad = jnp.zeros((BLOCK, LANES), F32)
        for number in range(count):
            m = low + number
            here = pl.ds(2 * m, 2)
            q_wide = jnp.concatenate([two(qt_ref, 2 * m), blank], axis=0)
            d_wide = jnp.concatenate([blank, two(doct_ref, 2 * m)], axis=0)
            visible = k_place >= q_rows_of(starts_ref, m)
            if number == 0:
                visible = visible & (k_place <= m * BLOCK + older + iota((1, BLOCK), 1))
            scores = jnp.where(visible, dot(kv, q_wide), NEG)
            probs = jnp.exp(scores - q_rows_of(lse_ref, m))
            grad_scores = (probs * (dot(kv, d_wide) - q_rows_of(delta_ref, m))).astype(BF16)
            grad = grad + dot(grad_scores, q_rows_s[here].reshape(BLOCK, LANES))
            grad = grad + dot(probs.astype(BF16), d_rows_s[here].reshape(BLOCK, LANES))
            dq_s[m] += dot(keys_turned, grad_scores)
        grad_s[...] = grad

    def settle(u):
        pair = u - reach
        if parts > 1:
            late = pair - (pairs_of_chunks - reach)

            @pl.when((late >= 0) & (place.part < parts - 1))
            def _():
                back_halo(late, place.part + 1).wait_recv()
                grad_s[...] += halo_in[pl.ds(2 * late, 2)].reshape(BLOCK, LANES).astype(F32)

        dkv_sum[pl.ds(2 * pair, 2)] = grad_s[...].astype(BF16).reshape(2, LANES, LANES)
        dq = dq_s[pair] * 0.125
        for side in range(2):
            send_to(dkv_copy, 2 * pair + side)
            dqt_ref[2 * pair + side] = dq[:, side * LANES : (side + 1) * LANES].astype(BF16)
            send_to(dq_copy, 2 * pair + side)

    def attend_back(u, carry):
        @pl.when(u == 0)
        def _():
            t_out.start_second()

        @pl.when(u == 5)
        def _():
            t_down0.start_first()

        @pl.when(u == 7)
        def _():
            t_down1.start_first()

        @pl.when(u < pairs_of_chunks)
        def _():
            ready(u)

        low = jnp.maximum(u - reach, 0)
        count = jnp.minimum(u, pairs_of_chunks - 1) - low + 1
        needed = (u >= reach) | (place.part > 0)
        for number in range(1, reach + 2):

            @pl.when(needed & (count == number))
            def _():
                key_block(u, low, number)

        if parts > 1:

            @pl.when((u < reach) & (place.part > 0))
            def _():
                halo_out[pl.ds(2 * u, 2)] = grad_s[...].astype(BF16).reshape(2, LANES, LANES)
                back_halo(u, place.part - 1).start()

        @pl.when(u >= reach)
        def _():
            settle(u)

        return carry

    lax.fori_loop(0, reach + pairs_of_chunks, attend_back, 0)
    dq_in[place.slot] = dqt_ref[place.slot]
    t_up0.start_first()
    t_up1.start_first()
    t_out.start_first()
    dkv_in[place.slot] = dkv_sum[place.slot]
    t_down0.start_line()
    t_down1.start_line()

    def weight_part(number):
        part = dot(tokens_turned, gp[:, number * width : (number + 1) * width]).astype(BF16)
        p_win[:, :, :, :, :, number * width : (number + 1) * width] = part.reshape(
            *lead, width // devices, width
        )

    def token_part(number):
        cols = slice(number * width, (number + 1) * width)
        return dot_nt(gp[:, cols], full_in[:, cols])

    tokens_turned = tokens.T
    full_in = gwin.reshape(width, 3 * width)
    all_here(dq_in, dq_sems)
    for s in range(2):
        turned = dq_in[pl.ds(s * HEADS, HEADS)].reshape(width, LANES).astype(F32)
        gp[s * LANES : (s + 1) * LANES, 2 * width :] = turned.T.astype(BF16)
    weight_part(2)
    t_q.start_core()
    query_row = jnp.sum(gp[:, 2 * width :].astype(F32), axis=0, keepdims=True)
    gx = gres_ref[...] + token_part(2)
    t_up0.start_line()
    t_up1.start_line()
    t_out.start_line()
    t_q.start_columns()

    all_here(dkv_in, dkv_sems)
    for number in range(2):
        for s in range(2):
            at_rows = slice(s * LANES, (s + 1) * LANES)
            for pair in range(number, HEADS // 2, 2):
                even = dkv_in[s * HEADS + 2 * pair].astype(F32)
                odd = dkv_in[s * HEADS + 2 * pair + 1].astype(F32)
                keys = jnp.where(low_lane, even, pltpu.roll(odd, HD, 1))
                values = jnp.where(low_lane, pltpu.roll(even, HD, 1), odd)
                at = column_of("k", pair, width)
                gp[at_rows, at : at + LANES] = keys.astype(BF16)
                at = column_of("v", pair, width)
                gp[at_rows, at : at + LANES] = values.astype(BF16)
        weight_part(number)
        (t_even, t_odd)[number].start_core()
    value_rows = []
    for pair in range(HEADS // 2):
        at = column_of("v", pair, width)
        value_rows.append(jnp.sum(gp[:, at : at + LANES].astype(F32), axis=0, keepdims=True))
    folded = fold_bias(query_row, devices * 8, "query", per) + fold_bias(
        jnp.concatenate(value_rows, axis=1), devices * 8, "value", per
    )
    p_aux[...] += folded.reshape(*lead, 8, LANES)
    t_aux.start_core()
    t_even.start_columns()
    t_q.start_line()
    t_odd.start_columns()
    t_aux.start_columns()
    t_down0.start_step()
    t_down1.start_step()
    t_up0.start_step()
    t_up1.start_step()
    t_out.start_step()
    gx = gx + token_part(0) + token_part(1)
    gx_ref[...] = gx.astype(BF16).reshape(2, LANES, width)
    t_even.start_line()
    t_aux.start_line()
    t_odd.start_line()
    for tree in early + (t_q, t_even, t_aux, t_odd):
        tree.finish()
    for source, target in columns_between(width):
        r_win[:, source : source + LANES] = r_win_s[:, target : target + LANES]

    all_sent(segs, seg_sems)
    all_sent(ks, k_sems)
    all_sent(qs, q_sems)
    all_sent(ot_ref, o_sems)
    all_sent(dos, d_sems)
    all_sent(dqt_ref, dq_sems)
    all_sent(dkv_sum, dkv_sems)
    if parts > 1:

        @pl.when(place.part < parts - 1)
        def _():
            loop(lambda number: kv_halo(number, place.part + 1).wait_send(), 0, window)

        @pl.when(place.part > 0)
        def _():
            loop(lambda u: back_halo(u, place.part - 1).wait_send(), 0, reach)

    for gather in (g_aux, g_even, g_odd, g_q, *rest):
        gather.drain()
    for tree in early + (t_q, t_even, t_odd, t_aux):
        tree.drain()


def two(ref, index):
    return jnp.concatenate([ref[index], ref[index + 1]], axis=1)


def hand_out_kernel(
    tokens_all, out_ref, gx_ref, win_ref, wo_ref, wup_ref, wdown_ref, sums_ref, *results
):
    for src, dst in zip((out_ref, gx_ref, win_ref, wo_ref, wup_ref, wdown_ref), results[:6]):
        dst[...] = src[...]
    named = dict(zip(("query", "value", "output", "up", "down"), results[6:11]))
    for name, ref in named.items():
        ref[...] = sums_ref[BIASES.index(name), 0 : ref.shape[0]]
    results[11][...] = sums_ref[SCALARS, 3:5]
    results[12][...] = jnp.sqrt(sums_ref[SCALARS, 0:3] * (1.0 / tokens_all))


def call(kernel, out_shape, in_specs, out_specs, scratch, collective=None):
    return pl.pallas_call(
        kernel,
        out_shape=out_shape,
        in_specs=in_specs,
        out_specs=out_specs,
        scratch_shapes=scratch,
        compiler_params=pltpu.CompilerParams(
            collective_id=collective,
            has_side_effects=collective is not None,
            vmem_limit_bytes=VMEM_BYTES,
        ),
    )


def local(
    layer_input,
    segments,
    input_weight,
    output_weight,
    up_weight,
    down_weight,
    query_bias,
    value_bias,
    output_bias,
    up_bias,
    down_bias,
    alphas,
    out_grad,
):
    heads, blocks = lax.axis_size("head"), lax.axis_size("blk")
    depth, devices = blocks // 2, heads * blocks
    seqs, rows, width = layer_input.shape
    hidden = up_weight.shape[1]
    seq_len = rows * devices
    assert heads == 4 and seqs * HEADS == GROUP and rows == LANES
    longest = 16 * math.isqrt(seq_len)
    window, parts = longest // rows, devices // GROUP
    docs = 2 * seq_len // longest
    assert window <= GROUP and window % 2 == 0
    span = window + GROUP

    def shape(*dims, dtype=BF16):
        return jax.ShapeDtypeStruct(dims, dtype)

    vmem, smem = pl.BlockSpec(memory_space=VMEM), pl.BlockSpec(memory_space=pltpu.SMEM)
    dma = pltpu.SemaphoreType.DMA
    lead = (2, 2, depth, 2)
    in_rows, up_rows = input_weight.shape[0], down_weight.shape[0]
    tree_parts = ((in_rows, width),) + ((in_rows, hidden // 2),) * 2 + ((up_rows, width // 2),) * 2
    tokens = seqs * rows
    results = (
        shape(seqs, rows, width),
        shape(seqs, rows, width),
        shape(in_rows, 3 * width, dtype=F32),
        shape(in_rows, width, dtype=F32),
        shape(in_rows, hidden, dtype=F32),
        shape(up_rows, width, dtype=F32),
    )
    carried = call(
        functools.partial(layer_kernel, blocks, parts, window, docs),
        results + (shape(8, LANES, dtype=F32),),
        [vmem] * 6 + [(vmem,) * 5] + [smem, vmem],
        (vmem,) * 7,
        [
            [
                VMEM((*lead, in_rows, 3 * width), BF16),
                VMEM((*lead, in_rows, width), BF16),
                VMEM((*lead, in_rows, hidden), BF16),
                VMEM((*lead, up_rows, width), BF16),
                VMEM((*lead, 8, LANES), F32),
            ],
            [dma((Gather.COUNT,))] * 4 + [dma((TreeGather.COUNT + depth - 1,))] * 5,
            [TreeReduce.scratch(depth, *sizes, BF16) for sizes in tree_parts]
            + [Reduce.scratch(depth, in_rows, width, BF16)] * 3
            + [Reduce.scratch(depth, 8, LANES, F32)],
            [dma((2,)), dma((GROUP,)), dma((2,)), dma((2,)), dma((GROUP,)), dma((2,)), dma((2,))],
            [dma((1,)), dma((1,)), dma((window,)), dma((window,)), dma((window // 2,)), dma((window // 2,))],
            VMEM((span, 16, LANES), BF16),
            VMEM((16, LANES), BF16),
            VMEM((8, LANES), F32),
            VMEM((GROUP, HD, LANES), BF16),
            VMEM((GROUP, LANES, LANES), BF16),
            VMEM((GROUP, HD, LANES), BF16),
            VMEM((span, LANES, LANES), BF16),
            VMEM((span, LANES, LANES), BF16),
            VMEM((GROUP, LANES), jnp.int32),
            VMEM((GROUP, HD, LANES), BF16),
            VMEM((GROUP, HD, LANES), F32),
            VMEM((GROUP, LANES), F32),
            VMEM((GROUP, HD, LANES), BF16),
            VMEM((GROUP, HD, LANES), BF16),
            VMEM((GROUP, HD, LANES), BF16),
            VMEM((tokens, hidden), BF16),
            VMEM((tokens, hidden), F32),
            VMEM((tokens, hidden), BF16),
            VMEM((tokens, width), F32),
            VMEM((GROUP, LANES, LANES), BF16),
            VMEM((GROUP, LANES, LANES), BF16),
            VMEM((GROUP, LANES), F32),
            VMEM((GROUP // 2, HD, BLOCK), F32),
            VMEM((BLOCK, LANES), F32),
            VMEM((GROUP, HD, LANES), BF16),
            VMEM((GROUP, LANES, LANES), BF16),
            VMEM((GROUP, HD, LANES), BF16),
            VMEM((GROUP, LANES, LANES), BF16),
            VMEM((window, LANES, LANES), BF16),
            VMEM((window, LANES, LANES), BF16),
            VMEM((tokens, 3 * width), BF16),
            VMEM((in_rows, 3 * width), BF16),
            VMEM((in_rows, 3 * width), F32),
            [
                VMEM((*lead, in_rows, 3 * width), BF16),
                VMEM((*lead, in_rows, width), BF16),
                VMEM((*lead, in_rows, hidden), BF16),
                VMEM((*lead, up_rows, width), BF16),
                VMEM((*lead, 8, LANES), F32),
            ],
        ],
        collective=0,
    )(
        layer_input,
        segments,
        input_weight,
        output_weight,
        up_weight,
        down_weight,
        (query_bias, value_bias, output_bias, down_bias, up_bias),
        alphas,
        out_grad,
    )
    per, per_up = width // devices, hidden // devices
    return call(
        functools.partial(hand_out_kernel, seqs * seq_len * width),
        results
        + tuple(
            shape(size, dtype=F32) for size in (per, per, per, per_up, per, 2, 3)
        ),
        [vmem] * 7,
        (vmem,) * 13,
        [],
    )(*carried)


def solution(mesh):
    tokens = P(None, ("head", "blk"), None)
    rows, flat = P(("head", "blk"), None), P(("head", "blk"))
    return jax.shard_map(
        local,
        mesh=mesh,
        in_specs=(
            tokens,
            P(None, ("head", "blk")),
            rows,
            rows,
            rows,
            rows,
            flat,
            flat,
            flat,
            flat,
            flat,
            P(),
            tokens,
        ),
        out_specs=(
            tokens,
            tokens,
            rows,
            rows,
            rows,
            rows,
            flat,
            flat,
            flat,
            flat,
            flat,
            P(),
            P(),
        ),
        check_vma=False,
    )
```

```python
import functools
import math

import jax
import jax.numpy as jnp
from jax import lax
from jax.experimental import pallas as pl
from jax.experimental.pallas import tpu as pltpu
from jax.sharding import PartitionSpec as P

HEADS = 8
HD = 64
LANES = 128
GROUP = 16
BLOCK = 256
VMEM_BYTES = 60 * 1024 * 1024
F32 = jnp.float32
BF16 = jnp.bfloat16
VMEM = pltpu.VMEM
NEG = -1e30


class Place:
    def __init__(self, blocks):
        self.blocks = blocks
        self.depth = blocks // 2
        head = lax.axis_index("head")
        block = lax.axis_index("blk")
        self.x, self.core = lax.div(head, 2), lax.rem(head, 2)
        self.z, self.y = lax.div(block, 2), lax.rem(block, 2)
        flat = head * blocks + block
        self.part, self.slot = lax.div(flat, GROUP), lax.rem(flat, GROUP)

    def at(self, x=None, core=None, z=None, y=None):
        x = self.x if x is None else x
        core = self.core if core is None else core
        z = self.z if z is None else z
        y = self.y if y is None else y
        return (x * 2 + core, z * 2 + y)

    def deeper(self, offset):
        return lax.rem(self.z + offset + self.depth, self.depth)

    def bits(self):
        bit = self.depth // 2
        while bit:
            yield bit
            bit //= 2

    def flipped(self, bits):
        z = self.z
        for bit in self.bits():
            if bits & bit:
                z = z + bit - 2 * bit * lax.rem(lax.div(self.z, bit), 2)
        return z

    def member(self, slot, part=None):
        part = self.part if part is None else part
        flat = part * GROUP + slot
        return (lax.div(flat, self.blocks), lax.rem(flat, self.blocks))

    def crossed(self, code):
        slot = self.slot
        for bit in (1, 2, 4, 8):
            if code & bit:
                slot = slot + bit - 2 * bit * lax.rem(lax.div(self.slot, bit), 2)
        return slot

    def other_slot(self, offset):
        return lax.rem(self.slot + offset + GROUP, GROUP)


def remote(src, dst, send, recv, device):
    return pltpu.make_async_remote_copy(
        src_ref=src,
        dst_ref=dst,
        send_sem=send,
        recv_sem=recv,
        device_id=device,
        device_id_type=pl.DeviceIdType.MESH,
    )


def greet(place, parts, tree):
    barrier = pltpu.get_barrier_semaphore()

    def hello(device):
        pl.semaphore_signal(barrier, inc=1, device_id=device, device_id_type=pl.DeviceIdType.MESH)

    def group(offset, carry):
        hello(place.member(place.other_slot(offset)))
        return carry

    lax.fori_loop(1, GROUP, group, 0)
    total = GROUP - 1
    if tree:

        def line(offset, carry):
            hello(place.at(z=place.deeper(offset)))
            return carry

        lax.fori_loop(1, place.depth, line, 0)
        hello(place.at(x=1 - place.x))
        hello(place.at(y=1 - place.y))
        hello(place.at(x=1 - place.x, y=1 - place.y))
        hello(place.at(core=1 - place.core))
        total += place.depth + 3

    def range_of(offset, carry):
        part = lax.rem(place.part + offset, parts)
        hello(place.member(place.slot, part))
        hello(place.member(place.crossed(1), part))
        return carry

    lax.fori_loop(1, parts, range_of, 0)
    pl.semaphore_wait(barrier, total + 2 * (parts - 1))


def halves_of(columns):
    if columns < 2 * LANES:
        return ((0, columns, "yx"),)
    most = columns // 2
    return ((0, most, "yx"), (most, columns - most, "xy"))


def wait_received(place, dst, sem):
    remote(dst, dst, sem, sem, place.at(core=1 - place.core)).wait_recv()


def wait_sent(place, src, sem):
    remote(src, src, sem, sem, place.at(core=1 - place.core)).wait_send()


class Gather:
    COUNT = 9

    def __init__(self, place, src, dst, sems, cols=None):
        self.place, self.src, self.dst, self.sems = place, src, dst, sems
        start, width = cols or (0, dst.shape[-1])
        self.cols = pl.ds(start, width)

    def part(self, *index):
        return self.dst.at[index + (slice(None), self.cols)]

    def column(self, core, x, y):
        return self.part(x, core, slice(None), y)

    def others(self):
        place = self.place
        return ((1 - place.x, place.y), (place.x, 1 - place.y), (1 - place.x, 1 - place.y))

    def own(self):
        place = self.place
        mine = self.part(place.x, place.core, place.z, place.y)
        return pltpu.make_async_copy(self.src.at[:, self.cols], mine, self.sems.at[0])

    def start_line(self):
        place = self.place
        for offset in range(1, place.depth):
            remote(
                self.src.at[:, self.cols],
                self.part(place.x, place.core, place.z, place.y),
                self.sems.at[1],
                self.sems.at[2],
                place.at(z=place.deeper(offset)),
            ).start()
        self.own().start()

    def lines(self):
        return self.part(0, 0, pl.ds(0, self.place.depth - 1), 0)

    def hand(self, x, y):
        place = self.place
        column = self.column(place.core, x, y)
        remote(
            column, column, self.sems.at[7], self.sems.at[8], place.at(core=1 - place.core)
        ).start()

    def start_columns(self):
        place = self.place
        self.own().wait()
        wait_received(place, self.lines(), self.sems.at[2])
        mine = self.column(place.core, place.x, place.y)
        for number, (x, y) in enumerate(self.others()):
            remote(
                mine, mine, self.sems.at[3], self.sems.at[4 + number], place.at(x=x, y=y)
            ).start()
        self.hand(place.x, place.y)

    def start_hands(self):
        for number, (x, y) in enumerate(self.others()):
            wait_received(
                self.place, self.column(self.place.core, x, y), self.sems.at[4 + number]
            )
            self.hand(x, y)

    def finish(self):
        every = slice(None)
        region = self.part(every, 1 - self.place.core, every, every)
        wait_received(self.place, region, self.sems.at[8])

    def drain(self):
        place = self.place
        wait_sent(place, self.lines(), self.sems.at[1])
        every = slice(None)
        wait_sent(
            place, self.part(every, every, pl.ds(0, 3 * place.depth // 4), 0), self.sems.at[3]
        )
        wait_sent(place, self.part(every, 0, every, every), self.sems.at[7])


def halves_of(columns):
    if columns < 2 * LANES:
        return ((0, columns, "yx"),)
    most = columns // 2
    return ((0, most, "yx"), (most, columns - most, "xy"))


class TreeGather:
    COUNT = 7

    def __init__(self, place, src, dst, sems, cols=None):
        self.place, self.src, self.dst, self.sems = place, src, dst, sems
        self.start, self.width = cols or (0, dst.shape[-1])
        self.halves = halves_of(self.width)
        self.cols = pl.ds(self.start, self.width)

    def part(self, *index):
        return self.dst.at[index + (slice(None), self.cols)]

    def cut(self, half, *index):
        start, width, _ = half
        return self.dst.at[index + (slice(None), pl.ds(self.start + start, width))]

    def across(self, half, first):
        place = self.place
        if (half[2] == "yx") == first:
            return place.x, 1 - place.y
        return 1 - place.x, place.y

    def region(self, half, first, core, x, y):
        every = slice(None)
        if first:
            return self.cut(half, x, core, every, y)
        if half[2] == "yx":
            return self.cut(half, x, core, every, every)
        return self.cut(half, every, core, every, y)

    def own(self):
        place = self.place
        mine = self.part(place.x, place.core, place.z, place.y)
        return pltpu.make_async_copy(self.src.at[:, self.cols], mine, self.sems.at[0])

    def send_piece(self, bits, bit):
        place = self.place
        piece = self.part(place.x, place.core, place.flipped(bits), place.y)
        remote(
            piece if bits else self.src.at[:, self.cols],
            piece,
            self.sems.at[1],
            self.sems.at[6 + (bits | bit)],
            place.at(z=place.flipped(bit)),
        ).start()

    def await_piece(self, bits):
        place = self.place
        piece = self.part(place.x, place.core, place.flipped(bits), place.y)
        wait_received(place, piece, self.sems.at[6 + bits])

    def start_line(self):
        for bit in self.place.bits():
            self.send_piece(0, bit)
        self.own().start()

    def start_step(self):
        known = [0]
        for bit in self.place.bits():
            for bits in known[1:]:
                self.send_piece(bits, bit)
            known += [bits | bit for bits in known]
            if bit > 1:
                for bits in known[len(known) // 2 :]:
                    self.await_piece(bits)

    def lines(self):
        return self.part(0, 0, pl.ds(0, self.place.depth - 1), 0)

    def exchange(self, number, first):
        place, half = self.place, self.halves[number]
        x, y = self.across(half, first)
        mine = self.region(half, first, place.core, place.x, place.y)
        return remote(
            mine,
            mine,
            self.sems.at[3],
            self.sems.at[4 if first else 5],
            place.at(x=x, y=y),
        )

    def all_received(self, first):
        every, place = slice(None), self.place
        xs = 0 if first else every
        wait_received(place, self.part(xs, 0, every, 0), self.sems.at[4 if first else 5])

    def received(self, number, first):
        half = self.halves[number]
        x, y = self.across(half, first)
        return self.region(half, first, self.place.core, x, y)

    def hand(self, region):
        place = self.place
        remote(
            region, region, self.sems.at[6], self.sems.at[2], place.at(core=1 - place.core)
        ).start()

    def start_first(self):
        place = self.place
        self.own().wait()
        for bits in range(1, place.depth, 2):
            self.await_piece(bits)
        for number in range(len(self.halves)):
            self.exchange(number, True).start()
        self.hand(self.part(place.x, place.core, slice(None), place.y))

    def start_second(self):
        self.all_received(True)
        for number in range(len(self.halves)):
            region = self.received(number, True)
            self.exchange(number, False).start()
            self.hand(region)

    def start_hands(self):
        self.all_received(False)
        for number in range(len(self.halves)):
            self.hand(self.received(number, False))

    def finish(self):
        every = slice(None)
        region = self.part(every, 1 - self.place.core, every, every)
        wait_received(self.place, region, self.sems.at[2])

    def drain(self):
        every, depth = slice(None), self.place.depth
        wait_sent(
            self.place, self.part(every, every, pl.ds(0, 3 * depth // 4), 0), self.sems.at[3]
        )
        wait_sent(self.place, self.lines(), self.sems.at[1])
        wait_sent(self.place, self.part(every, 0, every, every), self.sems.at[6])


class Reduce:
    COUNT = 8

    def __init__(self, place, part, out, rc, total, rn, rz, sems, cols=None):
        self.place, self.part = place, part
        self.cols = pl.ds(*(cols or (0, part.shape[-1])))
        self.out = out.at[:, self.cols]
        self.rc, self.total, self.rn, self.rz, self.sems = rc, total, rn, rz, sems

    @staticmethod
    def scratch(depth, rows, cols, dtype):
        return [
            VMEM((2, depth, 2, rows, cols), dtype),
            VMEM((2, depth, 2, rows, cols), dtype),
            VMEM((3, depth, rows, cols), dtype),
            VMEM((depth - 1, rows, cols), dtype),
            pltpu.SemaphoreType.DMA((Reduce.COUNT,)),
        ]

    def others(self):
        place = self.place
        return ((1 - place.x, place.y), (place.x, 1 - place.y), (1 - place.x, 1 - place.y))

    def core(self):
        place = self.place
        return remote(
            self.part.at[:, 1 - place.core, :, :, :, self.cols],
            self.rc,
            self.sems.at[0],
            self.sems.at[1],
            place.at(core=1 - place.core),
        )

    def columns(self):
        place = self.place
        for number, (x, y) in enumerate(self.others()):
            yield remote(
                self.total.at[x, :, y],
                self.rn.at[number],
                self.sems.at[2],
                self.sems.at[3 + number],
                place.at(x=x, y=y),
            )

    def line(self, offset):
        place = self.place
        return remote(
            self.total.at[place.x, place.deeper(offset), place.y],
            self.rz.at[offset - 1],
            self.sems.at[6],
            self.sems.at[7],
            place.at(z=place.deeper(offset)),
        )

    def start_core(self):
        self.core().start()

    def add_core(self, x, z, y):
        place = self.place
        self.total[x, z, y] = self.part[x, place.core, z, y, :, self.cols] + self.rc[x, z, y]

    def start_columns(self):
        place = self.place
        self.core().wait_recv()
        for copy, (x, y) in zip(self.columns(), self.others()):

            def add(z, carry):
                self.add_core(x, z, y)
                return carry

            lax.fori_loop(0, place.depth, add, 0)
            copy.start()

        def add(z, carry):
            self.add_core(place.x, z, place.y)
            return carry

        lax.fori_loop(0, place.depth, add, 0)

    def start_line(self):
        place = self.place
        for copy in self.columns():
            copy.wait_recv()
        here = (place.x, slice(None), place.y)
        total = self.total[here].astype(F32)
        for number in range(3):
            total = total + self.rn[number].astype(F32)
        self.total[here] = total.astype(self.total.dtype)
        for offset in range(1, place.depth):
            self.line(offset).start()

    def finish(self):
        place = self.place
        wait_received(place, self.rz, self.sems.at[7])
        result = self.total[place.x, place.z, place.y].astype(F32)
        for offset in range(1, place.depth):
            result = result + self.rz[offset - 1].astype(F32)
        self.out[...] = result

    def drain(self):
        place = self.place
        self.core().wait_send()
        wait_sent(place, self.rn, self.sems.at[2])
        wait_sent(place, self.rz, self.sems.at[6])


class Total:
    COUNT = 8

    def __init__(self, place, mine, rc, rn, rz, sums, sems):
        self.place, self.mine, self.rc, self.rn, self.rz = place, mine, rc, rn, rz
        self.sums, self.sems = sums, sems

    @staticmethod
    def scratch(depth, rows):
        return [
            VMEM((rows, LANES), F32),
            VMEM((rows, LANES), F32),
            VMEM((3, rows, LANES), F32),
            VMEM((depth - 1, rows, LANES), F32),
            VMEM((2, rows, LANES), F32),
            pltpu.SemaphoreType.DMA((Total.COUNT,)),
        ]

    others = Reduce.others

    def core(self):
        return remote(
            self.mine,
            self.rc,
            self.sems.at[0],
            self.sems.at[1],
            self.place.at(core=1 - self.place.core),
        )

    def start_core(self):
        self.core().start()

    def start_columns(self):
        self.core().wait_recv()
        self.sums[0] = self.mine[...] + self.rc[...]
        for number, (x, y) in enumerate(self.others()):
            remote(
                self.sums.at[0],
                self.rn.at[number],
                self.sems.at[2],
                self.sems.at[3],
                self.place.at(x=x, y=y),
            ).start()

    def start_line(self):
        place = self.place
        wait_received(place, self.rn, self.sems.at[3])
        self.sums[1] = self.sums[0] + self.rn[0] + self.rn[1] + self.rn[2]
        for offset in range(1, place.depth):
            remote(
                self.sums.at[1],
                self.rz.at[offset - 1],
                self.sems.at[4],
                self.sems.at[5],
                place.at(z=place.deeper(offset)),
            ).start()

    def result(self):
        place = self.place
        wait_received(place, self.rz, self.sems.at[5])
        total = self.sums[1]
        for offset in range(1, place.depth):
            total = total + self.rz[offset - 1]
        return total

    def drain(self):
        self.core().wait_send()
        wait_sent(self.place, self.rn, self.sems.at[2])
        wait_sent(self.place, self.rz, self.sems.at[4])


class TreeReduce:
    COUNT = 6

    def __init__(self, place, part, out, rc, total, ra, rb, fa, fb, rz, sems, cols=None):
        self.place, self.part = place, part
        self.cols = pl.ds(*(cols or (0, part.shape[-1])))
        self.out = out.at[:, self.cols]
        self.rc, self.total, self.rz = rc, total, rz
        self.second, self.first = (ra, rb), (fa, fb)
        self.sems = sems
        self.halves = halves_of(total.shape[-1])

    @staticmethod
    def scratch(depth, rows, cols, dtype):
        wide, narrow = [half[1] for half in halves_of(cols)]
        return [
            VMEM((2, depth, 2, rows, cols), dtype),
            VMEM((2, depth, 2, rows, cols), dtype),
            VMEM((depth, 2, rows, wide), dtype),
            VMEM((2, depth, rows, narrow), dtype),
            VMEM((depth, rows, wide), dtype),
            VMEM((depth, rows, narrow), dtype),
            VMEM((depth - 1, rows, cols), dtype),
            pltpu.SemaphoreType.DMA((TreeReduce.COUNT + depth - 1,)),
        ]

    core, start_core, add_core = Reduce.core, Reduce.start_core, Reduce.add_core

    def cut(self, half, *index):
        start, width, _ = half
        return index + (slice(None), pl.ds(start, width))

    def exchange(self, number, second):
        place, every = self.place, slice(None)
        half = self.halves[number]
        over_x = (half[2] == "yx") == second
        device = place.at(x=1 - place.x) if over_x else place.at(y=1 - place.y)
        if second:
            index = (1 - place.x, every, every) if over_x else (every, every, 1 - place.y)
            landing = self.second[number]
        else:
            index = (1 - place.x, every, place.y) if over_x else (place.x, every, 1 - place.y)
            landing = self.first[number]
        return remote(
            self.total.at[self.cut(half, *index)],
            landing,
            self.sems.at[2],
            self.sems.at[3 if second else 4],
            device,
        )

    def start_second(self):
        self.core().wait_recv()

        def add(z, carry):
            for x in range(2):
                for y in range(2):
                    self.add_core(x, z, y)
            return carry

        lax.fori_loop(0, self.place.depth, add, 0)
        for number in range(len(self.halves)):
            self.exchange(number, True).start()

    def accumulate(self, index, value):
        self.total[index] = self.total[index] + value

    def start_first(self):
        place = self.place
        wait_received(place, self.rc.at[0], self.sems.at[3])
        for number, half in enumerate(self.halves):
            landed = self.second[number]

            def add(z, carry):
                for other in range(2):
                    if half[2] == "yx":
                        self.accumulate(self.cut(half, place.x, z, other), landed[z, other])
                    else:
                        self.accumulate(self.cut(half, other, z, place.y), landed[other, z])
                return carry

            lax.fori_loop(0, place.depth, add, 0)
            self.exchange(number, False).start()

    def start_line(self):
        place = self.place
        wait_received(place, self.rc.at[0, :, 0], self.sems.at[4])
        for number, half in enumerate(self.halves):
            landed = self.first[number]

            def add(z, carry):
                self.accumulate(self.cut(half, place.x, z, place.y), landed[z])
                return carry

            lax.fori_loop(0, place.depth, add, 0)
        self.send_over(1)

    def offsets(self, bit):
        return range(bit, self.place.depth, 2 * bit)

    def send_over(self, bit):
        place = self.place
        for bits in self.offsets(bit):
            remote(
                self.total.at[place.x, place.flipped(bits), place.y],
                self.rz.at[bits - 1],
                self.sems.at[5],
                self.sems.at[5 + bits],
                place.at(z=place.flipped(bit)),
            ).start()

    def start_step(self):
        place = self.place
        bit = 1
        while 2 * bit < place.depth:
            for bits in self.offsets(bit):
                wait_received(place, self.rz.at[bits - 1], self.sems.at[5 + bits])
                here = (place.x, place.flipped(bits - bit), place.y)
                self.total[here] = self.total[here] + self.rz[bits - 1]
            bit *= 2
            self.send_over(bit)

    def finish(self):
        place = self.place
        last = place.depth // 2
        wait_received(place, self.rz.at[last - 1], self.sems.at[5 + last])
        total = self.total[place.x, place.z, place.y].astype(F32)
        self.out[...] = total + self.rz[last - 1].astype(F32)

    def drain(self):
        self.core().wait_send()
        wait_sent(self.place, self.rc.at[:, pl.ds(0, 3 * self.place.depth // 4)], self.sems.at[2])
        wait_sent(self.place, self.rz, self.sems.at[5])


def iota(shape, dim):
    return lax.broadcasted_iota(jnp.int32, shape, dim)


def dot(left, right):
    return lax.dot_general(left, right, (((1,), (0,)), ((), ())), preferred_element_type=F32)


def dot_nt(left, right):
    return lax.dot_general(left, right, (((1,), (1,)), ((), ())), preferred_element_type=F32)


def dot_tn(left, right):
    return lax.dot_general(left, right, (((0,), (0,)), ((), ())), preferred_element_type=F32)


def shift_of(size):
    assert size & (size - 1) == 0
    return size.bit_length() - 1


BIASES = ("query", "value", "output", "down", "up")
SCALARS = len(BIASES)


def spread_bias(gathered, name, per, total):
    rows = gathered.shape[0]
    pick = iota((LANES, total), 0) == (iota((LANES, total), 1) & (per - 1))
    spread = dot(gathered.astype(BF16), pick.astype(BF16))
    owner = jnp.right_shift(iota((rows, total), 1), shift_of(per)) * 8 + BIASES.index(name)
    return jnp.sum(jnp.where(iota((rows, total), 0) == owner, spread, 0.0), axis=0, keepdims=True)


def head_bias(gathered, name, per, head, first):
    rows = gathered.shape[0]
    column = iota((LANES, LANES), 1) - first
    pick = (iota((LANES, LANES), 0) == (column & (per - 1))) & (column >= 0) & (column < HD)
    spread = dot(gathered.astype(BF16), pick.astype(BF16))
    column = head * HD + iota((rows, LANES), 1) - first
    owner = jnp.right_shift(column, shift_of(per)) * 8 + BIASES.index(name)
    return jnp.sum(jnp.where(iota((rows, LANES), 0) == owner, spread, 0.0), axis=0, keepdims=True)


def own_values(total, base, per, flat):
    at = flat * per
    row = iota(total.shape, 0) == base + lax.div(at, LANES)
    chosen = jnp.sum(jnp.where(row, total, 0.0), axis=0, keepdims=True)
    shift = lax.rem(LANES - lax.rem(at, LANES), LANES)
    return pltpu.roll(jnp.broadcast_to(chosen, (8, LANES)), shift, 1)[0:1]


def layer_kernel(
    blocks,
    parts,
    window,
    docs,
    x_ref,
    seg_ref,
    win_ref,
    wo_ref,
    wup_ref,
    wdown_ref,
    bias_refs,
    alphas_ref,
    grad_ref,
    out_ref,
    gx_ref,
    r_win,
    r_out,
    r_up,
    r_down,
    r_aux,
    gathered,
    gather_sems,
    trees,
    exchange_sems,
    halo_sems,
    segs,
    tile,
    aux_ref,
    xg,
    ws,
    wh,
    pw,
    rw,
    wsum,
    w_in,
    qt_ref,
    kv_ref,
    kvt,
    starts_ref,
    ot_ref,
    of_ref,
    lse_ref,
    mixed_t,
    dos,
    doct_ref,
    act_s,
    slope_s,
    gpre_s,
    gres_ref,
    q_rows_s,
    d_rows_s,
    delta_ref,
    dq_s,
    grad_s,
    dqt_ref,
    dkv_sum,
    dq_in,
    dkv_in,
    halo_out,
    halo_in,
    gp,
    partials,
):
    place = Place(blocks)
    depth, devices = place.depth, 4 * blocks
    gwin, gwo, gwup, gwdown, gaux = gathered
    in_rows = win_ref.shape[0]
    p_out, p_up, p_down = partials
    width, hidden = gwin.shape[-1] // 3, gwup.shape[-1]
    per, per_up = width // devices, hidden // devices
    span, pairs_of_chunks, reach = window + GROUP, GROUP // 2, window // 2
    free = pairs_of_chunks - reach

    def loop(call, low=1, high=GROUP):
        def step(number, carry):
            call(number)
            return carry

        lax.fori_loop(low, high, step, 0)

    def exchange(src, dst, sems, each=False):
        def copy(offset, come=False):
            landing = place.other_slot(-offset) if come else place.slot
            target = place.other_slot(offset)
            return remote(
                src(target),
                dst(landing),
                sems.at[0],
                sems.at[offset if each else 1],
                place.member(target),
            )

        return copy

    def entry(ref, base=0):
        return lambda index: ref.at[base + index]

    seg_sems, x_s, x_r, w_sems, o_sems, d_sems, dq_sems, dkv_sems, g_sems = exchange_sems
    seg_copy = exchange(lambda target: tile, entry(segs, window), seg_sems)
    o_copy = exchange(entry(ot_ref), entry(mixed_t), o_sems)
    d_copy = exchange(entry(dos), entry(doct_ref), d_sems, True)
    dq_copy = exchange(entry(dqt_ref), entry(dq_in), dq_sems)
    dkv_copy = exchange(entry(dkv_sum), entry(dkv_in), dkv_sems)
    seg_hs, seg_hr, kv_hs, kv_hr, back_hs, back_hr = halo_sems

    def all_here(ref, sems):
        wait_received(place, ref.at[pl.ds(0, GROUP - 1)], sems.at[1])

    def all_sent(ref, sems):
        wait_sent(place, ref.at[pl.ds(0, GROUP - 1)], sems.at[0])

    def send_to(copy, target):
        offset = lax.rem(target - place.slot + GROUP, GROUP)

        @pl.when(offset != 0)
        def _():
            copy(offset).start()

    def await_from(copy, source):
        offset = lax.rem(place.slot - source + GROUP, GROUP)

        @pl.when(offset != 0)
        def _():
            copy(offset, True).wait_recv()

    greet(place, parts, True)

    head, sequence = lax.div(place.slot, 2), lax.rem(place.slot, 2)
    group_x = place.part * 2 + sequence
    row = iota((16, LANES), 0)
    numbers = seg_ref[...].astype(F32)
    tile[...] = jnp.where(row == 0, numbers[0:1], numbers[1:2]).astype(BF16)
    segs[window + place.slot] = tile[...]
    aux_ref[...] = jnp.zeros_like(aux_ref)
    for index, ref in enumerate(bias_refs):
        aux_ref[index : index + 1, 0 : ref.shape[-1]] = ref[...].astype(F32).reshape(1, ref.shape[-1])
    if window:

        @pl.when(place.part == 0)
        def _():
            kv_ref[pl.ds(0, window)] = jnp.zeros((window, LANES, LANES), BF16)

    g_aux = Gather(place, aux_ref, gaux, gather_sems[0])
    plan = (
        (wo_ref, gwo, None),
        (wup_ref, gwup, (0, hidden // 2)),
        (wup_ref, gwup, (hidden // 2, hidden // 2)),
        (wdown_ref, gwdown, (0, width // 2)),
        (wdown_ref, gwdown, (width // 2, width // 2)),
        (win_ref, gwin, None),
    )
    rest = [
        TreeGather(place, src, dst, sems, cols)
        for (src, dst, cols), sems in zip(plan, gather_sems[1:])
    ]
    g_wo, g_up0, g_up1, g_down0, g_down1, g_win = rest

    def x_send(code, bit, src=None):
        chunk = xg.at[place.crossed(code)]
        remote(
            chunk if src is None else src,
            chunk,
            x_s.at[0],
            x_r.at[code ^ bit],
            place.member(place.crossed(bit)),
        ).start()

    def x_here(*codes):
        for code in codes:
            wait_received(place, xg.at[place.crossed(code)], x_r.at[code])

    x_send(0, 1, x_ref.at[1 - sequence])
    g_wo.start_line()
    g_up0.start_line()
    g_up1.start_line()
    g_down0.start_line()
    g_down1.start_line()
    xg[pl.ds(place.slot, 1)] = x_ref[pl.ds(sequence, 1)]
    g_aux.start_line()

    low_rows = iota((in_rows, LANES), 1) < HD
    for pair in range(HEADS // 2):
        q_at, k_at, v_at = [
            win_ref[:, kind * width + pair * LANES : kind * width + (pair + 1) * LANES].astype(F32)
            for kind in range(3)
        ]
        ws[2 * pair, :, 0:LANES] = jnp.where(low_rows, k_at, swap_halves(v_at)).astype(BF16)
        ws[2 * pair, :, LANES:] = jnp.where(low_rows, q_at, 0.0).astype(BF16)
        ws[2 * pair + 1, :, 0:LANES] = jnp.where(low_rows, swap_halves(k_at), v_at).astype(BF16)
        ws[2 * pair + 1, :, LANES:] = jnp.where(low_rows, swap_halves(q_at), 0.0).astype(BF16)

    def to_heads(src, dst, send, recv):
        def step(offset):
            other = lax.rem(head + offset, HEADS)
            remote(src.at[other], dst, send, recv, place.member(2 * other + sequence)).start()

        loop(step, 1, HEADS)

    def to_head_group(src, dst, send, recv):
        for offset in range(1, 2 * parts):
            other = lax.rem(group_x + offset, 2 * parts)
            part, other_sequence = lax.div(other, 2), lax.rem(other, 2)
            device = place.member(2 * head + other_sequence, part)
            remote(src(part, other_sequence), dst(offset), send, recv, device).start()

    every = slice(None)
    to_heads(ws, wh.at[place.part, head, sequence], w_sems.at[0], w_sems.at[1])
    wh[place.part, head, sequence] = ws[head]
    loop(lambda offset: seg_copy(offset).start())
    g_wo.start_step()
    g_up0.start_step()
    g_up1.start_step()
    for bit in (4, 2, 8):
        x_send(0, bit, x_ref.at[sequence])
    g_down0.start_step()
    g_down1.start_step()
    x_here(1)
    for bit in (4, 2, 8):
        x_send(1, bit)
    g_wo.start_first()
    g_up0.start_first()
    g_up1.start_first()
    wait_received(place, ws.at[pl.ds(0, HEADS - 1)], w_sems.at[1])
    own_rows = wh.at[place.part, every, sequence]
    to_head_group(lambda *at: own_rows, lambda offset: own_rows, w_sems.at[2], w_sems.at[3])
    g_aux.start_columns()
    g_wo.start_second()

    wait_received(place, segs.at[pl.ds(0, GROUP - 1)], seg_sems.at[1])

    def seg_halo(part):
        return remote(
            segs.at[pl.ds(GROUP, window)],
            segs.at[pl.ds(0, window)],
            seg_hs.at[0],
            seg_hr.at[0],
            place.member(place.slot, part),
        )

    if parts > 1:

        @pl.when(place.part < parts - 1)
        def _():
            seg_halo(place.part + 1).start()

    x_here(4)
    x_send(4, 2)
    x_send(4, 8)
    g_down0.start_first()
    g_down1.start_first()
    g_up0.start_second()
    g_up1.start_second()
    g_aux.start_hands()
    x_here(5)
    x_send(5, 2)
    x_send(5, 8)
    x_here(2, 3)
    x_send(2, 8)
    x_send(3, 8)
    g_aux.finish()
    wait_received(place, rw, w_sems.at[3])

    aux = gaux[...].reshape(devices * 8, LANES)
    bias_q = head_bias(aux, "query", per, head, 0)
    bias_v = head_bias(aux, "value", per, head, HD)

    def kv_halo(number, part):
        return remote(
            kv_ref.at[GROUP + number],
            kv_ref.at[number],
            kv_hs.at[0],
            kv_hr.at[number],
            place.member(place.slot, part),
        )

    def project(code):
        first = 2 * lax.div(place.crossed(code), 2)
        rows = xg[pl.ds(first, 2)].reshape(2 * LANES, width)
        made = dot(rows, wh[...].reshape(width, 2 * LANES))
        kv = (made[:, :LANES] + bias_v).astype(BF16)
        q = (made[:, LANES:] + bias_q).astype(BF16).astype(F32) * 0.125
        for side in range(2):
            chunk = first + side
            at = slice(side * LANES, (side + 1) * LANES)
            kv_ref[window + chunk] = kv[at]
            kvt[window + chunk] = kv[at].T
            qt_ref[chunk] = q[at].T[:HD].astype(BF16)
            if parts > 1:

                @pl.when((place.part < parts - 1) & (chunk >= GROUP - window))
                def _():
                    kv_halo(chunk - (GROUP - window), place.part + 1).start()

    project(0)
    project(2)
    g_down0.start_second()
    g_down1.start_second()
    g_wo.start_hands()
    project(4)
    x_here(6, 7)
    x_send(6, 8)
    x_send(7, 8)
    project(6)
    g_up0.start_hands()
    g_up1.start_hands()
    x_here(8, 9)
    project(8)
    x_here(12, 13)
    project(12)
    g_down0.start_hands()
    g_down1.start_hands()

    if parts > 1:

        @pl.when(place.part < parts - 1)
        def _():
            seg_halo(place.part + 1).wait_send()

        @pl.when(place.part > 0)
        def _():
            seg_halo(place.part - 1).wait_recv()

    chosen = jnp.where(iota((span, 16, LANES), 1) == sequence, segs[...].astype(F32), 0.0)
    seen = jnp.sum(chosen, axis=1)
    outside = (iota((span, LANES), 0) < window) & (place.part == 0)
    seen = jnp.where(outside, -1.0, seen)
    own = seen[window:]
    start = jnp.zeros((GROUP, LANES), F32)
    for number in range(docs):
        count = jnp.sum(jnp.where(seen == number - 1, 1.0, 0.0), axis=0, keepdims=True)
        count = jnp.sum(count, axis=1, keepdims=True)
        start = start + jnp.where(own >= number, count, 0.0)
    starts_ref[...] = start.astype(jnp.int32)

    x_here(10, 11)
    project(10)
    x_here(14, 15)
    project(14)

    many = window + 2
    older = window * LANES

    def q_rows_of(ref, m):
        return jnp.concatenate([ref[pl.ds(2 * m, 1)], ref[pl.ds(2 * m + 1, 1)]], axis=1)

    def turned_window(m):
        return jnp.concatenate([kvt[2 * m + i] for i in range(many)], axis=1)

    def masked(scores, start, q_place, block, base):
        k_place = base + block * BLOCK + iota((BLOCK, BLOCK), 0)
        visible = k_place >= start
        if block == reach:
            visible = visible & (k_place <= q_place)
        return jnp.where(visible, scores, NEG)

    blank = jnp.zeros((HD, BLOCK), BF16)

    def attend(step, carry):
        @pl.when(step == 0)
        def _():
            g_win.start_line()

        @pl.when(step == 4)
        def _():
            g_win.start_step()

        @pl.when(step == 7)
        def _():
            g_win.start_first()

        if parts > 1:

            @pl.when((step == free) & (place.part > 0))
            def _():
                loop(lambda number: kv_halo(number, place.part - 1).wait_recv(), 0, window)

        @pl.when(step == free)
        def _():
            def turn(number):
                kvt[number] = kv_ref[number].T

            loop(turn, 0, window)

        turnover = place.slot
        late = lax.rem(step - free + GROUP + turnover, reach)
        if free:
            m = jnp.where(step < free, reach + lax.rem(step + turnover, free), late)
        else:
            m = late
        q_wide = jnp.concatenate([two(qt_ref, 2 * m), blank], axis=0)
        start = q_rows_of(starts_ref, m)
        base = m * BLOCK
        q_place = base + older + iota((1, BLOCK), 1)
        scores = [
            masked(
                dot(kv_ref[pl.ds(2 * (m + block), 2)].reshape(BLOCK, LANES), q_wide),
                start,
                q_place,
                block,
                base,
            )
            for block in range(reach + 1)
        ]
        peak = functools.reduce(jnp.maximum, scores)
        peak = jnp.max(peak, axis=0, keepdims=True)
        weights = [jnp.exp(score - peak) for score in scores]
        total = functools.reduce(jnp.add, weights)
        total = jnp.sum(total, axis=0, keepdims=True)
        weights = jnp.concatenate([weight.astype(BF16) for weight in weights], axis=0)
        out = dot(turned_window(m)[HD:], weights) / total
        lse = peak + jnp.log(total)
        for side in range(2):
            lanes = slice(side * LANES, (side + 1) * LANES)
            of_ref[2 * m + side] = out[:, lanes]
            ot_ref[2 * m + side] = out[:, lanes].astype(BF16)
            lse_ref[pl.ds(2 * m + side, 1)] = lse[:, lanes]
            send_to(o_copy, 2 * m + side)
        return carry

    lax.fori_loop(0, pairs_of_chunks, attend, 0)
    mixed_t[place.slot] = ot_ref[place.slot]

    a0, a1 = alphas_ref[0], alphas_ref[1]
    bias_out = spread_bias(aux, "output", per, width)
    bias_down = spread_bias(aux, "down", per, width)
    bias_up = spread_bias(aux, "up", per_up, hidden)
    rows = 2 * LANES
    wide_tokens = x_ref[...].reshape(rows, width).astype(F32)
    grads = grad_ref[...].reshape(rows, width).astype(F32)
    grad_ffn = (a1 * grads).astype(BF16)
    g_win.start_second()
    g_wo.finish()
    full_out = gwo[...].reshape(width, width)

    all_here(mixed_t, o_sems)
    mixed_all = mixed_t[...].reshape(HEADS, 2, HD, LANES)
    mixed_turned = [mixed_all[:, s].reshape(width, LANES) for s in range(2)]
    mixed = jnp.concatenate([mixed_turned[0].T, mixed_turned[1].T], axis=0)
    branch = dot(mixed, full_out) + bias_out
    attn_term = a0 * branch
    residual = wide_tokens + attn_term
    hidden_in = residual.astype(BF16)

    ffn = jnp.zeros((rows, width), F32) + bias_down
    grad_res = grads
    tile_up = 512
    g_up0.finish()
    g_up1.finish()
    whole_up = gwup.reshape(width, hidden)
    whole_down = gwdown.reshape(hidden, width)
    for t in range(hidden // tile_up):
        cols = pl.ds(t * tile_up, tile_up)
        pre = dot(hidden_in, whole_up[:, cols]) + bias_up[:, t * tile_up : (t + 1) * tile_up]
        phi = 0.5 * (1.0 + lax.erf(pre * (1.0 / math.sqrt(2.0))))
        act_s[:, cols] = (pre * phi).astype(BF16)
        slope = phi + pre * jnp.exp(-0.5 * pre * pre) * (1.0 / math.sqrt(2.0 * math.pi))
        slope_s[:, cols] = slope
    sources = [
        (TreeReduce, p_out, r_out, None),
        (TreeReduce, p_up, r_up, (0, hidden // 2)),
        (TreeReduce, p_up, r_up, (hidden // 2, hidden // 2)),
        (TreeReduce, p_down, r_down, (0, width // 2)),
        (TreeReduce, p_down, r_down, (width // 2, width // 2)),
    ]
    t_out, t_up0, t_up1, t_down0, t_down1 = [
        kind(place, part, out, *scratch, cols)
        for (kind, part, out, cols), scratch in zip(sources, trees)
    ]
    t_aux = Total(place, *trees[-1])
    flat_down, flat_up = p_down.reshape(hidden, width), p_up.reshape(width, hidden)
    for half, tree in enumerate((t_down0, t_down1)):
        at = slice(half * width // 2, (half + 1) * width // 2)
        for t in range(hidden // tile_up):
            cols = pl.ds(t * tile_up, tile_up)
            flat_down[cols, at] = dot_tn(act_s[:, cols], grad_ffn[:, at]).astype(BF16)
        tree.start_core()
    g_down0.finish()
    g_down1.finish()
    for t in range(hidden // tile_up):
        cols = pl.ds(t * tile_up, tile_up)
        w_down = whole_down[cols, :]
        gpre = (dot_nt(grad_ffn, w_down) * slope_s[:, cols]).astype(BF16)
        gpre_s[:, cols] = gpre
        grad_res = grad_res + dot_nt(gpre, whole_up[:, cols])
    hidden_turned = hidden_in.T

    def up_part(half, tree):
        for t in range(hidden // tile_up // 2):
            cols = pl.ds(half * hidden // 2 + t * tile_up, tile_up)
            flat_up[:, cols] = dot(hidden_turned, gpre_s[:, cols]).astype(BF16)
        tree.start_core()

    up_part(0, t_up0)
    t_down0.start_second()
    g_win.start_hands()
    up_part(1, t_up1)
    t_down1.start_second()
    gres_ref[...] = grad_res
    grad_branch = (a0 * grad_res).astype(BF16)
    grad_mixed = dot_nt(grad_branch, full_out).astype(BF16).astype(F32)
    for s in range(2):
        turned = grad_mixed[s * LANES : (s + 1) * LANES].T.astype(BF16)
        for number in range(HEADS):
            dos[2 * number + s] = turned[number * HD : (number + 1) * HD]
    loop(lambda offset: d_copy(offset).start())
    doct_ref[place.slot] = dos[place.slot]
    t_up0.start_second()

    p_out.reshape(width, width)[...] = dot(
        jnp.concatenate([mixed_turned[0], mixed_turned[1]], axis=1), grad_branch
    ).astype(BF16)
    t_out.start_core()
    t_up1.start_second()

    for t in range(hidden // tile_up):
        cols = pl.ds(t * tile_up, tile_up)
        ffn = ffn + dot(act_s[:, cols], whole_down[cols, :])
    ffn_term = a1 * ffn
    stream = residual + ffn_term
    out_ref[...] = stream.astype(BF16).reshape(2, LANES, width)

    def whole(values):
        return jnp.sum(jnp.sum(values, axis=0, keepdims=True), axis=1, keepdims=True)

    sums = (
        whole(stream * stream),
        whole(attn_term * attn_term),
        whole(ffn_term * ffn_term),
        whole(grad_res * branch),
        whole(grads * ffn),
    )
    lane = iota((1, LANES), 1)
    scalars = jnp.zeros((1, LANES), F32)
    for number, value in enumerate(sums):
        scalars = scalars + jnp.where(lane == number, value, 0.0)
    up_row = jnp.sum(gpre_s[...].astype(F32), axis=0, keepdims=True)
    down_row = jnp.sum(grad_ffn.astype(F32), axis=0, keepdims=True)
    out_row = jnp.sum(grad_branch.astype(F32), axis=0, keepdims=True)
    wide_rows = width // LANES
    bases = {name: number * wide_rows for number, name in enumerate(BIASES)}
    last_row = (len(BIASES) - 1) * wide_rows + hidden // LANES

    def keep(base, row):
        for number in range(row.shape[1] // LANES):
            here = slice(number * LANES, (number + 1) * LANES)
            t_aux.mine[base + number : base + number + 1] = row[:, here]

    t_aux.mine[...] = jnp.zeros_like(t_aux.mine)
    keep(bases["output"], out_row)
    keep(bases["down"], down_row)
    keep(bases["up"], up_row)
    keep(last_row, scalars)

    t_out.start_second()
    early = (t_down0, t_down1, t_up0, t_up1, t_out)
    low_block = iota((BLOCK, LANES), 1) < HD

    def clear(m):
        dq_s[m] = jnp.zeros((HD, BLOCK), F32)

    loop(clear, 0, pairs_of_chunks)

    def back_halo(u, part):
        pair = pl.ds(2 * u, 2)
        return remote(
            halo_out.at[pair],
            halo_in.at[pair],
            back_hs.at[0],
            back_hr.at[u],
            place.member(place.slot, part),
        )

    def ready(m):
        await_from(d_copy, 2 * m)
        await_from(d_copy, 2 * m + 1)
        qt, dt = two(qt_ref, 2 * m), two(doct_ref, 2 * m)
        both = jnp.concatenate([qt, dt], axis=0).astype(F32).T
        here = pl.ds(2 * m, 2)
        q_rows_s[here] = jnp.where(low_block, both, 0.0).astype(BF16).reshape(2, LANES, LANES)
        d_rows_s[here] = jnp.where(low_block, 0.0, both).astype(BF16).reshape(2, LANES, LANES)
        delta = jnp.sum(dt.astype(F32) * two(of_ref, 2 * m), axis=0, keepdims=True)
        delta_ref[pl.ds(2 * m, 1)] = delta[:, :LANES]
        delta_ref[pl.ds(2 * m + 1, 1)] = delta[:, LANES:]

    def key_block(u, low, count):
        kv = kv_ref[pl.ds(2 * u, 2)].reshape(BLOCK, LANES)
        keys_turned = two(kvt, 2 * u)[:HD]
        k_place = u * BLOCK + iota((BLOCK, BLOCK), 0)
        grad = jnp.zeros((BLOCK, LANES), F32)
        for number in range(count):
            m = low + number
            here = pl.ds(2 * m, 2)
            q_wide = jnp.concatenate([two(qt_ref, 2 * m), blank], axis=0)
            d_wide = jnp.concatenate([blank, two(doct_ref, 2 * m)], axis=0)
            visible = k_place >= q_rows_of(starts_ref, m)
            if number == 0:
                visible = visible & (k_place <= m * BLOCK + older + iota((1, BLOCK), 1))
            scores = jnp.where(visible, dot(kv, q_wide), NEG)
            probs = jnp.exp(scores - q_rows_of(lse_ref, m))
            grad_scores = (probs * (dot(kv, d_wide) - q_rows_of(delta_ref, m))).astype(BF16)
            grad = grad + dot(grad_scores, q_rows_s[here].reshape(BLOCK, LANES))
            grad = grad + dot(probs.astype(BF16), d_rows_s[here].reshape(BLOCK, LANES))
            dq_s[m] += dot(keys_turned, grad_scores)
        grad_s[...] = grad

    def settle(u):
        pair = u - reach
        if parts > 1:
            late = pair - (pairs_of_chunks - reach)

            @pl.when((late >= 0) & (place.part < parts - 1))
            def _():
                back_halo(late, place.part + 1).wait_recv()
                grad_s[...] += halo_in[pl.ds(2 * late, 2)].reshape(BLOCK, LANES).astype(F32)

        dkv_sum[pl.ds(2 * pair, 2)] = grad_s[...].astype(BF16).reshape(2, LANES, LANES)
        dq = dq_s[pair] * 0.125
        for side in range(2):
            send_to(dkv_copy, 2 * pair + side)
            dqt_ref[2 * pair + side] = dq[:, side * LANES : (side + 1) * LANES].astype(BF16)
            send_to(dq_copy, 2 * pair + side)

    def attend_back(u, carry):
        @pl.when(u == 1)
        def _():
            t_down0.start_first()

        @pl.when(u == 3)
        def _():
            t_down1.start_first()

        @pl.when(u == 5)
        def _():
            t_up0.start_first()

        @pl.when(u == 7)
        def _():
            t_up1.start_first()

        @pl.when(u == 9)
        def _():
            t_out.start_first()

        @pl.when(u < pairs_of_chunks)
        def _():
            ready(u)

        low = jnp.maximum(u - reach, 0)
        count = jnp.minimum(u, pairs_of_chunks - 1) - low + 1
        needed = (u >= reach) | (place.part > 0)
        for number in range(1, reach + 2):

            @pl.when(needed & (count == number))
            def _():
                key_block(u, low, number)

        if parts > 1:

            @pl.when((u < reach) & (place.part > 0))
            def _():
                halo_out[pl.ds(2 * u, 2)] = grad_s[...].astype(BF16).reshape(2, LANES, LANES)
                back_halo(u, place.part - 1).start()

        @pl.when(u >= reach)
        def _():
            settle(u)

        return carry

    lax.fori_loop(0, reach + pairs_of_chunks, attend_back, 0)
    dq_in[place.slot] = dqt_ref[place.slot]
    t_down0.start_line()
    t_down1.start_line()
    t_up0.start_line()
    t_up1.start_line()
    dkv_in[place.slot] = dkv_sum[place.slot]

    dq_all = jnp.concatenate([dqt_ref[i] for i in range(GROUP)], axis=1)
    dkv_all = dkv_sum[...].reshape(GROUP * LANES, LANES)
    twice = jnp.concatenate([dq_all, dq_all], axis=0)
    query_row = dot_nt(jnp.ones((8, GROUP * LANES), BF16), twice)[0:1]
    value_row = jnp.sum(dkv_all.astype(F32), axis=0, keepdims=True)
    value_row = jnp.where(lane < HD, swap_halves(value_row), value_row)
    mine = (iota((wide_rows, LANES), 0) == lax.div(head, 2)) & (
        lax.div(iota((wide_rows, LANES), 1), HD) == lax.rem(head, 2)
    )
    for name, sums_row in (("query", query_row), ("value", value_row)):
        t_aux.mine[bases[name] : bases[name] + wide_rows] = jnp.where(mine, sums_row, 0.0)
    t_aux.start_core()
    x_rows = xg[...].reshape(GROUP * LANES, width)
    turned = jnp.concatenate(
        [dot_tn(dkv_all, x_rows), dot(dq_all, x_rows), jnp.zeros((HD, width), F32)], axis=0
    )
    pw[...] = turned.T.astype(BF16).reshape(pw.shape)
    to_head_group(
        lambda *at: pw.at[at[0], every, at[1]],
        lambda offset: rw.at[offset - 1],
        g_sems.at[0],
        g_sems.at[1],
    )
    t_aux.start_columns()
    t_out.start_line()
    t_down0.start_step()
    wait_received(place, rw, g_sems.at[1])
    total = pw[place.part, every, sequence].astype(F32)
    for number in range(2 * parts - 1):
        total = total + rw[number].astype(F32)
    wsum[...] = total
    to_heads(wsum, w_in.at[head], g_sems.at[2], g_sems.at[3])
    w_in[head] = wsum[head]
    t_aux.start_line()
    t_down1.start_step()
    t_up0.start_step()

    all_here(dq_in, dq_sems)
    for s in range(2):
        turned = jnp.concatenate([dq_in[2 * number + s] for number in range(HEADS)], axis=0)
        gp[s * LANES : (s + 1) * LANES, 0:width] = turned.astype(F32).T.astype(BF16)
    g_win.finish()
    full_in = gwin.reshape(width, 3 * width)
    gx = gres_ref[...] + dot_nt(gp[:, 0:width], full_in[:, 0:width])
    t_up1.start_step()
    t_out.start_step()
    all_here(dkv_in, dkv_sems)
    low_lane = iota((LANES, LANES), 1) < HD
    for s in range(2):
        at_rows = slice(s * LANES, (s + 1) * LANES)
        for pair in range(HEADS // 2):
            even = dkv_in[4 * pair + s].astype(F32)
            odd = dkv_in[4 * pair + 2 + s].astype(F32)
            keys = jnp.where(low_lane, even, swap_halves(odd))
            values = jnp.where(low_lane, swap_halves(even), odd)
            at = width + pair * LANES
            gp[at_rows, at : at + LANES] = keys.astype(BF16)
            gp[at_rows, width + at : width + at + LANES] = values.astype(BF16)
    gx = gx + dot_nt(gp[:, width:], full_in[:, width:])
    gx_ref[...] = gx.astype(BF16).reshape(2, LANES, width)
    wait_received(place, w_in.at[pl.ds(0, HEADS - 1)], g_sems.at[3])
    for pair in range(HEADS // 2):
        even, odd = w_in[2 * pair], w_in[2 * pair + 1]
        even_kv, odd_kv = even[:, :LANES], odd[:, :LANES]
        parts_of = (
            jnp.where(low_rows, even[:, LANES:], swap_halves(odd[:, LANES:])),
            jnp.where(low_rows, even_kv, swap_halves(odd_kv)),
            jnp.where(low_rows, swap_halves(even_kv), odd_kv),
        )
        for kind, value in enumerate(parts_of):
            at = kind * width + pair * LANES
            r_win[:, at : at + LANES] = value
    for tree in early:
        tree.finish()
    totals = t_aux.result()
    flat = place.part * GROUP + place.slot
    for number, name in enumerate(BIASES):
        own = own_values(totals, bases[name], per_up if name == "up" else per, flat)
        r_aux[number : number + 1] = own
    r_aux[SCALARS : SCALARS + 1] = totals[last_row : last_row + 1]
    all_sent(segs, seg_sems)
    wait_sent(place, xg.at[pl.ds(0, GROUP - 1)], x_s.at[0])
    wait_sent(place, ws.at[pl.ds(0, HEADS - 1)], w_sems.at[0])
    wait_sent(place, rw, w_sems.at[2])
    wait_sent(place, rw, g_sems.at[0])
    wait_sent(place, w_in.at[pl.ds(0, HEADS - 1)], g_sems.at[2])
    all_sent(ot_ref, o_sems)
    all_sent(dos, d_sems)
    all_sent(dqt_ref, dq_sems)
    all_sent(dkv_sum, dkv_sems)
    if parts > 1:

        @pl.when(place.part < parts - 1)
        def _():
            wait_sent(place, kv_ref.at[pl.ds(0, window)], kv_hs.at[0])

        @pl.when(place.part > 0)
        def _():
            wait_sent(place, halo_out, back_hs.at[0])

    for gather in (g_aux, *rest):
        gather.drain()
    for tree in early + (t_aux,):
        tree.drain()


def swap_halves(values):
    return jnp.concatenate([values[:, HD:], values[:, :HD]], axis=1)


def two(ref, index):
    return jnp.concatenate([ref[index], ref[index + 1]], axis=1)


def hand_out_kernel(
    tokens_all, out_ref, gx_ref, win_ref, wo_ref, wup_ref, wdown_ref, sums_ref, *results
):
    for src, dst in zip((out_ref, gx_ref, win_ref, wo_ref, wup_ref, wdown_ref), results[:6]):
        dst[...] = src[...]
    named = dict(zip(("query", "value", "output", "up", "down"), results[6:11]))
    for name, ref in named.items():
        ref[...] = sums_ref[BIASES.index(name), 0 : ref.shape[0]]
    results[11][...] = sums_ref[SCALARS, 3:5]
    results[12][...] = jnp.sqrt(sums_ref[SCALARS, 0:3] * (1.0 / tokens_all))


def call(kernel, out_shape, in_specs, out_specs, scratch, collective=None):
    return pl.pallas_call(
        kernel,
        out_shape=out_shape,
        in_specs=in_specs,
        out_specs=out_specs,
        scratch_shapes=scratch,
        compiler_params=pltpu.CompilerParams(
            collective_id=collective,
            has_side_effects=collective is not None,
            vmem_limit_bytes=VMEM_BYTES,
        ),
    )


def local(
    layer_input,
    segments,
    input_weight,
    output_weight,
    up_weight,
    down_weight,
    query_bias,
    value_bias,
    output_bias,
    up_bias,
    down_bias,
    alphas,
    out_grad,
):
    heads, blocks = lax.axis_size("head"), lax.axis_size("blk")
    depth, devices = blocks // 2, heads * blocks
    seqs, rows, width = layer_input.shape
    hidden = up_weight.shape[1]
    seq_len = rows * devices
    assert heads == 4 and seqs * HEADS == GROUP and rows == LANES
    longest = 16 * math.isqrt(seq_len)
    window, parts = longest // rows, devices // GROUP
    docs = 2 * seq_len // longest
    assert window <= GROUP and window % 2 == 0
    span = window + GROUP

    def shape(*dims, dtype=BF16):
        return jax.ShapeDtypeStruct(dims, dtype)

    vmem, smem = pl.BlockSpec(memory_space=VMEM), pl.BlockSpec(memory_space=pltpu.SMEM)
    dma = pltpu.SemaphoreType.DMA
    lead = (2, 2, depth, 2)
    in_rows, up_rows = input_weight.shape[0], down_weight.shape[0]
    tree_parts = ((in_rows, width),) + ((in_rows, hidden // 2),) * 2 + ((up_rows, width // 2),) * 2
    tokens = seqs * rows
    total_rows = -(-((len(BIASES) - 1) * width + hidden + LANES) // (8 * LANES)) * 8
    results = (
        shape(seqs, rows, width),
        shape(seqs, rows, width),
        shape(in_rows, 3 * width, dtype=F32),
        shape(in_rows, width, dtype=F32),
        shape(in_rows, hidden, dtype=F32),
        shape(up_rows, width, dtype=F32),
    )
    carried = call(
        functools.partial(layer_kernel, blocks, parts, window, docs),
        results + (shape(8, LANES, dtype=F32),),
        [vmem] * 6 + [(vmem,) * 5] + [smem, vmem],
        (vmem,) * 7,
        [
            [
                VMEM((*lead, in_rows, 3 * width), BF16),
                VMEM((*lead, in_rows, width), BF16),
                VMEM((*lead, in_rows, hidden), BF16),
                VMEM((*lead, up_rows, width), BF16),
                VMEM((*lead, 8, LANES), F32),
            ],
            [dma((Gather.COUNT,))] + [dma((TreeGather.COUNT + depth - 1,))] * 6,
            [TreeReduce.scratch(depth, *sizes, BF16) for sizes in tree_parts]
            + [Total.scratch(depth, total_rows)],
            [dma((n,)) for n in (2, 1, GROUP, 4, 2, GROUP, 2, 2, 4)],
            [dma((1,)), dma((1,)), dma((1,)), dma((window,)), dma((1,)), dma((window // 2,))],
            VMEM((span, 16, LANES), BF16),
            VMEM((16, LANES), BF16),
            VMEM((8, LANES), F32),
            VMEM((GROUP, LANES, width), BF16),
            VMEM((HEADS, in_rows, 2 * LANES), BF16),
            VMEM((parts, HEADS, 2, in_rows, 2 * LANES), BF16),
            VMEM((parts, HEADS, 2, in_rows, 2 * LANES), BF16),
            VMEM((2 * parts - 1, HEADS, in_rows, 2 * LANES), BF16),
            VMEM((HEADS, in_rows, 2 * LANES), F32),
            VMEM((HEADS, in_rows, 2 * LANES), F32),
            VMEM((GROUP, HD, LANES), BF16),
            VMEM((span, LANES, LANES), BF16),
            VMEM((span, LANES, LANES), BF16),
            VMEM((GROUP, LANES), jnp.int32),
            VMEM((GROUP, HD, LANES), BF16),
            VMEM((GROUP, HD, LANES), F32),
            VMEM((GROUP, LANES), F32),
            VMEM((GROUP, HD, LANES), BF16),
            VMEM((GROUP, HD, LANES), BF16),
            VMEM((GROUP, HD, LANES), BF16),
            VMEM((tokens, hidden), BF16),
            VMEM((tokens, hidden), F32),
            VMEM((tokens, hidden), BF16),
            VMEM((tokens, width), F32),
            VMEM((GROUP, LANES, LANES), BF16),
            VMEM((GROUP, LANES, LANES), BF16),
            VMEM((GROUP, LANES), F32),
            VMEM((GROUP // 2, HD, BLOCK), F32),
            VMEM((BLOCK, LANES), F32),
            VMEM((GROUP, HD, LANES), BF16),
            VMEM((GROUP, LANES, LANES), BF16),
            VMEM((GROUP, HD, LANES), BF16),
            VMEM((GROUP, LANES, LANES), BF16),
            VMEM((window, LANES, LANES), BF16),
            VMEM((window, LANES, LANES), BF16),
            VMEM((tokens, 3 * width), BF16),
            [
                VMEM((*lead, in_rows, width), BF16),
                VMEM((*lead, in_rows, hidden), BF16),
                VMEM((*lead, up_rows, width), BF16),
            ],
        ],
        collective=0,
    )(
        layer_input,
        segments,
        input_weight,
        output_weight,
        up_weight,
        down_weight,
        (query_bias, value_bias, output_bias, down_bias, up_bias),
        alphas,
        out_grad,
    )
    per, per_up = width // devices, hidden // devices
    return call(
        functools.partial(hand_out_kernel, seqs * seq_len * width),
        results
        + tuple(
            shape(size, dtype=F32) for size in (per, per, per, per_up, per, 2, 3)
        ),
        [vmem] * 7,
        (vmem,) * 13,
        [],
    )(*carried)


def solution(mesh):
    tokens = P(None, ("head", "blk"), None)
    rows, flat = P(("head", "blk"), None), P(("head", "blk"))
    return jax.shard_map(
        local,
        mesh=mesh,
        in_specs=(
            tokens,
            P(None, ("head", "blk")),
            rows,
            rows,
            rows,
            rows,
            flat,
            flat,
            flat,
            flat,
            flat,
            P(),
            tokens,
        ),
        out_specs=(
            tokens,
            tokens,
            rows,
            rows,
            rows,
            rows,
            flat,
            flat,
            flat,
            flat,
            flat,
            P(),
            P(),
        ),
        check_vma=False,
    )
```

```python
import functools
import math

import jax
import jax.numpy as jnp
from jax import lax
from jax.experimental import pallas as pl
from jax.experimental.pallas import tpu as pltpu
from jax.sharding import PartitionSpec as P

HEADS = 8
HD = 64
LANES = 128
GROUP = 16
BLOCK = 256
F32 = jnp.float32
BF16 = jnp.bfloat16
VMEM = pltpu.VMEM
NEG = -1e30


class Place:
    def __init__(self, blocks):
        self.blocks = blocks
        self.depth = blocks // 2
        head = lax.axis_index("head")
        block = lax.axis_index("blk")
        self.x, self.core = lax.div(head, 2), lax.rem(head, 2)
        self.z, self.y = lax.div(block, 2), lax.rem(block, 2)
        flat = head * blocks + block
        self.part, self.slot = lax.div(flat, GROUP), lax.rem(flat, GROUP)

    def at(self, x=None, core=None, z=None, y=None):
        x = self.x if x is None else x
        core = self.core if core is None else core
        z = self.z if z is None else z
        y = self.y if y is None else y
        return (x * 2 + core, z * 2 + y)

    def deeper(self, offset):
        return lax.rem(self.z + offset + self.depth, self.depth)

    def bits(self):
        bit = self.depth // 2
        while bit:
            yield bit
            bit //= 2

    def flipped(self, bits):
        z = self.z
        for bit in self.bits():
            if bits & bit:
                z = z + bit - 2 * bit * lax.rem(lax.div(self.z, bit), 2)
        return z

    def member(self, slot, part=None):
        part = self.part if part is None else part
        flat = part * GROUP + slot
        return (lax.div(flat, self.blocks), lax.rem(flat, self.blocks))

    def crossed(self, code):
        slot = self.slot
        for bit in (1, 2, 4, 8):
            if code & bit:
                slot = slot + bit - 2 * bit * lax.rem(lax.div(self.slot, bit), 2)
        return slot

    def other_slot(self, offset):
        return lax.rem(self.slot + offset + GROUP, GROUP)


def remote(src, dst, send, recv, device):
    return pltpu.make_async_remote_copy(
        src_ref=src,
        dst_ref=dst,
        send_sem=send,
        recv_sem=recv,
        device_id=device,
        device_id_type=pl.DeviceIdType.MESH,
    )


def greet(place, parts, tree):
    barrier = pltpu.get_barrier_semaphore()

    def hello(device):
        pl.semaphore_signal(barrier, inc=1, device_id=device, device_id_type=pl.DeviceIdType.MESH)

    def group(offset, carry):
        hello(place.member(place.other_slot(offset)))
        return carry

    lax.fori_loop(1, GROUP, group, 0)
    total = GROUP - 1
    if tree:

        def line(offset, carry):
            hello(place.at(z=place.deeper(offset)))
            return carry

        lax.fori_loop(1, place.depth, line, 0)
        hello(place.at(x=1 - place.x))
        hello(place.at(y=1 - place.y))
        hello(place.at(x=1 - place.x, y=1 - place.y))
        hello(place.at(core=1 - place.core))
        total += place.depth + 3

    def range_of(offset, carry):
        part = lax.rem(place.part + offset, parts)
        hello(place.member(place.slot, part))
        hello(place.member(place.crossed(1), part))
        return carry

    lax.fori_loop(1, parts, range_of, 0)
    return barrier, total + 2 * (parts - 1)


def halves_of(columns):
    if columns < 2 * LANES:
        return ((0, columns, "yx"),)
    most = columns // 2
    return ((0, most, "yx"), (most, columns - most, "xy"))


def wait_received(place, dst, sem):
    remote(dst, dst, sem, sem, place.at(core=1 - place.core)).wait_recv()


def wait_sent(place, src, sem):
    remote(src, src, sem, sem, place.at(core=1 - place.core)).wait_send()


class Gather:
    COUNT = 9

    def __init__(self, place, src, dst, sems, cols=None):
        self.place, self.src, self.dst, self.sems = place, src, dst, sems
        start, width = cols or (0, dst.shape[-1])
        self.cols = pl.ds(start, width)

    def part(self, *index):
        return self.dst.at[index + (slice(None), self.cols)]

    def column(self, core, x, y):
        return self.part(x, core, slice(None), y)

    def others(self):
        place = self.place
        return ((1 - place.x, place.y), (place.x, 1 - place.y), (1 - place.x, 1 - place.y))

    def own(self):
        place = self.place
        mine = self.part(place.x, place.core, place.z, place.y)
        return pltpu.make_async_copy(self.src.at[:, self.cols], mine, self.sems.at[0])

    def start_line(self):
        place = self.place
        for offset in range(1, place.depth):
            remote(
                self.src.at[:, self.cols],
                self.part(place.x, place.core, place.z, place.y),
                self.sems.at[1],
                self.sems.at[2],
                place.at(z=place.deeper(offset)),
            ).start()
        self.own().start()

    def lines(self):
        return self.part(0, 0, pl.ds(0, self.place.depth - 1), 0)

    def hand(self, x, y):
        place = self.place
        column = self.column(place.core, x, y)
        remote(
            column, column, self.sems.at[7], self.sems.at[8], place.at(core=1 - place.core)
        ).start()

    def start_columns(self):
        place = self.place
        self.own().wait()
        wait_received(place, self.lines(), self.sems.at[2])
        mine = self.column(place.core, place.x, place.y)
        for number, (x, y) in enumerate(self.others()):
            remote(
                mine, mine, self.sems.at[3], self.sems.at[4 + number], place.at(x=x, y=y)
            ).start()
        self.hand(place.x, place.y)

    def start_hands(self):
        for number, (x, y) in enumerate(self.others()):
            wait_received(
                self.place, self.column(self.place.core, x, y), self.sems.at[4 + number]
            )
            self.hand(x, y)

    def finish(self):
        every = slice(None)
        region = self.part(every, 1 - self.place.core, every, every)
        wait_received(self.place, region, self.sems.at[8])

    def drain(self):
        place = self.place
        wait_sent(place, self.lines(), self.sems.at[1])
        every = slice(None)
        wait_sent(
            place, self.part(every, every, pl.ds(0, 3 * place.depth // 4), 0), self.sems.at[3]
        )
        wait_sent(place, self.part(every, 0, every, every), self.sems.at[7])


def halves_of(columns):
    if columns < 2 * LANES:
        return ((0, columns, "yx"),)
    most = columns // 2
    return ((0, most, "yx"), (most, columns - most, "xy"))


class TreeGather:
    COUNT = 7

    def __init__(self, place, src, dst, sems, cols=None):
        self.place, self.src, self.dst, self.sems = place, src, dst, sems
        self.start, self.width = cols or (0, dst.shape[-1])
        self.halves = halves_of(self.width)
        self.cols = pl.ds(self.start, self.width)

    def part(self, *index):
        return self.dst.at[index + (slice(None), self.cols)]

    def cut(self, half, *index):
        start, width, _ = half
        return self.dst.at[index + (slice(None), pl.ds(self.start + start, width))]

    def across(self, half, first):
        place = self.place
        if (half[2] == "yx") == first:
            return place.x, 1 - place.y
        return 1 - place.x, place.y

    def region(self, half, first, core, x, y):
        every = slice(None)
        if first:
            return self.cut(half, x, core, every, y)
        if half[2] == "yx":
            return self.cut(half, x, core, every, every)
        return self.cut(half, every, core, every, y)

    def own(self):
        place = self.place
        mine = self.part(place.x, place.core, place.z, place.y)
        return pltpu.make_async_copy(self.src.at[:, self.cols], mine, self.sems.at[0])

    def send_piece(self, bits, bit):
        place = self.place
        piece = self.part(place.x, place.core, place.flipped(bits), place.y)
        remote(
            piece if bits else self.src.at[:, self.cols],
            piece,
            self.sems.at[1],
            self.sems.at[6 + (bits | bit)],
            place.at(z=place.flipped(bit)),
        ).start()

    def await_piece(self, bits):
        place = self.place
        piece = self.part(place.x, place.core, place.flipped(bits), place.y)
        wait_received(place, piece, self.sems.at[6 + bits])

    def start_line(self):
        for bit in self.place.bits():
            self.send_piece(0, bit)
        self.own().start()

    def start_step(self):
        known = [0]
        for bit in self.place.bits():
            for bits in known[1:]:
                self.send_piece(bits, bit)
            known += [bits | bit for bits in known]
            if bit > 1:
                for bits in known[len(known) // 2 :]:
                    self.await_piece(bits)

    def lines(self):
        return self.part(0, 0, pl.ds(0, self.place.depth - 1), 0)

    def exchange(self, number, first):
        place, half = self.place, self.halves[number]
        x, y = self.across(half, first)
        mine = self.region(half, first, place.core, place.x, place.y)
        return remote(
            mine,
            mine,
            self.sems.at[3],
            self.sems.at[4 if first else 5],
            place.at(x=x, y=y),
        )

    def all_received(self, first):
        every, place = slice(None), self.place
        xs = 0 if first else every
        wait_received(place, self.part(xs, 0, every, 0), self.sems.at[4 if first else 5])

    def received(self, number, first):
        half = self.halves[number]
        x, y = self.across(half, first)
        return self.region(half, first, self.place.core, x, y)

    def hand(self, region):
        place = self.place
        remote(
            region, region, self.sems.at[6], self.sems.at[2], place.at(core=1 - place.core)
        ).start()

    def start_first(self):
        place = self.place
        self.own().wait()
        for bits in range(1, place.depth, 2):
            self.await_piece(bits)
        for number in range(len(self.halves)):
            self.exchange(number, True).start()
        self.hand(self.part(place.x, place.core, slice(None), place.y))

    def start_second(self):
        self.all_received(True)
        for number in range(len(self.halves)):
            region = self.received(number, True)
            self.exchange(number, False).start()
            self.hand(region)

    def start_hands(self):
        self.all_received(False)
        for number in range(len(self.halves)):
            self.hand(self.received(number, False))

    def finish(self):
        every = slice(None)
        region = self.part(every, 1 - self.place.core, every, every)
        wait_received(self.place, region, self.sems.at[2])

    def drain(self):
        every, depth = slice(None), self.place.depth
        wait_sent(
            self.place, self.part(every, every, pl.ds(0, 3 * depth // 4), 0), self.sems.at[3]
        )
        wait_sent(self.place, self.lines(), self.sems.at[1])
        wait_sent(self.place, self.part(every, 0, every, every), self.sems.at[6])


class Reduce:
    COUNT = 8

    def __init__(self, place, part, out, rc, total, rn, rz, sems, cols=None):
        self.place, self.part = place, part
        self.cols = pl.ds(*(cols or (0, part.shape[-1])))
        self.out = out.at[:, self.cols]
        self.rc, self.total, self.rn, self.rz, self.sems = rc, total, rn, rz, sems

    @staticmethod
    def scratch(depth, rows, cols, dtype):
        return [
            VMEM((2, depth, 2, rows, cols), dtype),
            VMEM((2, depth, 2, rows, cols), dtype),
            VMEM((3, depth, rows, cols), dtype),
            VMEM((depth - 1, rows, cols), dtype),
            pltpu.SemaphoreType.DMA((Reduce.COUNT,)),
        ]

    def others(self):
        place = self.place
        return ((1 - place.x, place.y), (place.x, 1 - place.y), (1 - place.x, 1 - place.y))

    def core(self):
        place = self.place
        return remote(
            self.part.at[:, 1 - place.core, :, :, :, self.cols],
            self.rc,
            self.sems.at[0],
            self.sems.at[1],
            place.at(core=1 - place.core),
        )

    def columns(self):
        place = self.place
        for number, (x, y) in enumerate(self.others()):
            yield remote(
                self.total.at[x, :, y],
                self.rn.at[number],
                self.sems.at[2],
                self.sems.at[3 + number],
                place.at(x=x, y=y),
            )

    def line(self, offset):
        place = self.place
        return remote(
            self.total.at[place.x, place.deeper(offset), place.y],
            self.rz.at[offset - 1],
            self.sems.at[6],
            self.sems.at[7],
            place.at(z=place.deeper(offset)),
        )

    def start_core(self):
        self.core().start()

    def add_core(self, x, z, y):
        place = self.place
        self.total[x, z, y] = self.part[x, place.core, z, y, :, self.cols] + self.rc[x, z, y]

    def start_columns(self):
        place = self.place
        self.core().wait_recv()
        for copy, (x, y) in zip(self.columns(), self.others()):

            def add(z, carry):
                self.add_core(x, z, y)
                return carry

            lax.fori_loop(0, place.depth, add, 0)
            copy.start()

        def add(z, carry):
            self.add_core(place.x, z, place.y)
            return carry

        lax.fori_loop(0, place.depth, add, 0)

    def start_line(self):
        place = self.place
        for copy in self.columns():
            copy.wait_recv()
        here = (place.x, slice(None), place.y)
        total = self.total[here].astype(F32)
        for number in range(3):
            total = total + self.rn[number].astype(F32)
        self.total[here] = total.astype(self.total.dtype)
        for offset in range(1, place.depth):
            self.line(offset).start()

    def finish(self):
        place = self.place
        wait_received(place, self.rz, self.sems.at[7])
        result = self.total[place.x, place.z, place.y].astype(F32)
        for offset in range(1, place.depth):
            result = result + self.rz[offset - 1].astype(F32)
        self.out[...] = result

    def drain(self):
        place = self.place
        self.core().wait_send()
        wait_sent(place, self.rn, self.sems.at[2])
        wait_sent(place, self.rz, self.sems.at[6])


class Total:
    COUNT = 8

    def __init__(self, place, mine, rc, rn, rz, sums, sems):
        self.place, self.mine, self.rc, self.rn, self.rz = place, mine, rc, rn, rz
        self.sums, self.sems = sums, sems

    @staticmethod
    def scratch(depth, rows):
        return [
            VMEM((rows, LANES), F32),
            VMEM((rows, LANES), F32),
            VMEM((3, rows, LANES), F32),
            VMEM((depth - 1, rows, LANES), F32),
            VMEM((2, rows, LANES), F32),
            pltpu.SemaphoreType.DMA((Total.COUNT,)),
        ]

    others = Reduce.others

    def core(self):
        return remote(
            self.mine,
            self.rc,
            self.sems.at[0],
            self.sems.at[1],
            self.place.at(core=1 - self.place.core),
        )

    def start_core(self):
        self.core().start()

    def start_columns(self):
        self.core().wait_recv()
        self.sums[0] = self.mine[...] + self.rc[...]
        for number, (x, y) in enumerate(self.others()):
            remote(
                self.sums.at[0],
                self.rn.at[number],
                self.sems.at[2],
                self.sems.at[3],
                self.place.at(x=x, y=y),
            ).start()

    def start_line(self):
        place = self.place
        wait_received(place, self.rn, self.sems.at[3])
        self.sums[1] = self.sums[0] + self.rn[0] + self.rn[1] + self.rn[2]
        for offset in range(1, place.depth):
            remote(
                self.sums.at[1],
                self.rz.at[offset - 1],
                self.sems.at[4],
                self.sems.at[5],
                place.at(z=place.deeper(offset)),
            ).start()

    def result(self):
        place = self.place
        wait_received(place, self.rz, self.sems.at[5])
        total = self.sums[1]
        for offset in range(1, place.depth):
            total = total + self.rz[offset - 1]
        return total

    def drain(self):
        self.core().wait_send()
        wait_sent(self.place, self.rn, self.sems.at[2])
        wait_sent(self.place, self.rz, self.sems.at[4])


class TreeReduce:
    COUNT = 6

    def __init__(self, place, part, out, rc, total, ra, rb, fa, fb, rz, sems, cols=None):
        self.place, self.part = place, part
        self.cols = pl.ds(*(cols or (0, part.shape[-1])))
        self.out = out.at[:, self.cols]
        self.rc, self.total, self.rz = rc, total, rz
        self.second, self.first = (ra, rb), (fa, fb)
        self.sems = sems
        self.halves = halves_of(total.shape[-1])

    @staticmethod
    def scratch(depth, rows, cols, dtype):
        wide, narrow = [half[1] for half in halves_of(cols)]
        return [
            VMEM((2, depth, 2, rows, cols), dtype),
            VMEM((2, depth, 2, rows, cols), dtype),
            VMEM((depth, 2, rows, wide), dtype),
            VMEM((2, depth, rows, narrow), dtype),
            VMEM((depth, rows, wide), dtype),
            VMEM((depth, rows, narrow), dtype),
            VMEM((depth - 1, rows, cols), dtype),
            pltpu.SemaphoreType.DMA((TreeReduce.COUNT + depth - 1,)),
        ]

    core, start_core, add_core = Reduce.core, Reduce.start_core, Reduce.add_core

    def cut(self, half, *index):
        start, width, _ = half
        return index + (slice(None), pl.ds(start, width))

    def exchange(self, number, second):
        place, every = self.place, slice(None)
        half = self.halves[number]
        over_x = (half[2] == "yx") == second
        device = place.at(x=1 - place.x) if over_x else place.at(y=1 - place.y)
        if second:
            index = (1 - place.x, every, every) if over_x else (every, every, 1 - place.y)
            landing = self.second[number]
        else:
            index = (1 - place.x, every, place.y) if over_x else (place.x, every, 1 - place.y)
            landing = self.first[number]
        return remote(
            self.total.at[self.cut(half, *index)],
            landing,
            self.sems.at[2],
            self.sems.at[3 if second else 4],
            device,
        )

    def start_second(self):
        self.core().wait_recv()

        def add(z, carry):
            for x in range(2):
                for y in range(2):
                    self.add_core(x, z, y)
            return carry

        lax.fori_loop(0, self.place.depth, add, 0)
        for number in range(len(self.halves)):
            self.exchange(number, True).start()

    def accumulate(self, index, value):
        self.total[index] = self.total[index] + value

    def start_first(self):
        place = self.place
        wait_received(place, self.rc.at[0], self.sems.at[3])
        for number, half in enumerate(self.halves):
            landed = self.second[number]

            def add(z, carry):
                for other in range(2):
                    if half[2] == "yx":
                        self.accumulate(self.cut(half, place.x, z, other), landed[z, other])
                    else:
                        self.accumulate(self.cut(half, other, z, place.y), landed[other, z])
                return carry

            lax.fori_loop(0, place.depth, add, 0)
            self.exchange(number, False).start()

    def start_line(self):
        place = self.place
        wait_received(place, self.rc.at[0, :, 0], self.sems.at[4])
        for number, half in enumerate(self.halves):
            landed = self.first[number]

            def add(z, carry):
                self.accumulate(self.cut(half, place.x, z, place.y), landed[z])
                return carry

            lax.fori_loop(0, place.depth, add, 0)
        self.send_over(1)

    def offsets(self, bit):
        return range(bit, self.place.depth, 2 * bit)

    def send_over(self, bit):
        place = self.place
        for bits in self.offsets(bit):
            remote(
                self.total.at[place.x, place.flipped(bits), place.y],
                self.rz.at[bits - 1],
                self.sems.at[5],
                self.sems.at[5 + bits],
                place.at(z=place.flipped(bit)),
            ).start()

    def start_step(self):
        place = self.place
        bit = 1
        while 2 * bit < place.depth:
            for bits in self.offsets(bit):
                wait_received(place, self.rz.at[bits - 1], self.sems.at[5 + bits])
                here = (place.x, place.flipped(bits - bit), place.y)
                self.total[here] = self.total[here] + self.rz[bits - 1]
            bit *= 2
            self.send_over(bit)

    def finish(self):
        place = self.place
        last = place.depth // 2
        wait_received(place, self.rz.at[last - 1], self.sems.at[5 + last])
        total = self.total[place.x, place.z, place.y].astype(F32)
        self.out[...] = total + self.rz[last - 1].astype(F32)

    def drain(self):
        self.core().wait_send()
        wait_sent(self.place, self.rc.at[:, pl.ds(0, 3 * self.place.depth // 4)], self.sems.at[2])
        wait_sent(self.place, self.rz, self.sems.at[5])


def iota(shape, dim):
    return lax.broadcasted_iota(jnp.int32, shape, dim)


def dot(left, right):
    return lax.dot_general(left, right, (((1,), (0,)), ((), ())), preferred_element_type=F32)


def dot_nt(left, right):
    return lax.dot_general(left, right, (((1,), (1,)), ((), ())), preferred_element_type=F32)


def dot_tn(left, right):
    return lax.dot_general(left, right, (((0,), (0,)), ((), ())), preferred_element_type=F32)


def shift_of(size):
    assert size & (size - 1) == 0
    return size.bit_length() - 1


BIASES = ("query", "value", "output", "down", "up")
SCALARS = len(BIASES)


def spread_bias(gathered, name, per, total):
    rows = gathered.shape[0]
    pick = iota((LANES, total), 0) == (iota((LANES, total), 1) & (per - 1))
    spread = dot(gathered.astype(BF16), pick.astype(BF16))
    owner = jnp.right_shift(iota((rows, total), 1), shift_of(per)) * 8 + BIASES.index(name)
    return jnp.sum(jnp.where(iota((rows, total), 0) == owner, spread, 0.0), axis=0, keepdims=True)


def head_bias(gathered, name, per, head, first):
    rows = gathered.shape[0]
    column = iota((LANES, LANES), 1) - first
    pick = (iota((LANES, LANES), 0) == (column & (per - 1))) & (column >= 0) & (column < HD)
    spread = dot(gathered.astype(BF16), pick.astype(BF16))
    column = head * HD + iota((rows, LANES), 1) - first
    owner = jnp.right_shift(column, shift_of(per)) * 8 + BIASES.index(name)
    return jnp.sum(jnp.where(iota((rows, LANES), 0) == owner, spread, 0.0), axis=0, keepdims=True)


def own_values(total, base, per, flat):
    at = flat * per
    row = iota(total.shape, 0) == base + lax.div(at, LANES)
    chosen = jnp.sum(jnp.where(row, total, 0.0), axis=0, keepdims=True)
    shift = lax.rem(LANES - lax.rem(at, LANES), LANES)
    return pltpu.roll(jnp.broadcast_to(chosen, (8, LANES)), shift, 1)[0:1]


def layer_kernel(
    blocks,
    parts,
    window,
    docs,
    x_hbm,
    seg_hbm,
    win_hbm,
    wo_hbm,
    wup_hbm,
    wdown_hbm,
    bias_hbm,
    alphas_ref,
    grad_hbm,
    out_ref,
    gx_ref,
    r_win,
    r_out,
    r_up,
    r_down,
    r_aux,
    gathered,
    gather_sems,
    trees,
    exchange_sems,
    halo_sems,
    segs,
    tile,
    aux_ref,
    xg,
    ws,
    wh,
    pw,
    rw,
    wsum,
    w_in,
    qt_ref,
    kv_ref,
    kvt,
    starts_ref,
    ot_ref,
    of_ref,
    lse_ref,
    mixed_t,
    dos,
    doct_ref,
    act_s,
    slope_s,
    gpre_s,
    gres_ref,
    q_rows_s,
    d_rows_s,
    delta_ref,
    dq_s,
    grad_s,
    dqt_ref,
    dkv_sum,
    dq_in,
    dkv_in,
    halo_out,
    halo_in,
    gp,
    partials,
    loaded,
    load_sems,
):
    place = Place(blocks)
    depth, devices = place.depth, 4 * blocks
    x_ref, seg_ref, win_ref, wo_ref, wup_ref, wdown_ref, grad_ref, *bias_refs = loaded
    gwin, gwo, gwup, gwdown, gaux = gathered
    in_rows = win_ref.shape[0]
    p_out, p_up, p_down = partials
    width, hidden = gwin.shape[-1] // 3, gwup.shape[-1]
    per, per_up = width // devices, hidden // devices
    span, pairs_of_chunks, reach = window + GROUP, GROUP // 2, window // 2
    free = pairs_of_chunks - reach

    def loop(call, low=1, high=GROUP):
        def step(number, carry):
            call(number)
            return carry

        lax.fori_loop(low, high, step, 0)

    def exchange(src, dst, sems, each=False):
        def copy(offset, come=False):
            landing = place.other_slot(-offset) if come else place.slot
            target = place.other_slot(offset)
            return remote(
                src(target),
                dst(landing),
                sems.at[0],
                sems.at[offset if each else 1],
                place.member(target),
            )

        return copy

    def entry(ref, base=0):
        return lambda index: ref.at[base + index]

    seg_sems, x_s, x_r, w_sems, o_sems, d_sems, dq_sems, dkv_sems, g_sems = exchange_sems
    seg_copy = exchange(lambda target: tile, entry(segs, window), seg_sems)
    o_copy = exchange(entry(ot_ref), entry(mixed_t), o_sems)
    d_copy = exchange(entry(dos), entry(doct_ref), d_sems, True)
    dq_copy = exchange(entry(dqt_ref), entry(dq_in), dq_sems)
    dkv_copy = exchange(entry(dkv_sum), entry(dkv_in), dkv_sems)
    seg_hs, seg_hr, kv_hs, kv_hr, back_hs, back_hr = halo_sems

    def all_here(ref, sems):
        wait_received(place, ref.at[pl.ds(0, GROUP - 1)], sems.at[1])

    def all_sent(ref, sems):
        wait_sent(place, ref.at[pl.ds(0, GROUP - 1)], sems.at[0])

    def send_to(copy, target):
        offset = lax.rem(target - place.slot + GROUP, GROUP)

        @pl.when(offset != 0)
        def _():
            copy(offset).start()

    def await_from(copy, source):
        offset = lax.rem(place.slot - source + GROUP, GROUP)

        @pl.when(offset != 0)
        def _():
            copy(offset, True).wait_recv()

    sources = (x_hbm, seg_hbm, win_hbm, wo_hbm, wup_hbm, wdown_hbm, grad_hbm, *bias_hbm)
    loads = [
        pltpu.make_async_copy(src, dst, load_sems.at[number])
        for number, (src, dst) in enumerate(zip(sources, loaded))
    ]
    for load in loads:
        load.start()
    barrier, expected = greet(place, parts, True)
    for load in loads:
        load.wait()

    head, sequence = lax.div(place.slot, 2), lax.rem(place.slot, 2)
    group_x = place.part * 2 + sequence
    row = iota((16, LANES), 0)
    numbers = seg_ref[...].astype(F32)
    tile[...] = jnp.where(row == 0, numbers[0:1], numbers[1:2]).astype(BF16)
    segs[window + place.slot] = tile[...]
    aux_ref[...] = jnp.zeros_like(aux_ref)
    for index, ref in enumerate(bias_refs):
        aux_ref[index : index + 1, 0 : ref.shape[-1]] = ref[...].astype(F32).reshape(1, ref.shape[-1])
    if window:

        @pl.when(place.part == 0)
        def _():
            kv_ref[pl.ds(0, window)] = jnp.zeros((window, LANES, LANES), BF16)

    g_aux = Gather(place, aux_ref, gaux, gather_sems[0])
    plan = (
        (wo_ref, gwo, None),
        (wup_ref, gwup, (0, hidden // 2)),
        (wup_ref, gwup, (hidden // 2, hidden // 2)),
        (wdown_ref, gwdown, (0, width // 2)),
        (wdown_ref, gwdown, (width // 2, width // 2)),
        (win_ref, gwin, None),
    )
    rest = [
        TreeGather(place, src, dst, sems, cols)
        for (src, dst, cols), sems in zip(plan, gather_sems[1:])
    ]
    g_wo, g_up0, g_up1, g_down0, g_down1, g_win = rest

    def x_send(code, bit, src=None):
        chunk = xg.at[place.crossed(code)]
        remote(
            chunk if src is None else src,
            chunk,
            x_s.at[0],
            x_r.at[code ^ bit],
            place.member(place.crossed(bit)),
        ).start()

    def x_here(*codes):
        for code in codes:
            wait_received(place, xg.at[place.crossed(code)], x_r.at[code])

    low_rows = iota((in_rows, LANES), 1) < HD
    for pair in range(HEADS // 2):
        q_at, k_at, v_at = [
            win_ref[:, kind * width + pair * LANES : kind * width + (pair + 1) * LANES].astype(F32)
            for kind in range(3)
        ]
        ws[2 * pair, :, 0:LANES] = jnp.where(low_rows, k_at, swap_halves(v_at)).astype(BF16)
        ws[2 * pair, :, LANES:] = jnp.where(low_rows, q_at, 0.0).astype(BF16)
        ws[2 * pair + 1, :, 0:LANES] = jnp.where(low_rows, swap_halves(k_at), v_at).astype(BF16)
        ws[2 * pair + 1, :, LANES:] = jnp.where(low_rows, swap_halves(q_at), 0.0).astype(BF16)

    xg[pl.ds(place.slot, 1)] = x_ref[pl.ds(sequence, 1)]
    pl.semaphore_wait(barrier, expected)

    x_send(0, 1, x_ref.at[1 - sequence])
    g_wo.start_line()
    g_up0.start_line()
    g_up1.start_line()
    g_down0.start_line()
    g_down1.start_line()
    g_aux.start_line()

    def to_heads(src, dst, send, recv):
        def step(offset):
            other = lax.rem(head + offset, HEADS)
            remote(src.at[other], dst, send, recv, place.member(2 * other + sequence)).start()

        loop(step, 1, HEADS)

    def to_head_group(src, dst, send, recv):
        for offset in range(1, 2 * parts):
            other = lax.rem(group_x + offset, 2 * parts)
            part, other_sequence = lax.div(other, 2), lax.rem(other, 2)
            device = place.member(2 * head + other_sequence, part)
            remote(src(part, other_sequence), dst(offset), send, recv, device).start()

    every = slice(None)
    to_heads(ws, wh.at[place.part, head, sequence], w_sems.at[0], w_sems.at[1])
    wh[place.part, head, sequence] = ws[head]
    loop(lambda offset: seg_copy(offset).start())
    g_wo.start_step()
    g_up0.start_step()
    g_up1.start_step()
    for bit in (4, 2, 8):
        x_send(0, bit, x_ref.at[sequence])
    g_down0.start_step()
    g_down1.start_step()
    x_here(1)
    for bit in (4, 2, 8):
        x_send(1, bit)
    g_wo.start_first()
    g_up0.start_first()
    g_up1.start_first()
    wait_received(place, ws.at[pl.ds(0, HEADS - 1)], w_sems.at[1])
    own_rows = wh.at[place.part, every, sequence]
    to_head_group(lambda *at: own_rows, lambda offset: own_rows, w_sems.at[2], w_sems.at[3])
    g_aux.start_columns()
    g_wo.start_second()

    wait_received(place, segs.at[pl.ds(0, GROUP - 1)], seg_sems.at[1])

    def seg_halo(part):
        return remote(
            segs.at[pl.ds(GROUP, window)],
            segs.at[pl.ds(0, window)],
            seg_hs.at[0],
            seg_hr.at[0],
            place.member(place.slot, part),
        )

    if parts > 1:

        @pl.when(place.part < parts - 1)
        def _():
            seg_halo(place.part + 1).start()

    x_here(4)
    x_send(4, 2)
    x_send(4, 8)
    g_down0.start_first()
    g_down1.start_first()
    g_up0.start_second()
    g_up1.start_second()
    g_aux.start_hands()
    x_here(5)
    x_send(5, 2)
    x_send(5, 8)
    x_here(2, 3)
    x_send(2, 8)
    x_send(3, 8)
    g_aux.finish()
    wait_received(place, rw, w_sems.at[3])

    aux = gaux[...].reshape(devices * 8, LANES)
    bias_q = head_bias(aux, "query", per, head, 0)
    bias_v = head_bias(aux, "value", per, head, HD)

    def kv_halo(number, part):
        return remote(
            kv_ref.at[GROUP + number],
            kv_ref.at[number],
            kv_hs.at[0],
            kv_hr.at[number],
            place.member(place.slot, part),
        )

    def project(code):
        first = 2 * lax.div(place.crossed(code), 2)
        rows = xg[pl.ds(first, 2)].reshape(2 * LANES, width)
        made = dot(rows, wh[...].reshape(width, 2 * LANES))
        kv = (made[:, :LANES] + bias_v).astype(BF16)
        q = (made[:, LANES:] + bias_q).astype(BF16).astype(F32) * 0.125
        for side in range(2):
            chunk = first + side
            at = slice(side * LANES, (side + 1) * LANES)
            kv_ref[window + chunk] = kv[at]
            kvt[window + chunk] = kv[at].T
            qt_ref[chunk] = q[at].T[:HD].astype(BF16)
            if parts > 1:

                @pl.when((place.part < parts - 1) & (chunk >= GROUP - window))
                def _():
                    kv_halo(chunk - (GROUP - window), place.part + 1).start()

    project(0)
    project(2)
    g_down0.start_second()
    g_down1.start_second()
    g_wo.start_hands()
    project(4)
    x_here(6, 7)
    x_send(6, 8)
    x_send(7, 8)
    project(6)
    g_up0.start_hands()
    g_up1.start_hands()
    x_here(8, 9)
    project(8)
    x_here(12, 13)
    project(12)
    g_down0.start_hands()
    g_down1.start_hands()

    if parts > 1:

        @pl.when(place.part < parts - 1)
        def _():
            seg_halo(place.part + 1).wait_send()

        @pl.when(place.part > 0)
        def _():
            seg_halo(place.part - 1).wait_recv()

    chosen = jnp.where(iota((span, 16, LANES), 1) == sequence, segs[...].astype(F32), 0.0)
    seen = jnp.sum(chosen, axis=1)
    outside = (iota((span, LANES), 0) < window) & (place.part == 0)
    seen = jnp.where(outside, -1.0, seen)
    own = seen[window:]
    start = jnp.zeros((GROUP, LANES), F32)
    for number in range(docs):
        count = jnp.sum(jnp.where(seen == number - 1, 1.0, 0.0), axis=0, keepdims=True)
        count = jnp.sum(count, axis=1, keepdims=True)
        start = start + jnp.where(own >= number, count, 0.0)
    starts_ref[...] = start.astype(jnp.int32)

    x_here(10, 11)
    project(10)
    x_here(14, 15)
    project(14)

    many = window + 2
    older = window * LANES

    def q_rows_of(ref, m):
        return jnp.concatenate([ref[pl.ds(2 * m, 1)], ref[pl.ds(2 * m + 1, 1)]], axis=1)

    def turned_window(m):
        return jnp.concatenate([kvt[2 * m + i] for i in range(many)], axis=1)

    def masked(scores, start, q_place, block, base):
        k_place = base + block * BLOCK + iota((BLOCK, BLOCK), 0)
        visible = k_place >= start
        if block == reach:
            visible = visible & (k_place <= q_place)
        return jnp.where(visible, scores, NEG)

    blank = jnp.zeros((HD, BLOCK), BF16)

    def attend(step, carry):
        @pl.when(step == 0)
        def _():
            g_win.start_line()

        @pl.when(step == 4)
        def _():
            g_win.start_step()

        @pl.when(step == 7)
        def _():
            g_win.start_first()

        if parts > 1:

            @pl.when((step == free) & (place.part > 0))
            def _():
                loop(lambda number: kv_halo(number, place.part - 1).wait_recv(), 0, window)

        @pl.when(step == free)
        def _():
            def turn(number):
                kvt[number] = kv_ref[number].T

            loop(turn, 0, window)

        turnover = place.slot
        late = lax.rem(step - free + GROUP + turnover, reach)
        if free:
            m = jnp.where(step < free, reach + lax.rem(step + turnover, free), late)
        else:
            m = late
        q_wide = jnp.concatenate([two(qt_ref, 2 * m), blank], axis=0)
        start = q_rows_of(starts_ref, m)
        base = m * BLOCK
        q_place = base + older + iota((1, BLOCK), 1)
        scores = [
            masked(
                dot(kv_ref[pl.ds(2 * (m + block), 2)].reshape(BLOCK, LANES), q_wide),
                start,
                q_place,
                block,
                base,
            )
            for block in range(reach + 1)
        ]
        peak = functools.reduce(jnp.maximum, scores)
        peak = jnp.max(peak, axis=0, keepdims=True)
        weights = [jnp.exp(score - peak) for score in scores]
        total = functools.reduce(jnp.add, weights)
        total = jnp.sum(total, axis=0, keepdims=True)
        weights = jnp.concatenate([weight.astype(BF16) for weight in weights], axis=0)
        out = dot(turned_window(m)[HD:], weights) / total
        lse = peak + jnp.log(total)
        for side in range(2):
            lanes = slice(side * LANES, (side + 1) * LANES)
            of_ref[2 * m + side] = out[:, lanes]
            ot_ref[2 * m + side] = out[:, lanes].astype(BF16)
            lse_ref[pl.ds(2 * m + side, 1)] = lse[:, lanes]
            send_to(o_copy, 2 * m + side)
        return carry

    lax.fori_loop(0, pairs_of_chunks, attend, 0)
    mixed_t[place.slot] = ot_ref[place.slot]

    a0, a1 = alphas_ref[0], alphas_ref[1]
    bias_out = spread_bias(aux, "output", per, width)
    bias_down = spread_bias(aux, "down", per, width)
    bias_up = spread_bias(aux, "up", per_up, hidden)
    rows = 2 * LANES
    wide_tokens = x_ref[...].reshape(rows, width).astype(F32)
    grads = grad_ref[...].reshape(rows, width).astype(F32)
    grad_ffn = (a1 * grads).astype(BF16)
    g_win.start_second()
    g_wo.finish()
    full_out = gwo[...].reshape(width, width)

    all_here(mixed_t, o_sems)
    mixed_all = mixed_t[...].reshape(HEADS, 2, HD, LANES)
    mixed_turned = [mixed_all[:, s].reshape(width, LANES) for s in range(2)]
    mixed = jnp.concatenate([mixed_turned[0].T, mixed_turned[1].T], axis=0)
    branch = dot(mixed, full_out) + bias_out
    attn_term = a0 * branch
    residual = wide_tokens + attn_term
    hidden_in = residual.astype(BF16)

    ffn = jnp.zeros((rows, width), F32) + bias_down
    grad_res = grads
    tile_up = 512
    g_up0.finish()
    g_up1.finish()
    whole_up = gwup.reshape(width, hidden)
    whole_down = gwdown.reshape(hidden, width)
    for t in range(hidden // tile_up):
        cols = pl.ds(t * tile_up, tile_up)
        pre = dot(hidden_in, whole_up[:, cols]) + bias_up[:, t * tile_up : (t + 1) * tile_up]
        phi = 0.5 * (1.0 + lax.erf(pre * (1.0 / math.sqrt(2.0))))
        act_s[:, cols] = (pre * phi).astype(BF16)
        slope = phi + pre * jnp.exp(-0.5 * pre * pre) * (1.0 / math.sqrt(2.0 * math.pi))
        slope_s[:, cols] = slope
    sources = [
        (TreeReduce, p_out, r_out, None),
        (TreeReduce, p_up, r_up, (0, hidden // 2)),
        (TreeReduce, p_up, r_up, (hidden // 2, hidden // 2)),
        (TreeReduce, p_down, r_down, (0, width // 2)),
        (TreeReduce, p_down, r_down, (width // 2, width // 2)),
    ]
    t_out, t_up0, t_up1, t_down0, t_down1 = [
        kind(place, part, out, *scratch, cols)
        for (kind, part, out, cols), scratch in zip(sources, trees)
    ]
    t_aux = Total(place, *trees[-1])
    flat_down, flat_up = p_down.reshape(hidden, width), p_up.reshape(width, hidden)
    for half, tree in enumerate((t_down0, t_down1)):
        at = slice(half * width // 2, (half + 1) * width // 2)
        for t in range(hidden // tile_up):
            cols = pl.ds(t * tile_up, tile_up)
            flat_down[cols, at] = dot_tn(act_s[:, cols], grad_ffn[:, at]).astype(BF16)
        tree.start_core()
    g_down0.finish()
    g_down1.finish()
    for t in range(hidden // tile_up):
        cols = pl.ds(t * tile_up, tile_up)
        w_down = whole_down[cols, :]
        gpre = (dot_nt(grad_ffn, w_down) * slope_s[:, cols]).astype(BF16)
        gpre_s[:, cols] = gpre
        grad_res = grad_res + dot_nt(gpre, whole_up[:, cols])
    hidden_turned = hidden_in.T

    def up_part(half, tree):
        for t in range(hidden // tile_up // 2):
            cols = pl.ds(half * hidden // 2 + t * tile_up, tile_up)
            flat_up[:, cols] = dot(hidden_turned, gpre_s[:, cols]).astype(BF16)
        tree.start_core()

    up_part(0, t_up0)
    t_down0.start_second()
    g_win.start_hands()
    up_part(1, t_up1)
    t_down1.start_second()
    gres_ref[...] = grad_res
    grad_branch = (a0 * grad_res).astype(BF16)
    grad_mixed = dot_nt(grad_branch, full_out).astype(BF16).astype(F32)
    for s in range(2):
        turned = grad_mixed[s * LANES : (s + 1) * LANES].T.astype(BF16)
        for number in range(HEADS):
            dos[2 * number + s] = turned[number * HD : (number + 1) * HD]
    loop(lambda offset: d_copy(offset).start())
    doct_ref[place.slot] = dos[place.slot]
    t_up0.start_second()

    p_out.reshape(width, width)[...] = dot(
        jnp.concatenate([mixed_turned[0], mixed_turned[1]], axis=1), grad_branch
    ).astype(BF16)
    t_out.start_core()
    t_up1.start_second()

    for t in range(hidden // tile_up):
        cols = pl.ds(t * tile_up, tile_up)
        ffn = ffn + dot(act_s[:, cols], whole_down[cols, :])
    ffn_term = a1 * ffn
    stream = residual + ffn_term
    out_ref[...] = stream.astype(BF16).reshape(2, LANES, width)

    def whole(values):
        return jnp.sum(jnp.sum(values, axis=0, keepdims=True), axis=1, keepdims=True)

    sums = (
        whole(stream * stream),
        whole(attn_term * attn_term),
        whole(ffn_term * ffn_term),
        whole(grad_res * branch),
        whole(grads * ffn),
    )
    lane = iota((1, LANES), 1)
    scalars = jnp.zeros((1, LANES), F32)
    for number, value in enumerate(sums):
        scalars = scalars + jnp.where(lane == number, value, 0.0)
    up_row = jnp.sum(gpre_s[...].astype(F32), axis=0, keepdims=True)
    down_row = jnp.sum(grad_ffn.astype(F32), axis=0, keepdims=True)
    out_row = jnp.sum(grad_branch.astype(F32), axis=0, keepdims=True)
    wide_rows = width // LANES
    bases = {name: number * wide_rows for number, name in enumerate(BIASES)}
    last_row = (len(BIASES) - 1) * wide_rows + hidden // LANES

    def keep(base, row):
        for number in range(row.shape[1] // LANES):
            here = slice(number * LANES, (number + 1) * LANES)
            t_aux.mine[base + number : base + number + 1] = row[:, here]

    t_aux.mine[...] = jnp.zeros_like(t_aux.mine)
    keep(bases["output"], out_row)
    keep(bases["down"], down_row)
    keep(bases["up"], up_row)
    keep(last_row, scalars)

    t_out.start_second()
    early = (t_down0, t_down1, t_up0, t_up1, t_out)
    low_block = iota((BLOCK, LANES), 1) < HD

    def clear(m):
        dq_s[m] = jnp.zeros((HD, BLOCK), F32)

    loop(clear, 0, pairs_of_chunks)

    def back_halo(u, part):
        pair = pl.ds(2 * u, 2)
        return remote(
            halo_out.at[pair],
            halo_in.at[pair],
            back_hs.at[0],
            back_hr.at[u],
            place.member(place.slot, part),
        )

    def ready(m):
        await_from(d_copy, 2 * m)
        await_from(d_copy, 2 * m + 1)
        qt, dt = two(qt_ref, 2 * m), two(doct_ref, 2 * m)
        both = jnp.concatenate([qt, dt], axis=0).astype(F32).T
        here = pl.ds(2 * m, 2)
        q_rows_s[here] = jnp.where(low_block, both, 0.0).astype(BF16).reshape(2, LANES, LANES)
        d_rows_s[here] = jnp.where(low_block, 0.0, both).astype(BF16).reshape(2, LANES, LANES)
        delta = jnp.sum(dt.astype(F32) * two(of_ref, 2 * m), axis=0, keepdims=True)
        delta_ref[pl.ds(2 * m, 1)] = delta[:, :LANES]
        delta_ref[pl.ds(2 * m + 1, 1)] = delta[:, LANES:]

    def key_block(u, low, count):
        kv = kv_ref[pl.ds(2 * u, 2)].reshape(BLOCK, LANES)
        keys_turned = two(kvt, 2 * u)[:HD]
        k_place = u * BLOCK + iota((BLOCK, BLOCK), 0)
        grad = jnp.zeros((BLOCK, LANES), F32)
        for number in range(count):
            m = low + number
            here = pl.ds(2 * m, 2)
            q_wide = jnp.concatenate([two(qt_ref, 2 * m), blank], axis=0)
            d_wide = jnp.concatenate([blank, two(doct_ref, 2 * m)], axis=0)
            visible = k_place >= q_rows_of(starts_ref, m)
            if number == 0:
                visible = visible & (k_place <= m * BLOCK + older + iota((1, BLOCK), 1))
            scores = jnp.where(visible, dot(kv, q_wide), NEG)
            probs = jnp.exp(scores - q_rows_of(lse_ref, m))
            grad_scores = (probs * (dot(kv, d_wide) - q_rows_of(delta_ref, m))).astype(BF16)
            grad = grad + dot(grad_scores, q_rows_s[here].reshape(BLOCK, LANES))
            grad = grad + dot(probs.astype(BF16), d_rows_s[here].reshape(BLOCK, LANES))
            dq_s[m] += dot(keys_turned, grad_scores)
        grad_s[...] = grad

    def settle(u):
        pair = u - reach
        if parts > 1:
            late = pair - (pairs_of_chunks - reach)

            @pl.when((late >= 0) & (place.part < parts - 1))
            def _():
                back_halo(late, place.part + 1).wait_recv()
                grad_s[...] += halo_in[pl.ds(2 * late, 2)].reshape(BLOCK, LANES).astype(F32)

        dkv_sum[pl.ds(2 * pair, 2)] = grad_s[...].astype(BF16).reshape(2, LANES, LANES)
        dq = dq_s[pair] * 0.125
        for side in range(2):
            send_to(dkv_copy, 2 * pair + side)
            dqt_ref[2 * pair + side] = dq[:, side * LANES : (side + 1) * LANES].astype(BF16)
            send_to(dq_copy, 2 * pair + side)

    def attend_back(u, carry):
        @pl.when(u == 1)
        def _():
            t_down0.start_first()

        @pl.when(u == 3)
        def _():
            t_down1.start_first()

        @pl.when(u == 5)
        def _():
            t_up0.start_first()

        @pl.when(u == 7)
        def _():
            t_up1.start_first()

        @pl.when(u == 9)
        def _():
            t_out.start_first()

        @pl.when(u < pairs_of_chunks)
        def _():
            ready(u)

        low = jnp.maximum(u - reach, 0)
        count = jnp.minimum(u, pairs_of_chunks - 1) - low + 1
        needed = (u >= reach) | (place.part > 0)
        for number in range(1, reach + 2):

            @pl.when(needed & (count == number))
            def _():
                key_block(u, low, number)

        if parts > 1:

            @pl.when((u < reach) & (place.part > 0))
            def _():
                halo_out[pl.ds(2 * u, 2)] = grad_s[...].astype(BF16).reshape(2, LANES, LANES)
                back_halo(u, place.part - 1).start()

        @pl.when(u >= reach)
        def _():
            settle(u)

        return carry

    lax.fori_loop(0, reach + pairs_of_chunks, attend_back, 0)
    dq_in[place.slot] = dqt_ref[place.slot]
    t_down0.start_line()
    t_down1.start_line()
    t_up0.start_line()
    t_up1.start_line()
    dkv_in[place.slot] = dkv_sum[place.slot]

    dq_all = jnp.concatenate([dqt_ref[i] for i in range(GROUP)], axis=1)
    dkv_all = dkv_sum[...].reshape(GROUP * LANES, LANES)
    twice = jnp.concatenate([dq_all, dq_all], axis=0)
    query_row = dot_nt(jnp.ones((8, GROUP * LANES), BF16), twice)[0:1]
    value_row = jnp.sum(dkv_all.astype(F32), axis=0, keepdims=True)
    value_row = jnp.where(lane < HD, swap_halves(value_row), value_row)
    mine = (iota((wide_rows, LANES), 0) == lax.div(head, 2)) & (
        lax.div(iota((wide_rows, LANES), 1), HD) == lax.rem(head, 2)
    )
    for name, sums_row in (("query", query_row), ("value", value_row)):
        t_aux.mine[bases[name] : bases[name] + wide_rows] = jnp.where(mine, sums_row, 0.0)
    t_aux.start_core()
    x_rows = xg[...].reshape(GROUP * LANES, width)
    turned = jnp.concatenate(
        [dot_tn(dkv_all, x_rows), dot(dq_all, x_rows), jnp.zeros((HD, width), F32)], axis=0
    )
    pw[...] = turned.T.astype(BF16).reshape(pw.shape)
    to_head_group(
        lambda *at: pw.at[at[0], every, at[1]],
        lambda offset: rw.at[offset - 1],
        g_sems.at[0],
        g_sems.at[1],
    )
    t_aux.start_columns()
    t_out.start_line()
    t_down0.start_step()
    wait_received(place, rw, g_sems.at[1])
    total = pw[place.part, every, sequence].astype(F32)
    for number in range(2 * parts - 1):
        total = total + rw[number].astype(F32)
    wsum[...] = total
    to_heads(wsum, w_in.at[head], g_sems.at[2], g_sems.at[3])
    w_in[head] = wsum[head]
    t_aux.start_line()
    t_down1.start_step()
    t_up0.start_step()

    all_here(dq_in, dq_sems)
    for s in range(2):
        turned = jnp.concatenate([dq_in[2 * number + s] for number in range(HEADS)], axis=0)
        gp[s * LANES : (s + 1) * LANES, 0:width] = turned.astype(F32).T.astype(BF16)
    g_win.finish()
    full_in = gwin.reshape(width, 3 * width)
    gx = gres_ref[...] + dot_nt(gp[:, 0:width], full_in[:, 0:width])
    t_up1.start_step()
    t_out.start_step()
    all_here(dkv_in, dkv_sems)
    low_lane = iota((LANES, LANES), 1) < HD
    for s in range(2):
        at_rows = slice(s * LANES, (s + 1) * LANES)
        for pair in range(HEADS // 2):
            even = dkv_in[4 * pair + s].astype(F32)
            odd = dkv_in[4 * pair + 2 + s].astype(F32)
            keys = jnp.where(low_lane, even, swap_halves(odd))
            values = jnp.where(low_lane, swap_halves(even), odd)
            at = width + pair * LANES
            gp[at_rows, at : at + LANES] = keys.astype(BF16)
            gp[at_rows, width + at : width + at + LANES] = values.astype(BF16)
    gx = gx + dot_nt(gp[:, width:], full_in[:, width:])
    gx_ref[...] = gx.astype(BF16).reshape(2, LANES, width)
    wait_received(place, w_in.at[pl.ds(0, HEADS - 1)], g_sems.at[3])
    for pair in range(HEADS // 2):
        even, odd = w_in[2 * pair], w_in[2 * pair + 1]
        even_kv, odd_kv = even[:, :LANES], odd[:, :LANES]
        parts_of = (
            jnp.where(low_rows, even[:, LANES:], swap_halves(odd[:, LANES:])),
            jnp.where(low_rows, even_kv, swap_halves(odd_kv)),
            jnp.where(low_rows, swap_halves(even_kv), odd_kv),
        )
        for kind, value in enumerate(parts_of):
            at = kind * width + pair * LANES
            r_win[:, at : at + LANES] = value
    for tree in early:
        tree.finish()
    totals = t_aux.result()
    flat = place.part * GROUP + place.slot
    for number, name in enumerate(BIASES):
        own = own_values(totals, bases[name], per_up if name == "up" else per, flat)
        r_aux[number : number + 1] = own
    r_aux[SCALARS : SCALARS + 1] = totals[last_row : last_row + 1]
    all_sent(segs, seg_sems)
    wait_sent(place, xg.at[pl.ds(0, GROUP - 1)], x_s.at[0])
    wait_sent(place, ws.at[pl.ds(0, HEADS - 1)], w_sems.at[0])
    wait_sent(place, rw, w_sems.at[2])
    wait_sent(place, rw, g_sems.at[0])
    wait_sent(place, w_in.at[pl.ds(0, HEADS - 1)], g_sems.at[2])
    all_sent(ot_ref, o_sems)
    all_sent(dos, d_sems)
    all_sent(dqt_ref, dq_sems)
    all_sent(dkv_sum, dkv_sems)
    if parts > 1:

        @pl.when(place.part < parts - 1)
        def _():
            wait_sent(place, kv_ref.at[pl.ds(0, window)], kv_hs.at[0])

        @pl.when(place.part > 0)
        def _():
            wait_sent(place, halo_out, back_hs.at[0])

    for gather in (g_aux, *rest):
        gather.drain()
    for tree in early + (t_aux,):
        tree.drain()


def swap_halves(values):
    return jnp.concatenate([values[:, HD:], values[:, :HD]], axis=1)


def two(ref, index):
    return jnp.concatenate([ref[index], ref[index + 1]], axis=1)


def hand_out_kernel(
    tokens_all, out_ref, gx_ref, win_ref, wo_ref, wup_ref, wdown_ref, sums_ref, *results
):
    for src, dst in zip((out_ref, gx_ref, win_ref, wo_ref, wup_ref, wdown_ref), results[:6]):
        dst[...] = src[...]
    named = dict(zip(("query", "value", "output", "up", "down"), results[6:11]))
    for name, ref in named.items():
        ref[...] = sums_ref[BIASES.index(name), 0 : ref.shape[0]]
    results[11][...] = sums_ref[SCALARS, 3:5]
    results[12][...] = jnp.sqrt(sums_ref[SCALARS, 0:3] * (1.0 / tokens_all))


def call(kernel, out_shape, in_specs, out_specs, scratch, megabytes, collective=None):
    return pl.pallas_call(
        kernel,
        out_shape=out_shape,
        in_specs=in_specs,
        out_specs=out_specs,
        scratch_shapes=scratch,
        compiler_params=pltpu.CompilerParams(
            collective_id=collective,
            has_side_effects=collective is not None,
            vmem_limit_bytes=megabytes * 1024 * 1024,
        ),
    )


def local(
    layer_input,
    segments,
    input_weight,
    output_weight,
    up_weight,
    down_weight,
    query_bias,
    value_bias,
    output_bias,
    up_bias,
    down_bias,
    alphas,
    out_grad,
):
    heads, blocks = lax.axis_size("head"), lax.axis_size("blk")
    depth, devices = blocks // 2, heads * blocks
    seqs, rows, width = layer_input.shape
    hidden = up_weight.shape[1]
    seq_len = rows * devices
    assert heads == 4 and seqs * HEADS == GROUP and rows == LANES
    longest = 16 * math.isqrt(seq_len)
    window, parts = longest // rows, devices // GROUP
    docs = 2 * seq_len // longest
    assert window <= GROUP and window % 2 == 0
    span = window + GROUP

    def shape(*dims, dtype=BF16):
        return jax.ShapeDtypeStruct(dims, dtype)

    vmem, smem = pl.BlockSpec(memory_space=VMEM), pl.BlockSpec(memory_space=pltpu.SMEM)
    hbm = pl.BlockSpec(memory_space=pltpu.HBM)
    dma = pltpu.SemaphoreType.DMA
    lead = (2, 2, depth, 2)
    in_rows, up_rows = input_weight.shape[0], down_weight.shape[0]
    tree_parts = ((in_rows, width),) + ((in_rows, hidden // 2),) * 2 + ((up_rows, width // 2),) * 2
    tokens = seqs * rows
    total_rows = -(-((len(BIASES) - 1) * width + hidden + LANES) // (8 * LANES)) * 8
    results = (
        shape(seqs, rows, width),
        shape(seqs, rows, width),
        shape(in_rows, 3 * width, dtype=F32),
        shape(in_rows, width, dtype=F32),
        shape(in_rows, hidden, dtype=F32),
        shape(up_rows, width, dtype=F32),
    )
    carried = call(
        functools.partial(layer_kernel, blocks, parts, window, docs),
        results + (shape(8, LANES, dtype=F32),),
        [hbm] * 6 + [(hbm,) * 5] + [smem, hbm],
        (vmem,) * 7,
        [
            [
                VMEM((*lead, in_rows, 3 * width), BF16),
                VMEM((*lead, in_rows, width), BF16),
                VMEM((*lead, in_rows, hidden), BF16),
                VMEM((*lead, up_rows, width), BF16),
                VMEM((*lead, 8, LANES), F32),
            ],
            [dma((Gather.COUNT,))] + [dma((TreeGather.COUNT + depth - 1,))] * 6,
            [TreeReduce.scratch(depth, *sizes, BF16) for sizes in tree_parts]
            + [Total.scratch(depth, total_rows)],
            [dma((n,)) for n in (2, 1, GROUP, 4, 2, GROUP, 2, 2, 4)],
            [dma((1,)), dma((1,)), dma((1,)), dma((window,)), dma((1,)), dma((window // 2,))],
            VMEM((span, 16, LANES), BF16),
            VMEM((16, LANES), BF16),
            VMEM((8, LANES), F32),
            VMEM((GROUP, LANES, width), BF16),
            VMEM((HEADS, in_rows, 2 * LANES), BF16),
            VMEM((parts, HEADS, 2, in_rows, 2 * LANES), BF16),
            VMEM((parts, HEADS, 2, in_rows, 2 * LANES), BF16),
            VMEM((2 * parts - 1, HEADS, in_rows, 2 * LANES), BF16),
            VMEM((HEADS, in_rows, 2 * LANES), F32),
            VMEM((HEADS, in_rows, 2 * LANES), F32),
            VMEM((GROUP, HD, LANES), BF16),
            VMEM((span, LANES, LANES), BF16),
            VMEM((span, LANES, LANES), BF16),
            VMEM((GROUP, LANES), jnp.int32),
            VMEM((GROUP, HD, LANES), BF16),
            VMEM((GROUP, HD, LANES), F32),
            VMEM((GROUP, LANES), F32),
            VMEM((GROUP, HD, LANES), BF16),
            VMEM((GROUP, HD, LANES), BF16),
            VMEM((GROUP, HD, LANES), BF16),
            VMEM((tokens, hidden), BF16),
            VMEM((tokens, hidden), F32),
            VMEM((tokens, hidden), BF16),
            VMEM((tokens, width), F32),
            VMEM((GROUP, LANES, LANES), BF16),
            VMEM((GROUP, LANES, LANES), BF16),
            VMEM((GROUP, LANES), F32),
            VMEM((GROUP // 2, HD, BLOCK), F32),
            VMEM((BLOCK, LANES), F32),
            VMEM((GROUP, HD, LANES), BF16),
            VMEM((GROUP, LANES, LANES), BF16),
            VMEM((GROUP, HD, LANES), BF16),
            VMEM((GROUP, LANES, LANES), BF16),
            VMEM((window, LANES, LANES), BF16),
            VMEM((window, LANES, LANES), BF16),
            VMEM((tokens, 3 * width), BF16),
            [
                VMEM((*lead, in_rows, width), BF16),
                VMEM((*lead, in_rows, hidden), BF16),
                VMEM((*lead, up_rows, width), BF16),
            ],
            [
                VMEM(array.shape, array.dtype)
                for array in (
                    layer_input,
                    segments,
                    input_weight,
                    output_weight,
                    up_weight,
                    down_weight,
                    out_grad,
                    query_bias,
                    value_bias,
                    output_bias,
                    down_bias,
                    up_bias,
                )
            ],
            dma((12,)),
        ],
        megabytes=60 if in_rows >= 16 else 60,
        collective=0,
    )(
        layer_input,
        segments,
        input_weight,
        output_weight,
        up_weight,
        down_weight,
        (query_bias, value_bias, output_bias, down_bias, up_bias),
        alphas,
        out_grad,
    )
    per, per_up = width // devices, hidden // devices
    return call(
        functools.partial(hand_out_kernel, seqs * seq_len * width),
        results
        + tuple(
            shape(size, dtype=F32) for size in (per, per, per, per_up, per, 2, 3)
        ),
        [vmem] * 7,
        (vmem,) * 13,
        [],
        megabytes=60,
    )(*carried)


def solution(mesh):
    tokens = P(None, ("head", "blk"), None)
    rows, flat = P(("head", "blk"), None), P(("head", "blk"))
    return jax.shard_map(
        local,
        mesh=mesh,
        in_specs=(
            tokens,
            P(None, ("head", "blk")),
            rows,
            rows,
            rows,
            rows,
            flat,
            flat,
            flat,
            flat,
            flat,
            P(),
            tokens,
        ),
        out_specs=(
            tokens,
            tokens,
            rows,
            rows,
            rows,
            rows,
            flat,
            flat,
            flat,
            flat,
            flat,
            P(),
            P(),
        ),
        check_vma=False,
    )
```
